1024 devices in a mesh: dp: 16 (over z_lo, x), mp: 64 (over z_hi, y, core).
Axes of the slice: x: 8, y: 8, z: 8 (z_hi: 4, z_lo: 2; z = z_hi * 2 + z_lo), core: 2. Of those that a mesh axis runs over, the one named last changes fastest.
Arguments:
- upstream: bfloat16 [2048, 6144], P(('dp', 'mp')), may hold values from -6 to 6
- pre_act: bfloat16 [2048, 12288], P('dp', 'mp'), may hold values from -6 to 6
- w_down: bfloat16 [12288, 6144], P('mp'), may hold values from -0.078125 to 0.078125
- first_moment: float32 [12288, 6144], P(('mp', 'dp')), may hold values from -6 to 6
- second_moment: float32 [12288, 6144], P(('mp', 'dp')), may hold values from 1 to 16
- signs: int32 [6144], replicated, may hold values from 0 to 1
- exponents: int32 [12288, 6], P('mp'), may hold values from -6 to -1
Outputs:
- pre_grad: bfloat16 [2048, 12288], P('dp', 'mp')
- grad_mean: float32 [12288, 6144], P(('mp', 'dp'))
- first_new: float32 [12288, 6144], P(('mp', 'dp'))
- second_new: float32 [12288, 6144], P(('mp', 'dp'))
- weight_new: bfloat16 [12288, 6144], P('mp')
The draws below stay inside these ranges and needn't reach their ends.
Inputs may be any that keep to these rules, and one draw needn't show every extreme that they name: `signs`: 1 turns a column's sign over. `exponents`: equal for every replica.
All inputs are finite; a program needn't handle non-finite values.
Results may differ from the reference program's by a relative error of at most 0.017.
Values may be sent and summed in bfloat16 or wider, within the bound.
No kernel may reach another device: no remote copies, remote signals or barrier semaphores. Data moves between devices by JAX's collectives and lax.ppermute only.
A program may use at most 64 MiB of HBM per device.

```python
import math
import jax
import jax.numpy as jnp
from jax import lax

D = 6144
FF_W = 12288
BLOCK = 1024
TOK_REP = 128
TOKENS = 2048
N_DP = 16


def with_ends(drawn, rng, low, high):
    longest = drawn.shape.index(max(drawn.shape))
    spots = []
    for shift in (0, 1):
        where = [jax.random.randint(jax.random.fold_in(rng, axis), (), 0, length) for axis, length in enumerate(drawn.shape)]
        where[longest] = (where[longest] + shift) % drawn.shape[longest]
        spots.append(tuple(where))
    return drawn.at[spots[0]].set(low).at[spots[1]].set(high)


def shard_levels(stream_key, dims, cuts, least, largest):
    def one(dim, blocks):
        steps = jax.random.uniform(jax.random.fold_in(jax.random.fold_in(stream_key, 6), dim), (blocks,), jnp.float32, least / len(cuts), largest / len(cuts))
        return jnp.repeat(jnp.exp(steps), dims[dim] // blocks).reshape((-1,) + (1,) * (len(dims) - dim - 1))

    gain = one(*cuts[0])
    for cut in cuts[1:]:
        gain = gain * one(*cut)
    return gain


def scatter_about(stream_key, dims, deviation, most, cuts=(), held_as=jnp.bfloat16):
    array = deviation * jax.random.normal(stream_key, dims, jnp.float32)
    if cuts:
        array = array * shard_levels(stream_key, dims, cuts, -0.22, 0.18)
    return jnp.clip(array, -most, most).astype(held_as)


def setup_inputs(seed: int = 0) -> dict:
    key_list = jax.random.split(jax.random.key(seed), 8)
    upstream = scatter_about(key_list[0], (TOKENS, D), 1.0, 6.0, ((0, 1024),))
    pre_act = scatter_about(key_list[1], (TOKENS, FF_W), 1.0, 6.0, ((0, 16), (1, 64)))
    w_down = scatter_about(key_list[2], (FF_W, D), D ** -0.5, 0.078125, ((0, 64),))
    first_moment = scatter_about(key_list[3], (FF_W, D), 1.0, 6.0, ((0, 1024),), jnp.float32)
    second_moment = jnp.clip(jnp.exp(math.log(16.0) - 2.7725887 * jax.random.uniform(key_list[4], (FF_W, D), jnp.float32) ** shard_levels(key_list[4], (FF_W, D), ((0, 1024),), -0.2, 0.2)), 1.0, 16.0)
    signs = with_ends(jax.random.randint(key_list[5], (D,), 0, 2), jax.random.fold_in(key_list[5], 1), 0, 1).astype(jnp.int32)
    exponents = with_ends(jax.random.randint(key_list[6], (FF_W, D // BLOCK), -6, 0), jax.random.fold_in(key_list[6], 1), -6, -1).astype(jnp.int32)
    return dict(upstream=upstream, pre_act=pre_act, w_down=w_down, first_moment=first_moment, second_moment=second_moment, signs=signs, exponents=exponents)


hadamard_norm = 0.03125
clip_limit = 448.0
root_half = 0.7071067811865476
density_norm = 0.3989422804014327

def hadamard_table(table_order):
    indices = jnp.arange(table_order, dtype=jnp.int32)
    common = indices[:, None] & indices[None, :]
    parity = jnp.zeros((table_order, table_order), jnp.int32)
    for position in range(table_order.bit_length() - 1):
        parity = parity + (common >> position & 1)
    return (1 - 2 * (parity % 2)).astype(jnp.float32)

def rotate(values):
    leading = values.shape[:-1]
    shaped = values.reshape(leading + (8, 128))
    mixed = jnp.einsum('...aq,ab->...bq', shaped, hadamard_table(8), precision=lax.Precision.HIGHEST)
    mixed = jnp.einsum('...bq,qp->...bp', mixed, hadamard_table(128), precision=lax.Precision.HIGHEST)
    return (mixed * hadamard_norm).reshape(values.shape)

def encode(gradient, multiplier, sign_vector):
    row_count = gradient.shape[0]
    blocks = sign_vector.shape[0]
    shaped = gradient.reshape(row_count, blocks, 1024) * sign_vector[None]
    turned = rotate(shaped) * multiplier[:, :, None]
    return jnp.clip(turned, -clip_limit, clip_limit).reshape(gradient.shape)

def reference(upstream, pre_act, w_down, first_moment, second_moment, signs, exponents):
    preact = pre_act.astype(jnp.float32)
    normal_cdf = 0.5 * (1.0 + lax.erf(preact * root_half))
    hidden = (preact * normal_cdf).astype(jnp.bfloat16)
    derivative = normal_cdf + preact * jnp.exp(-0.5 * preact * preact) * density_norm
    hidden_grad = lax.dot_general(upstream, w_down, (((1,), (1,)), ((), ())), preferred_element_type=jnp.float32)
    pre_grad = (hidden_grad * derivative).astype(jnp.bfloat16)
    blocks = D // BLOCK
    sign_vector = (1 - 2 * signs).astype(jnp.float32).reshape(blocks, BLOCK)
    scale_power = exponents.astype(jnp.float32)
    shrink = jnp.exp2(-scale_power)

    def replica(accumulated, replica_idx):
        begin = (replica_idx * TOK_REP).astype(jnp.int32)
        own_hidden = lax.dynamic_slice_in_dim(hidden, begin, TOK_REP, 0)
        own_upstream = lax.dynamic_slice_in_dim(upstream, begin, TOK_REP, 0)
        gradient = lax.dot_general(own_hidden, own_upstream, (((0,), (0,)), ((), ())), preferred_element_type=jnp.float32)
        encoded = encode(gradient, shrink, sign_vector).astype(jnp.bfloat16)
        encoded = lax.optimization_barrier(encoded)
        return (accumulated + encoded.astype(jnp.float32), None)
    start_sum = jnp.zeros((FF_W, D), jnp.float32)
    summed, _ = lax.scan(replica, start_sum, jnp.arange(N_DP, dtype=jnp.int32))
    grown = summed.reshape(FF_W, blocks, BLOCK) * jnp.exp2(scale_power)[:, :, None]
    grad_mean = (rotate(grown) * sign_vector[None]).reshape(FF_W, D) / N_DP
    first_new = 0.9 * first_moment + 0.1 * grad_mean
    second_new = 0.95 * second_moment + 0.05 * grad_mean * grad_mean
    adjusted = first_new / 0.6513215599 / (jnp.sqrt(second_new / 0.4012630608) + 1e-08)
    weight_new = (w_down.astype(jnp.float32) * (1.0 - 0.01 * 0.1) - 0.01 * adjusted).astype(jnp.bfloat16)
    return (pre_grad, grad_mean, first_new, second_new, weight_new)
```

```python
import jax
import jax.numpy as jnp
import numpy as np
from jax import lax
from jax.experimental import pallas as pl
from jax.experimental.pallas import tpu as pltpu
from jax.sharding import Mesh
from jax.sharding import PartitionSpec as P

hadamard_norm = 0.03125
clip_limit = 448.0
root_half = 0.7071067811865476
density_norm = 0.3989422804014327

REPLICAS = 16
ROWS = 192
OWN = 12
COLS = 6144
SEGS = 4
SEG = 1536
BLOCKS = 6
TOK = 128
PEERS = 32
LANES = 128
VMEM = 48 * 1024 * 1024
bf16 = jnp.bfloat16
f32 = jnp.float32


def hadamard(order):
    indices = np.arange(order)
    common = indices[:, None] & indices[None, :]
    parity = np.zeros((order, order), np.int64)
    for position in range(order.bit_length() - 1):
        parity += common >> position & 1
    return (1 - 2 * (parity % 2)).astype(np.float32)


def tables():
    row = np.arange(REPLICAS * SEGS * OWN)
    owner, segment, own = row // (SEGS * OWN), row % (SEGS * OWN) // OWN, row % OWN
    spread = (owner * OWN + own)[:, None] == np.arange(ROWS)[None, :]
    col = np.arange(2 * PEERS * SEGS * 2)
    patch = col // (SEGS * 2) * 2 + col % 2
    col_segment = col % (SEGS * 2) // 2
    widen = np.arange(TOK)[:, None] == patch[None, :]
    same = segment[:, None] == col_segment[None, :]
    return (
        spread.astype(np.float32),
        widen.astype(np.float32),
        same.astype(np.float32),
        col_segment,
    )


def butterfly(parts):
    parts = list(parts)
    span = 1
    while span < len(parts):
        for start in range(0, len(parts), 2 * span):
            for k in range(start, start + span):
                first, second = parts[k], parts[k + span]
                parts[k], parts[k + span] = first + second, first - second
        span *= 2
    return parts


def whole(shape):
    return pl.BlockSpec(shape, lambda *_: (0,) * len(shape))


def params():
    return pltpu.CompilerParams(vmem_limit_bytes=VMEM)


def rotate_upstream_kernel(u_ref, sign_ref, had_ref, out_ref, x_ref, z_ref):
    turned = u_ref[...].astype(f32) * sign_ref[...]
    for t in range(COLS // LANES):
        x_ref[2 * t : 2 * t + 2, :] = turned[:, LANES * t : LANES * (t + 1)]
    x_ref[...] = jnp.dot(
        x_ref[...].astype(bf16), had_ref[...], preferred_element_type=f32
    )
    for b in range(BLOCKS):
        mixed = butterfly([x_ref[2 * t : 2 * t + 2, :] for t in range(8 * b, 8 * b + 8)])
        for k, part in enumerate(mixed):
            s, lane = divmod(8 * b + k, SEG // LANES)
            z_ref[2 * s : 2 * s + 2, LANES * lane : LANES * (lane + 1)] = (
                part * hadamard_norm
            )
    out_ref[...] = z_ref[...].astype(bf16)


def rotate_upstream(upstream, sign_row, had):
    return pl.pallas_call(
        rotate_upstream_kernel,
        out_shape=jax.ShapeDtypeStruct((2 * SEGS, SEG), bf16),
        scratch_shapes=[
            pltpu.VMEM((2 * COLS // LANES, LANES), f32),
            pltpu.VMEM((2 * SEGS, SEG), f32),
        ],
        compiler_params=params(),
        name="rotate_upstream",
    )(upstream, sign_row, had)


def expand_hidden_kernel(hidden_ref, spread_ref, widen_ref, same_ref, out_ref):
    rows = lax.dot_general(
        spread_ref[...],
        hidden_ref[...],
        (((1,), (1,)), ((), ())),
        preferred_element_type=f32,
    ).astype(bf16)
    wide = jnp.dot(rows, widen_ref[...], preferred_element_type=f32)
    out_ref[...] = (wide * same_ref[...].astype(f32)).astype(bf16)


def expand_hidden(hidden, spread, widen, same):
    return pl.pallas_call(
        expand_hidden_kernel,
        out_shape=jax.ShapeDtypeStruct(same.shape, bf16),
        compiler_params=params(),
        cost_estimate=pl.CostEstimate(
            flops=2 * 768 * 128 * 700, bytes_accessed=4 << 20, transcendentals=0
        ),
        name="expand_hidden",
    )(hidden, spread, widen, same)


TILE = 256


def encode_kernel(left_ref, own_ref, other_ref, scale_ref, out_ref):
    half = own_ref.shape[0]
    total = jnp.dot(left_ref[:, :half], own_ref[...], preferred_element_type=f32)
    total += jnp.dot(left_ref[:, half:], other_ref[...], preferred_element_type=f32)
    total = jnp.clip(total * scale_ref[0], -clip_limit, clip_limit)
    out_ref[...] = total.astype(bf16)


def encode(left, own, other, scale):
    rows = left.shape[0]
    half = own.shape[0]
    return pl.pallas_call(
        encode_kernel,
        out_shape=jax.ShapeDtypeStruct((rows, SEG), bf16),
        grid=(SEG // TILE,),
        in_specs=[
            whole(left.shape),
            pl.BlockSpec((half, TILE), lambda n: (0, n)),
            pl.BlockSpec((half, TILE), lambda n: (0, n)),
            pl.BlockSpec((1, rows, 1), lambda n: (n // 2, 0, 0)),
        ],
        out_specs=pl.BlockSpec((rows, TILE), lambda n: (0, n)),
        compiler_params=params(),
        cost_estimate=pl.CostEstimate(
            flops=2 * rows * 2 * half * SEG, bytes_accessed=6 << 20, transcendentals=0
        ),
        name="encode",
    )(left, own, other, scale)


def update_kernel(
    received_ref, power_ref, sign_ref, had_ref, first_ref, second_ref, weight_ref,
    mean_ref, first_out, second_out, sent_ref, sum_ref, x_ref, y_ref,
):
    total = received_ref[0].astype(f32)
    for source in range(1, received_ref.shape[0]):
        total += received_ref[source].astype(f32)
    sum_ref[...] = total
    x_ref[...] = jnp.zeros_like(x_ref)
    for t in range(COLS // LANES):
        s, lane = divmod(t, SEG // LANES)
        x_ref[16 * t : 16 * t + OWN, :] = (
            sum_ref[OWN * s : OWN * (s + 1), LANES * lane : LANES * (lane + 1)]
            * power_ref[:, t // 8 : t // 8 + 1]
        )
    x = x_ref[...]
    high = x.astype(bf16)
    low = (x - high.astype(f32)).astype(bf16)
    y_ref[...] = jnp.dot(high, had_ref[...], preferred_element_type=f32) + jnp.dot(
        low, had_ref[...], preferred_element_type=f32
    )
    for b in range(BLOCKS):
        mixed = butterfly(
            [y_ref[16 * t : 16 * t + OWN, :] for t in range(8 * b, 8 * b + 8)]
        )
        for k, part in enumerate(mixed):
            t = 8 * b + k
            s, lane = divmod(t, SEG // LANES)
            lanes = slice(LANES * t, LANES * (t + 1))
            mean = part * (hadamard_norm / REPLICAS) * sign_ref[:, lanes]
            mean_ref[:, lanes] = mean
            first = 0.9 * first_ref[:, lanes] + 0.1 * mean
            second = 0.95 * second_ref[:, lanes] + 0.05 * mean * mean
            first_out[:, lanes] = first
            second_out[:, lanes] = second
            adjusted = first / 0.6513215599 / (jnp.sqrt(second / 0.4012630608) + 1e-08)
            sum_ref[OWN * s : OWN * (s + 1), LANES * lane : LANES * (lane + 1)] = (
                weight_ref[:, lanes].astype(f32) * (1.0 - 0.01 * 0.1) - 0.01 * adjusted
            )
    sent_ref[...] = sum_ref[...].astype(bf16)


def update(received, power, sign_row, had, first, second, weight):
    own = jax.ShapeDtypeStruct((OWN, COLS), f32)
    return pl.pallas_call(
        update_kernel,
        out_shape=(own, own, own, jax.ShapeDtypeStruct((SEGS * OWN, SEG), bf16)),
        scratch_shapes=[
            pltpu.VMEM((SEGS * OWN, SEG), f32),
            pltpu.VMEM((16 * COLS // LANES, LANES), f32),
            pltpu.VMEM((16 * COLS // LANES, LANES), f32),
        ],
        compiler_params=params(),
        name="update",
    )(received, power, sign_row, had, first, second, weight)


def place_kernel(gathered_ref, out_ref, rows_ref):
    for d in range(REPLICAS):
        chunk = gathered_ref[d].astype(f32)
        for s in range(SEGS):
            rows_ref[OWN * d : OWN * (d + 1), SEG * s : SEG * (s + 1)] = chunk[
                OWN * s : OWN * (s + 1), :
            ]
    out_ref[...] = rows_ref[...].astype(bf16)


def place(gathered):
    return pl.pallas_call(
        place_kernel,
        out_shape=jax.ShapeDtypeStruct((ROWS, COLS), bf16),
        scratch_shapes=[pltpu.VMEM((ROWS, COLS), f32)],
        compiler_params=params(),
        name="place",
    )(gathered)


def rotate_weight_kernel(w_ref, sign_ref, had_ref, out_ref):
    turned = w_ref[...].astype(f32) * sign_ref[...]
    parts = [
        jnp.dot(
            turned[:, LANES * k : LANES * (k + 1)].astype(bf16),
            had_ref[...],
            preferred_element_type=f32,
        )
        for k in range(8)
    ]
    for k, part in enumerate(butterfly(parts)):
        out_ref[:, LANES * k : LANES * (k + 1)] = (part * hadamard_norm).astype(bf16)


def rotate_weight(weight, sign_row, had):
    return pl.pallas_call(
        rotate_weight_kernel,
        out_shape=jax.ShapeDtypeStruct((ROWS, COLS), bf16),
        grid=(BLOCKS,),
        in_specs=[
            pl.BlockSpec((ROWS, 1024), lambda b: (0, b)),
            pl.BlockSpec((1, 1024), lambda b: (0, b)),
            whole((LANES, LANES)),
        ],
        out_specs=pl.BlockSpec((ROWS, 1024), lambda b: (0, b)),
        compiler_params=params(),
        cost_estimate=pl.CostEstimate(
            flops=2 * ROWS * COLS * 1024, bytes_accessed=5 << 20, transcendentals=0
        ),
        name="rotate_weight",
    )(weight, sign_row, had)


def pre_grad_kernel(own_ref, other_ref, w_ref, slope_ref, collect_ref, out_ref, acc_ref):
    half = own_ref.shape[0]
    place_in_pair = lax.broadcasted_iota(jnp.int32, (half, 1), 0) & (2 * SEGS - 1)
    for index, rows_ref in enumerate((own_ref, other_ref)):
        rows = rows_ref[...]
        total = jnp.zeros((half, ROWS), f32)
        for s in range(SEGS):
            part = lax.dot_general(
                rows,
                w_ref[:, SEG * s : SEG * (s + 1)],
                (((1,), (1,)), ((), ())),
                preferred_element_type=f32,
            )
            total = jnp.where(place_in_pair >> 1 == s, part, total)
        acc_ref[half * index : half * (index + 1), :] = total
    hidden_grad = jnp.dot(
        collect_ref[...].astype(f32),
        acc_ref[...],
        precision=lax.Precision.HIGHEST,
        preferred_element_type=f32,
    )
    out_ref[...] = (hidden_grad * slope_ref[...]).astype(bf16)


def pre_grad_product(own, other, weight, slope, collect):
    return pl.pallas_call(
        pre_grad_kernel,
        out_shape=jax.ShapeDtypeStruct((TOK, ROWS), bf16),
        scratch_shapes=[pltpu.VMEM((2 * own.shape[0], ROWS), f32)],
        compiler_params=params(),
        cost_estimate=pl.CostEstimate(
            flops=8 * 512 * SEG * ROWS, bytes_accessed=6 << 20, transcendentals=0
        ),
        name="pre_grad",
    )(own, other, weight, slope, collect)


def swap_core(values):
    return lax.ppermute(values, "core", [(0, 1), (1, 0)])


def body(upstream, pre_act, w_down, first_moment, second_moment, signs, exponents):
    spread_np, widen_np, same_np, _ = tables()
    had = jnp.asarray(hadamard(LANES), bf16)
    spread = jnp.asarray(spread_np, bf16)
    widen = jnp.asarray(widen_np, bf16)
    same = jnp.asarray(same_np, bf16)
    sign_row = (1 - 2 * signs).astype(f32).reshape(1, COLS)
    core = lax.axis_index("core")

    rotated = rotate_upstream(upstream, sign_row, had)
    own = lax.all_to_all(
        jnp.broadcast_to(rotated[None], (PEERS, 2 * SEGS, SEG)),
        ("z_hi", "y"),
        0,
        0,
        tiled=True,
    ).reshape(PEERS * 2 * SEGS, SEG)
    other = swap_core(own)

    pairs = pre_act.reshape(PEERS, 2, 2, ROWS)
    mine = jnp.where(core == 0, pairs[:, 0], pairs[:, 1]).reshape(TOK // 2, ROWS)
    yours = jnp.where(core == 0, pairs[:, 1], pairs[:, 0]).reshape(TOK // 2, ROWS)
    preact = jnp.concatenate([mine, yours], axis=0).astype(f32)
    normal_cdf = 0.5 * (1.0 + lax.erf(preact * root_half))
    hidden = (preact * normal_cdf).astype(bf16)
    slope = normal_cdf + preact * jnp.exp(-0.5 * preact * preact) * density_norm

    scale_power = exponents.astype(f32)
    shrink = jnp.exp2(-scale_power)
    picked = jnp.stack(
        [
            jnp.stack([shrink[:, (3 * s + u) // 2] for s in range(SEGS)], axis=0)
            for u in range(3)
        ],
        axis=0,
    )
    scale = (
        picked.reshape(3, SEGS, REPLICAS, OWN)
        .transpose(0, 2, 1, 3)
        .reshape(3, REPLICAS * SEGS * OWN, 1)
    )
    left = expand_hidden(hidden, spread, widen, same)
    encoded = encode(left, own, other, scale)
    received = lax.all_to_all(
        encoded.reshape(REPLICAS, SEGS * OWN, SEG), ("z_lo", "x"), 0, 0, tiled=True
    )

    turned_weight = rotate_weight(w_down, sign_row, had)
    mixed = pre_grad_product(own, other, turned_weight, slope, widen)
    halves = mixed.reshape(2, PEERS, 2, ROWS)
    zero = jnp.where(core == 0, halves[0], halves[1])
    one = jnp.where(core == 0, halves[1], halves[0])
    pre_grad = jnp.stack([zero, one], axis=1).reshape(TOK, ROWS)

    offset = lax.axis_index(("z_lo", "x")) * OWN
    own_power = jnp.exp2(lax.dynamic_slice_in_dim(scale_power, offset, OWN, 0))
    own_weight = lax.dynamic_slice_in_dim(w_down, offset, OWN, 0)
    grad_mean, first_new, second_new, sent = update(
        received, own_power, sign_row, had, first_moment, second_moment, own_weight
    )
    gathered = lax.all_to_all(
        jnp.broadcast_to(sent[None], (REPLICAS, SEGS * OWN, SEG)),
        ("z_lo", "x"),
        0,
        0,
        tiled=True,
    )
    weight_new = place(gathered)
    return (pre_grad, grad_mean, first_new, second_new, weight_new)


def solution(mesh):
    fine = Mesh(
        mesh.devices.reshape(2, 8, 4, 8, 2), ("z_lo", "x", "z_hi", "y", "core")
    )
    dp = ("z_lo", "x")
    mp = ("z_hi", "y", "core")
    placed = (
        P(dp + mp, None),
        P(dp, mp),
        P(mp, None),
        P(mp + dp, None),
        P(mp + dp, None),
        P(),
        P(mp, None),
    )
    return jax.shard_map(
        body,
        mesh=fine,
        in_specs=placed,
        out_specs=(
            P(dp, mp),
            P(mp + dp, None),
            P(mp + dp, None),
            P(mp + dp, None),
            P(mp, None),
        ),
        check_vma=False,
    )
```

```python
import functools

import jax
import jax.numpy as jnp
import numpy as np
from jax import lax
from jax.experimental import pallas as pl
from jax.experimental.pallas import tpu as pltpu
from jax.sharding import Mesh
from jax.sharding import PartitionSpec as P

hadamard_norm = 0.03125
clip_limit = 448.0
root_half = 0.7071067811865476
density_norm = 0.3989422804014327

REPLICAS = 16
ROWS = 192
OWN = 12
COLS = 6144
HALF = 3072
SEGS = 4
SEG = 768
BLOCKS = 3
TOK = 128
LINE = 8
SHARE = LINE * OWN
PEERS = 32
LANES = 128
TILE = 256
bf16 = jnp.bfloat16
f32 = jnp.float32


def hadamard(order):
    indices = np.arange(order)
    common = indices[:, None] & indices[None, :]
    parity = np.zeros((order, order), np.int64)
    for position in range(order.bit_length() - 1):
        parity += common >> position & 1
    return (1 - 2 * (parity % 2)).astype(np.float32)


def tables():
    row = np.arange(LINE * SEGS * OWN)
    owner, segment, own = row // (SEGS * OWN), row % (SEGS * OWN) // OWN, row % OWN
    spread = (owner * OWN + own)[:, None] == np.arange(SHARE)[None, :]
    col = np.arange(2 * PEERS * SEGS * 2)
    patch = col // (SEGS * 2) * 2 + col % 2
    col_segment = col % (SEGS * 2) // 2
    widen = np.arange(TOK)[:, None] == patch[None, :]
    same = segment[:, None] == col_segment[None, :]
    return [jnp.asarray(table, bf16) for table in (spread, widen, same)]


def butterfly(parts):
    parts = list(parts)
    span = 1
    while span < len(parts):
        for start in range(0, len(parts), 2 * span):
            for k in range(start, start + span):
                first, second = parts[k], parts[k + span]
                parts[k], parts[k + span] = first + second, first - second
        span *= 2
    return parts


def whole(shape):
    return pl.BlockSpec(shape, lambda *_: (0,) * len(shape))


def params(mebibytes=8):
    return pltpu.CompilerParams(vmem_limit_bytes=mebibytes << 20)


def rotate_upstream_kernel(u_ref, sign_ref, had_ref, low_ref, high_ref, x_ref, z_ref):
    turned = u_ref[...].astype(f32) * sign_ref[...]
    for t in range(COLS // LANES):
        x_ref[2 * t : 2 * t + 2, :] = turned[:, LANES * t : LANES * (t + 1)]
    x_ref[...] = jnp.dot(
        x_ref[...].astype(bf16), had_ref[...], preferred_element_type=f32
    )
    for half, out_ref in enumerate((low_ref, high_ref)):
        for b in range(BLOCKS):
            base = half * HALF // LANES + 8 * b
            mixed = butterfly([x_ref[2 * t : 2 * t + 2, :] for t in range(base, base + 8)])
            for k, part in enumerate(mixed):
                s, lane = divmod(8 * b + k, SEG // LANES)
                z_ref[2 * s : 2 * s + 2, LANES * lane : LANES * (lane + 1)] = (
                    part * hadamard_norm
                )
        out_ref[...] = z_ref[...].astype(bf16)


def rotate_upstream(upstream, sign_row, had):
    part = jax.ShapeDtypeStruct((2 * SEGS, SEG), bf16)
    return pl.pallas_call(
        rotate_upstream_kernel,
        out_shape=(part, part),
        scratch_shapes=[
            pltpu.VMEM((2 * COLS // LANES, LANES), f32),
            pltpu.VMEM((2 * SEGS, SEG), f32),
        ],
        compiler_params=params(),
        name="rotate_upstream",
    )(upstream, sign_row, had)


def expand_hidden_kernel(hidden_ref, spread_ref, widen_ref, same_ref, out_ref):
    rows = lax.dot_general(
        spread_ref[...],
        hidden_ref[...],
        (((1,), (1,)), ((), ())),
        preferred_element_type=f32,
    ).astype(bf16)
    wide = jnp.dot(rows, widen_ref[...], preferred_element_type=f32)
    out_ref[...] = (wide * same_ref[...].astype(f32)).astype(bf16)


def expand_hidden(hidden, spread, widen, same):
    return pl.pallas_call(
        expand_hidden_kernel,
        out_shape=jax.ShapeDtypeStruct(same.shape, bf16),
        compiler_params=params(),
        cost_estimate=pl.CostEstimate(
            flops=2 * 768 * 128 * 700, bytes_accessed=4 << 20, transcendentals=0
        ),
        name="expand_hidden",
    )(hidden, spread, widen, same)


def encode_kernel(
    mine_ref, theirs_ref, own0_ref, other0_ref, own1_ref, other1_ref, scale_ref, out_ref
):
    total = None
    for left_ref, own_ref, other_ref in (
        (mine_ref, own0_ref, other0_ref),
        (theirs_ref, own1_ref, other1_ref),
    ):
        half = own_ref.shape[0]
        term = jnp.dot(left_ref[:, :half], own_ref[...], preferred_element_type=f32)
        term += jnp.dot(left_ref[:, half:], other_ref[...], preferred_element_type=f32)
        term = jnp.clip(term * scale_ref[0], -clip_limit, clip_limit)
        term = term.astype(bf16).astype(f32)
        total = term if total is None else total + term
    out_ref[...] = total.astype(bf16)


def encode(mine, theirs, parts, scale):
    rows = mine.shape[0]
    depth = parts[0].shape[0]
    return pl.pallas_call(
        encode_kernel,
        out_shape=jax.ShapeDtypeStruct((rows, SEG), bf16),
        grid=(SEG // TILE,),
        in_specs=[whole(mine.shape), whole(theirs.shape)]
        + [pl.BlockSpec((depth, TILE), lambda n: (0, n))] * 4
        + [pl.BlockSpec((1, rows, 1), lambda n: (n, 0, 0))],
        out_specs=pl.BlockSpec((rows, TILE), lambda n: (0, n)),
        compiler_params=params(12),
        cost_estimate=pl.CostEstimate(
            flops=8 * rows * depth * SEG, bytes_accessed=4 << 20, transcendentals=0
        ),
        name="encode",
    )(mine, theirs, *parts, scale)


def update_kernel(
    half, received_ref, power_ref, sign_ref, had_ref, first_ref, second_ref,
    weight_ref, *refs,
):
    mean_ref, first_out, second_out, sent_ref, sum_ref, x_ref, y_ref = refs[-7:]
    total = received_ref[0].astype(f32)
    for source in range(1, received_ref.shape[0]):
        total += received_ref[source].astype(f32)
    sum_ref[...] = total
    x_ref[...] = jnp.zeros_like(x_ref)
    for t in range(HALF // LANES):
        s, lane = divmod(t, SEG // LANES)
        block = BLOCKS * half + t // 8
        x_ref[16 * t : 16 * t + OWN, :] = (
            sum_ref[OWN * s : OWN * (s + 1), LANES * lane : LANES * (lane + 1)]
            * power_ref[:, block : block + 1]
        )
    x = x_ref[...]
    high = x.astype(bf16)
    low = (x - high.astype(f32)).astype(bf16)
    y_ref[...] = jnp.dot(high, had_ref[...], preferred_element_type=f32) + jnp.dot(
        low, had_ref[...], preferred_element_type=f32
    )
    for b in range(BLOCKS):
        mixed = butterfly(
            [y_ref[16 * t : 16 * t + OWN, :] for t in range(8 * b, 8 * b + 8)]
        )
        for k, part in enumerate(mixed):
            t = 8 * b + k
            s, lane = divmod(t, SEG // LANES)
            lanes = slice(LANES * t, LANES * (t + 1))
            mean = part * (hadamard_norm / REPLICAS) * sign_ref[:, lanes]
            mean_ref[:, lanes] = mean
            first = 0.9 * first_ref[:, lanes] + 0.1 * mean
            second = 0.95 * second_ref[:, lanes] + 0.05 * mean * mean
            first_out[:, lanes] = first
            second_out[:, lanes] = second
            adjusted = first / 0.6513215599 / (jnp.sqrt(second / 0.4012630608) + 1e-08)
            sum_ref[OWN * s : OWN * (s + 1), LANES * lane : LANES * (lane + 1)] = (
                weight_ref[:, lanes].astype(f32) * (1.0 - 0.01 * 0.1) - 0.01 * adjusted
            )
    sent_ref[...] = sum_ref[...].astype(bf16)


def update(half, received, power, sign_row, had, first, second, weight, earlier):
    own = jax.ShapeDtypeStruct((OWN, COLS), f32)
    sent = jax.ShapeDtypeStruct((SEGS * OWN, SEG), bf16)

    def part(rows):
        return pl.BlockSpec((rows, HALF), lambda _: (0, half))

    kept = [pl.BlockSpec(memory_space=pl.ANY)] * len(earlier)
    return pl.pallas_call(
        functools.partial(update_kernel, half),
        out_shape=(own, own, own, sent),
        grid=(1,),
        in_specs=[
            whole(received.shape),
            whole(power.shape),
            part(1),
            whole(had.shape),
            part(OWN),
            part(OWN),
            part(OWN),
        ]
        + kept,
        out_specs=(part(OWN), part(OWN), part(OWN), whole(sent.shape)),
        scratch_shapes=[
            pltpu.VMEM((SEGS * OWN, SEG), f32),
            pltpu.VMEM((16 * HALF // LANES, LANES), f32),
            pltpu.VMEM((16 * HALF // LANES, LANES), f32),
        ],
        input_output_aliases={7 + k: k for k in range(len(earlier))},
        compiler_params=params(),
        name=f"update_{half}",
    )(received, power, sign_row, had, first, second, weight, *earlier)


def place_kernel(plane_ref, own_ref, other_ref, direct_ref, out_ref, rows_ref):
    plane = plane_ref[0]
    for d in range(REPLICAS):
        here = plane == d // LINE
        near = jnp.where(here, own_ref[d % LINE], other_ref[d % LINE]).astype(f32)
        far = direct_ref[d].astype(f32)
        for half, chunk in enumerate((near, far)):
            for s in range(SEGS):
                start = half * HALF + SEG * s
                rows_ref[OWN * d : OWN * (d + 1), start : start + SEG] = chunk[
                    OWN * s : OWN * (s + 1), :
                ]
    out_ref[...] = rows_ref[...].astype(bf16)


def place(plane, own, other, direct):
    return pl.pallas_call(
        place_kernel,
        out_shape=jax.ShapeDtypeStruct((ROWS, COLS), bf16),
        in_specs=[pl.BlockSpec(memory_space=pltpu.SMEM)]
        + [pl.BlockSpec(memory_space=pltpu.VMEM)] * 3,
        scratch_shapes=[pltpu.VMEM((ROWS, COLS), f32)],
        compiler_params=params(20),
        name="place",
    )(plane, own, other, direct)


def rotate_weight_kernel(w_ref, sign_ref, had_ref, out_ref):
    turned = w_ref[...].astype(f32) * sign_ref[...]
    parts = [
        jnp.dot(
            turned[:, LANES * k : LANES * (k + 1)].astype(bf16),
            had_ref[...],
            preferred_element_type=f32,
        )
        for k in range(8)
    ]
    for k, part in enumerate(butterfly(parts)):
        out_ref[:, LANES * k : LANES * (k + 1)] = (part * hadamard_norm).astype(bf16)


def rotate_weight(weight, sign_row, had):
    return pl.pallas_call(
        rotate_weight_kernel,
        out_shape=jax.ShapeDtypeStruct((ROWS, COLS), bf16),
        grid=(COLS // 1024,),
        in_specs=[
            pl.BlockSpec((ROWS, 1024), lambda b: (0, b)),
            pl.BlockSpec((1, 1024), lambda b: (0, b)),
            whole((LANES, LANES)),
        ],
        out_specs=pl.BlockSpec((ROWS, 1024), lambda b: (0, b)),
        compiler_params=params(),
        cost_estimate=pl.CostEstimate(
            flops=2 * ROWS * COLS * 1024, bytes_accessed=5 << 20, transcendentals=0
        ),
        name="rotate_weight",
    )(weight, sign_row, had)


def pre_grad_kernel(
    own0_ref, other0_ref, own1_ref, other1_ref, w_ref, slope_ref, collect_ref,
    out_ref, acc_ref,
):
    rows = own0_ref.shape[0]
    place_in_pair = lax.broadcasted_iota(jnp.int32, (rows, 1), 0) & (2 * SEGS - 1)
    for index, refs in enumerate(((own0_ref, own1_ref), (other0_ref, other1_ref))):
        total = None
        for half, rows_ref in enumerate(refs):
            left = rows_ref[...]
            chosen = jnp.zeros((rows, ROWS), f32)
            for s in range(SEGS):
                column = half * HALF + SEG * s
                part = lax.dot_general(
                    left,
                    w_ref[:, column : column + SEG],
                    (((1,), (1,)), ((), ())),
                    preferred_element_type=f32,
                )
                chosen = jnp.where(place_in_pair >> 1 == s, part, chosen)
            total = chosen if total is None else total + chosen
        acc_ref[rows * index : rows * (index + 1), :] = total
    hidden_grad = jnp.dot(
        collect_ref[...].astype(f32),
        acc_ref[...],
        precision=lax.Precision.HIGHEST,
        preferred_element_type=f32,
    )
    out_ref[...] = (hidden_grad * slope_ref[...]).astype(bf16)


def pre_grad_product(own0, other0, own1, other1, weight, slope, collect):
    return pl.pallas_call(
        pre_grad_kernel,
        out_shape=jax.ShapeDtypeStruct((TOK, ROWS), bf16),
        scratch_shapes=[pltpu.VMEM((2 * own0.shape[0], ROWS), f32)],
        compiler_params=params(16),
        cost_estimate=pl.CostEstimate(
            flops=8 * 512 * 1536 * ROWS, bytes_accessed=6 << 20, transcendentals=0
        ),
        name="pre_grad",
    )(own0, other0, own1, other1, weight, slope, collect)


def swap(values, axis):
    return lax.ppermute(values, axis, [(0, 1), (1, 0)])


def to_all(values, axes, count):
    return lax.all_to_all(
        jnp.broadcast_to(values[None], (count,) + values.shape), axes, 0, 0, tiled=True
    )


def body(upstream, pre_act, w_down, first_moment, second_moment, signs, exponents):
    spread, widen, same = tables()
    had = jnp.asarray(hadamard(LANES), bf16)
    sign_row = (1 - 2 * signs).astype(f32).reshape(1, COLS)
    core = lax.axis_index("core")
    plane = lax.axis_index("z_lo")
    plane_array = plane.astype(jnp.int32).reshape(1)

    pairs = pre_act.reshape(PEERS, 2, 2, ROWS)
    mine = jnp.where(core == 0, pairs[:, 0], pairs[:, 1]).reshape(TOK // 2, ROWS)
    yours = jnp.where(core == 0, pairs[:, 1], pairs[:, 0]).reshape(TOK // 2, ROWS)
    ordered = jnp.concatenate([mine, yours], axis=0)
    kept = jnp.where(plane == 0, ordered[:, :SHARE], ordered[:, SHARE:])
    given = jnp.where(plane == 0, ordered[:, SHARE:], ordered[:, :SHARE])
    taken = swap(given, "z_lo")

    rotated = rotate_upstream(upstream, sign_row, had)
    own = [to_all(part, ("z_hi", "y"), PEERS).reshape(-1, SEG) for part in rotated]
    other = [swap(part, "core") for part in own]
    partner = [swap(part, "z_lo") for part in own]
    partner_other = [swap(part, "core") for part in partner]

    preact = ordered.astype(f32)
    normal_cdf = 0.5 * (1.0 + lax.erf(preact * root_half))
    slope = normal_cdf + preact * jnp.exp(-0.5 * preact * preact) * density_norm

    def activate(values):
        values = values.astype(f32)
        return (values * (0.5 * (1.0 + lax.erf(values * root_half)))).astype(bf16)

    left = [
        expand_hidden(activate(values), spread, widen, same)
        for values in (kept, taken)
    ]

    scale_power = exponents.astype(f32)
    shrink = jnp.exp2(-jnp.where(plane == 0, scale_power[:SHARE], scale_power[SHARE:]))
    offset = lax.axis_index(("z_lo", "x")) * OWN
    own_power = jnp.exp2(lax.dynamic_slice_in_dim(scale_power, offset, OWN, 0))
    own_weight = lax.dynamic_slice_in_dim(w_down, offset, OWN, 0)

    received = []
    for half in range(2):
        picked = jnp.stack(
            [
                shrink[:, BLOCKS * half + (3 * s + n) // 4]
                for n in range(SEG // TILE)
                for s in range(SEGS)
            ],
            axis=0,
        )
        scale = (
            picked.reshape(SEG // TILE, SEGS, LINE, OWN)
            .transpose(0, 2, 1, 3)
            .reshape(SEG // TILE, LINE * SEGS * OWN, 1)
        )
        parts = (own[half], other[half], partner[half], partner_other[half])
        encoded = encode(left[0], left[1], parts, scale)
        received.append(
            lax.all_to_all(
                encoded.reshape(LINE, SEGS * OWN, SEG), "x", 0, 0, tiled=True
            )
        )

    states = (sign_row, had, first_moment, second_moment, own_weight)
    *earlier, sent0 = update(0, received[0], own_power, *states, ())
    near = to_all(sent0, "x", LINE)
    across = swap(near, "z_lo")
    *updated, sent1 = update(1, received[1], own_power, *states, earlier)
    direct = to_all(sent1, ("z_lo", "x"), REPLICAS)

    turned_weight = rotate_weight(w_down, sign_row, had)
    mixed = pre_grad_product(
        own[0], other[0], own[1], other[1], turned_weight, slope, widen
    )
    halves = mixed.reshape(2, PEERS, 2, ROWS)
    zero = jnp.where(core == 0, halves[0], halves[1])
    one = jnp.where(core == 0, halves[1], halves[0])
    pre_grad = jnp.stack([zero, one], axis=1).reshape(TOK, ROWS)

    weight_new = place(plane_array, near, across, direct)
    return (pre_grad, *updated, weight_new)


def solution(mesh):
    fine = Mesh(
        mesh.devices.reshape(2, 8, 4, 8, 2), ("z_lo", "x", "z_hi", "y", "core")
    )
    dp = ("z_lo", "x")
    mp = ("z_hi", "y", "core")
    placed = (
        P(dp + mp, None),
        P(dp, mp),
        P(mp, None),
        P(mp + dp, None),
        P(mp + dp, None),
        P(),
        P(mp, None),
    )
    return jax.shard_map(
        body,
        mesh=fine,
        in_specs=placed,
        out_specs=(
            P(dp, mp),
            P(mp + dp, None),
            P(mp + dp, None),
            P(mp + dp, None),
            P(mp, None),
        ),
        check_vma=False,
    )
```

```python
import functools

import jax
import jax.numpy as jnp
import numpy as np
from jax import lax
from jax.experimental import pallas as pl
from jax.experimental.pallas import tpu as pltpu
from jax.sharding import Mesh
from jax.sharding import PartitionSpec as P

hadamard_norm = 0.03125
clip_limit = 448.0
root_half = 0.7071067811865476
density_norm = 0.3989422804014327

REPLICAS = 16
ROWS = 192
OWN = 12
COLS = 6144
HALF = 3072
SEGS = 4
SEG = 768
BLOCKS = 3
TOK = 128
LINE = 8
PEERS = 32
LANES = 128
TILE = 256
bf16 = jnp.bfloat16
f32 = jnp.float32


def hadamard(order):
    indices = np.arange(order)
    common = indices[:, None] & indices[None, :]
    parity = np.zeros((order, order), np.int64)
    for position in range(order.bit_length() - 1):
        parity += common >> position & 1
    return (1 - 2 * (parity % 2)).astype(np.float32)


def tables():
    row = np.arange(REPLICAS * SEGS * OWN)
    owner, segment, own = row // (SEGS * OWN), row % (SEGS * OWN) // OWN, row % OWN
    spread = (owner * OWN + own)[:, None] == np.arange(ROWS)[None, :]
    col = np.arange(2 * PEERS * SEGS * 2)
    patch = col // (SEGS * 2) * 2 + col % 2
    col_segment = col % (SEGS * 2) // 2
    widen = np.arange(TOK)[:, None] == patch[None, :]
    same = segment[:, None] == col_segment[None, :]
    return [jnp.asarray(table, bf16) for table in (spread, widen, same)]


def butterfly(parts):
    parts = list(parts)
    span = 1
    while span < len(parts):
        for start in range(0, len(parts), 2 * span):
            for k in range(start, start + span):
                first, second = parts[k], parts[k + span]
                parts[k], parts[k + span] = first + second, first - second
        span *= 2
    return parts


def whole(shape):
    return pl.BlockSpec(shape, lambda *_: (0,) * len(shape))


def params(mebibytes=8):
    return pltpu.CompilerParams(vmem_limit_bytes=mebibytes << 20)


def rotate_upstream_kernel(u_ref, sign_ref, had_ref, out_ref, x_ref, z_ref):
    turned = u_ref[...].astype(f32) * sign_ref[...]
    for t in range(COLS // LANES):
        x_ref[2 * t : 2 * t + 2, :] = turned[:, LANES * t : LANES * (t + 1)]
    x_ref[...] = jnp.dot(
        x_ref[...].astype(bf16), had_ref[...], preferred_element_type=f32
    )
    for half in range(2):
        for b in range(BLOCKS):
            base = half * HALF // LANES + 8 * b
            mixed = butterfly([x_ref[2 * t : 2 * t + 2, :] for t in range(base, base + 8)])
            for k, part in enumerate(mixed):
                s, lane = divmod(8 * b + k, SEG // LANES)
                start = half * SEG + LANES * lane
                z_ref[2 * s : 2 * s + 2, start : start + LANES] = part * hadamard_norm
    out_ref[...] = z_ref[...].astype(bf16)


def rotate_upstream(upstream, sign_row, had):
    return pl.pallas_call(
        rotate_upstream_kernel,
        out_shape=jax.ShapeDtypeStruct((2 * SEGS, 2 * SEG), bf16),
        scratch_shapes=[
            pltpu.VMEM((2 * COLS // LANES, LANES), f32),
            pltpu.VMEM((2 * SEGS, 2 * SEG), f32),
        ],
        compiler_params=params(),
        name="rotate_upstream",
    )(upstream, sign_row, had)


def expand_hidden_kernel(hidden_ref, spread_ref, widen_ref, same_ref, out_ref):
    rows = lax.dot_general(
        spread_ref[...],
        hidden_ref[...],
        (((1,), (1,)), ((), ())),
        preferred_element_type=f32,
    ).astype(bf16)
    wide = jnp.dot(rows, widen_ref[...], preferred_element_type=f32)
    out_ref[...] = (wide * same_ref[...].astype(f32)).astype(bf16)


def expand_hidden(hidden, spread, widen, same):
    return pl.pallas_call(
        expand_hidden_kernel,
        out_shape=jax.ShapeDtypeStruct(same.shape, bf16),
        compiler_params=params(),
        cost_estimate=pl.CostEstimate(
            flops=2 * 768 * 128 * 700, bytes_accessed=4 << 20, transcendentals=0
        ),
        name="expand_hidden",
    )(hidden, spread, widen, same)


def encode_kernel(by_line, left_ref, own_ref, other_ref, scale_ref, out_ref):
    half = own_ref.shape[0]
    total = jnp.dot(left_ref[:, :half], own_ref[...], preferred_element_type=f32)
    total += jnp.dot(left_ref[:, half:], other_ref[...], preferred_element_type=f32)
    total = jnp.clip(total * scale_ref[0], -clip_limit, clip_limit).astype(bf16)
    step = SEGS * OWN
    for d in range(REPLICAS):
        to = d % LINE * 2 + d // LINE if by_line else d
        out_ref[step * to : step * (to + 1), :] = total[step * d : step * (d + 1), :]


def encode(half, by_line, left, own, other, scale):
    rows = left.shape[0]
    depth = own.shape[0]
    tiles = SEG // TILE
    return pl.pallas_call(
        functools.partial(encode_kernel, by_line),
        out_shape=jax.ShapeDtypeStruct((rows, SEG), bf16),
        grid=(tiles,),
        in_specs=[
            whole(left.shape),
            pl.BlockSpec((depth, TILE), lambda n: (0, half * tiles + n)),
            pl.BlockSpec((depth, TILE), lambda n: (0, half * tiles + n)),
            pl.BlockSpec((1, rows, 1), lambda n: (n, 0, 0)),
        ],
        out_specs=pl.BlockSpec((rows, TILE), lambda n: (0, n)),
        compiler_params=params(12),
        cost_estimate=pl.CostEstimate(
            flops=4 * rows * depth * SEG, bytes_accessed=4 << 20, transcendentals=0
        ),
        name=f"encode_{half}",
    )(left, own, other, scale)


def update_kernel(
    half, count, power_ref, sign_ref, had_ref, first_ref, second_ref, weight_ref, *refs
):
    mean_ref, first_out, second_out, sent_ref, sum_ref, x_ref, y_ref = refs[-7:]
    total = None
    for received_ref in refs[:count]:
        for source in range(received_ref.shape[0]):
            term = received_ref[source].astype(f32)
            total = term if total is None else total + term
    sum_ref[...] = total
    x_ref[...] = jnp.zeros_like(x_ref)
    for t in range(HALF // LANES):
        s, lane = divmod(t, SEG // LANES)
        block = BLOCKS * half + t // 8
        x_ref[16 * t : 16 * t + OWN, :] = (
            sum_ref[OWN * s : OWN * (s + 1), LANES * lane : LANES * (lane + 1)]
            * power_ref[:, block : block + 1]
        )
    x = x_ref[...]
    high = x.astype(bf16)
    low = (x - high.astype(f32)).astype(bf16)
    y_ref[...] = jnp.dot(high, had_ref[...], preferred_element_type=f32) + jnp.dot(
        low, had_ref[...], preferred_element_type=f32
    )
    for b in range(BLOCKS):
        mixed = butterfly(
            [y_ref[16 * t : 16 * t + OWN, :] for t in range(8 * b, 8 * b + 8)]
        )
        for k, part in enumerate(mixed):
            t = 8 * b + k
            s, lane = divmod(t, SEG // LANES)
            lanes = slice(LANES * t, LANES * (t + 1))
            mean = part * (hadamard_norm / REPLICAS) * sign_ref[:, lanes]
            mean_ref[:, lanes] = mean
            first = 0.9 * first_ref[:, lanes] + 0.1 * mean
            second = 0.95 * second_ref[:, lanes] + 0.05 * mean * mean
            first_out[:, lanes] = first
            second_out[:, lanes] = second
            adjusted = first / 0.6513215599 / (jnp.sqrt(second / 0.4012630608) + 1e-08)
            sum_ref[OWN * s : OWN * (s + 1), LANES * lane : LANES * (lane + 1)] = (
                weight_ref[:, lanes].astype(f32) * (1.0 - 0.01 * 0.1) - 0.01 * adjusted
            )
    sent_ref[...] = sum_ref[...].astype(bf16)


def update(half, received, power, sign_row, had, first, second, weight, earlier):
    own = jax.ShapeDtypeStruct((OWN, COLS), f32)
    sent = jax.ShapeDtypeStruct((SEGS * OWN, SEG), bf16)

    def part(rows):
        return pl.BlockSpec((rows, HALF), lambda _: (0, half))

    kept = [pl.BlockSpec(memory_space=pl.ANY)] * len(earlier)
    return pl.pallas_call(
        functools.partial(update_kernel, half, len(received)),
        out_shape=(own, own, own, sent),
        grid=(1,),
        in_specs=[
            whole(power.shape),
            part(1),
            whole(had.shape),
            part(OWN),
            part(OWN),
            part(OWN),
        ]
        + [whole(array.shape) for array in received]
        + kept,
        out_specs=(part(OWN), part(OWN), part(OWN), whole(sent.shape)),
        scratch_shapes=[
            pltpu.VMEM((SEGS * OWN, SEG), f32),
            pltpu.VMEM((16 * HALF // LANES, LANES), f32),
            pltpu.VMEM((16 * HALF // LANES, LANES), f32),
        ],
        input_output_aliases={6 + len(received) + k: k for k in range(len(earlier))},
        compiler_params=params(),
        name=f"update_{half}",
    )(power, sign_row, had, first, second, weight, *received, *earlier)


def place_kernel(by_line, chunks_ref, *refs):
    out_ref, rows_ref = refs[-2:]
    for d in range(REPLICAS):
        source = d % LINE * 2 + d // LINE if by_line else d
        chunk = chunks_ref[source].astype(f32)
        for s in range(SEGS):
            rows_ref[OWN * d : OWN * (d + 1), SEG * s : SEG * (s + 1)] = chunk[
                OWN * s : OWN * (s + 1), :
            ]
    out_ref[...] = rows_ref[...].astype(bf16)


def place(half, by_line, chunks, earlier, flops):
    return pl.pallas_call(
        functools.partial(place_kernel, by_line),
        out_shape=jax.ShapeDtypeStruct((ROWS, COLS), bf16),
        grid=(1,),
        in_specs=[whole(chunks.shape)]
        + [pl.BlockSpec(memory_space=pl.ANY)] * len(earlier),
        out_specs=pl.BlockSpec((ROWS, HALF), lambda _: (0, half)),
        scratch_shapes=[pltpu.VMEM((ROWS, HALF), f32)],
        input_output_aliases={1 + k: k for k in range(len(earlier))},
        compiler_params=params(12),
        cost_estimate=pl.CostEstimate(
            flops=flops, bytes_accessed=3 << 20, transcendentals=0
        ),
        name=f"place_{half}",
    )(chunks, *earlier)


def rotate_weight_kernel(w_ref, sign_ref, had_ref, out_ref):
    turned = w_ref[...].astype(f32) * sign_ref[...]
    parts = [
        jnp.dot(
            turned[:, LANES * k : LANES * (k + 1)].astype(bf16),
            had_ref[...],
            preferred_element_type=f32,
        )
        for k in range(8)
    ]
    for k, part in enumerate(butterfly(parts)):
        out_ref[:, LANES * k : LANES * (k + 1)] = (part * hadamard_norm).astype(bf16)


def rotate_weight(weight, sign_row, had):
    return pl.pallas_call(
        rotate_weight_kernel,
        out_shape=jax.ShapeDtypeStruct((ROWS, COLS), bf16),
        grid=(COLS // 1024,),
        in_specs=[
            pl.BlockSpec((ROWS, 1024), lambda b: (0, b)),
            pl.BlockSpec((1, 1024), lambda b: (0, b)),
            whole((LANES, LANES)),
        ],
        out_specs=pl.BlockSpec((ROWS, 1024), lambda b: (0, b)),
        compiler_params=params(),
        cost_estimate=pl.CostEstimate(
            flops=2 * ROWS * COLS * 1024, bytes_accessed=5 << 20, transcendentals=0
        ),
        name="rotate_weight",
    )(weight, sign_row, had)


def pre_grad_kernel(own_ref, other_ref, w_ref, slope_ref, collect_ref, out_ref, acc_ref):
    rows = own_ref.shape[0]
    place_in_pair = lax.broadcasted_iota(jnp.int32, (rows, 1), 0) & (2 * SEGS - 1)
    for index, rows_ref in enumerate((own_ref, other_ref)):
        total = None
        for half in range(2):
            left = rows_ref[:, SEG * half : SEG * (half + 1)]
            chosen = jnp.zeros((rows, ROWS), f32)
            for s in range(SEGS):
                column = half * HALF + SEG * s
                part = lax.dot_general(
                    left,
                    w_ref[:, column : column + SEG],
                    (((1,), (1,)), ((), ())),
                    preferred_element_type=f32,
                )
                chosen = jnp.where(place_in_pair >> 1 == s, part, chosen)
            total = chosen if total is None else total + chosen
        acc_ref[rows * index : rows * (index + 1), :] = total
    hidden_grad = jnp.dot(
        collect_ref[...].astype(f32),
        acc_ref[...],
        precision=lax.Precision.HIGHEST,
        preferred_element_type=f32,
    )
    out_ref[...] = (hidden_grad * slope_ref[...]).astype(bf16)


def pre_grad_product(own, other, weight, slope, collect):
    return pl.pallas_call(
        pre_grad_kernel,
        out_shape=jax.ShapeDtypeStruct((TOK, ROWS), bf16),
        scratch_shapes=[pltpu.VMEM((2 * own.shape[0], ROWS), f32)],
        compiler_params=params(16),
        cost_estimate=pl.CostEstimate(
            flops=8 * 512 * 1536 * ROWS, bytes_accessed=6 << 20, transcendentals=0
        ),
        name="pre_grad",
    )(own, other, weight, slope, collect)


def swap(values, axis):
    return lax.ppermute(values, axis, [(0, 1), (1, 0)])


def to_all(values, axes, count):
    return lax.all_to_all(
        jnp.broadcast_to(values[None], (count,) + values.shape), axes, 0, 0, tiled=True
    )


def body(upstream, pre_act, w_down, first_moment, second_moment, signs, exponents):
    spread, widen, same = tables()
    had = jnp.asarray(hadamard(LANES), bf16)
    sign_row = (1 - 2 * signs).astype(f32).reshape(1, COLS)
    core = lax.axis_index("core")
    plane = lax.axis_index("z_lo")

    rotated = rotate_upstream(upstream, sign_row, had)
    own = to_all(rotated, ("z_hi", "y"), PEERS).reshape(-1, 2 * SEG)
    other = swap(own, "core")

    pairs = pre_act.reshape(PEERS, 2, 2, ROWS)
    mine = jnp.where(core == 0, pairs[:, 0], pairs[:, 1]).reshape(TOK // 2, ROWS)
    yours = jnp.where(core == 0, pairs[:, 1], pairs[:, 0]).reshape(TOK // 2, ROWS)
    preact = jnp.concatenate([mine, yours], axis=0).astype(f32)
    normal_cdf = 0.5 * (1.0 + lax.erf(preact * root_half))
    hidden = (preact * normal_cdf).astype(bf16)
    slope = normal_cdf + preact * jnp.exp(-0.5 * preact * preact) * density_norm
    left = expand_hidden(hidden, spread, widen, same)

    scale_power = exponents.astype(f32)
    shrink = jnp.exp2(-scale_power)
    offset = lax.axis_index(("z_lo", "x")) * OWN
    own_power = jnp.exp2(lax.dynamic_slice_in_dim(scale_power, offset, OWN, 0))
    own_weight = lax.dynamic_slice_in_dim(w_down, offset, OWN, 0)

    encoded = []
    for half in range(2):
        picked = jnp.stack(
            [
                shrink[:, BLOCKS * half + (3 * s + n) // 4]
                for n in range(SEG // TILE)
                for s in range(SEGS)
            ],
            axis=0,
        )
        scale = (
            picked.reshape(SEG // TILE, SEGS, REPLICAS, OWN)
            .transpose(0, 2, 1, 3)
            .reshape(SEG // TILE, REPLICAS * SEGS * OWN, 1)
        )
        encoded.append(encode(half, half == 0, left, own, other, scale))

    along = lax.psum_scatter(encoded[0], "x", scatter_dimension=0, tiled=True)
    terms = lax.all_to_all(
        encoded[1].reshape(REPLICAS, SEGS * OWN, SEG), ("z_lo", "x"), 0, 0, tiled=True
    )
    states = (sign_row, had, first_moment, second_moment, own_weight)
    *earlier, sent1 = update(1, [terms], own_power, *states, ())
    across = swap(sent1, "z_lo")
    both = jnp.where(
        plane == 0,
        jnp.concatenate([sent1, across], axis=0),
        jnp.concatenate([across, sent1], axis=0),
    )
    turned_weight = rotate_weight(w_down, sign_row, had)
    mixed = pre_grad_product(own, other, turned_weight, slope, widen)
    halves = mixed.reshape(2, PEERS, 2, ROWS)
    zero = jnp.where(core == 0, halves[0], halves[1])
    one = jnp.where(core == 0, halves[1], halves[0])
    pre_grad = jnp.stack([zero, one], axis=1).reshape(TOK, ROWS)

    both, along, pre_grad = lax.optimization_barrier((both, along, pre_grad))
    line = lax.all_gather(both, "x", axis=0, tiled=True)
    upper, lower = along[: SEGS * OWN], along[SEGS * OWN :]
    kept = jnp.where(plane == 0, upper, lower)
    taken = swap(jnp.where(plane == 0, lower, upper), "z_lo")
    *updated, sent0 = update(0, [kept[None], taken[None]], own_power, *states, earlier)
    direct = to_all(sent0, ("z_lo", "x"), REPLICAS)

    placed = place(1, True, line.reshape(REPLICAS, SEGS * OWN, SEG), (), 10**11)
    weight_new = place(0, False, direct, (placed,), 10**9)
    return (pre_grad, *updated, weight_new)


def solution(mesh):
    fine = Mesh(
        mesh.devices.reshape(2, 8, 4, 8, 2), ("z_lo", "x", "z_hi", "y", "core")
    )
    dp = ("z_lo", "x")
    mp = ("z_hi", "y", "core")
    placed = (
        P(dp + mp, None),
        P(dp, mp),
        P(mp, None),
        P(mp + dp, None),
        P(mp + dp, None),
        P(),
        P(mp, None),
    )
    return jax.shard_map(
        body,
        mesh=fine,
        in_specs=placed,
        out_specs=(
            P(dp, mp),
            P(mp + dp, None),
            P(mp + dp, None),
            P(mp + dp, None),
            P(mp, None),
        ),
        check_vma=False,
    )
```

```python
import functools

import jax
import jax.numpy as jnp
import numpy as np
from jax import lax
from jax.experimental import pallas as pl
from jax.experimental.pallas import tpu as pltpu
from jax.sharding import Mesh
from jax.sharding import PartitionSpec as P

hadamard_norm = 0.03125
clip_limit = 448.0
root_half = 0.7071067811865476
density_norm = 0.3989422804014327

REPLICAS = 16
ROWS = 192
OWN = 12
COLS = 6144
HALF = 3072
SEGS = 4
SEG = 768
BLOCKS = 3
TOK = 128
LINE = 8
PEERS = 32
LANES = 128
TILE = 256
bf16 = jnp.bfloat16
f32 = jnp.float32


def hadamard(order):
    indices = np.arange(order)
    common = indices[:, None] & indices[None, :]
    parity = np.zeros((order, order), np.int64)
    for position in range(order.bit_length() - 1):
        parity += common >> position & 1
    return (1 - 2 * (parity % 2)).astype(np.float32)


def tables():
    row = np.arange(REPLICAS * SEGS * OWN)
    owner, segment, own = row // (SEGS * OWN), row % (SEGS * OWN) // OWN, row % OWN
    spread = (owner * OWN + own)[:, None] == np.arange(ROWS)[None, :]
    col = np.arange(2 * PEERS * SEGS * 2)
    patch = col // (SEGS * 2) * 2 + col % 2
    col_segment = col % (SEGS * 2) // 2
    widen = np.arange(TOK)[:, None] == patch[None, :]
    same = segment[:, None] == col_segment[None, :]
    tile = np.arange(COLS // 1024)[None, :]
    block = tile // 3 * BLOCKS + (3 * segment[:, None] + tile % 3) // 4
    choice = block[:, :, None] == np.arange(COLS // 1024)
    gather = np.repeat(np.eye(COLS // 1024), COLS // 1024, axis=0)
    shown = (spread, widen, same, choice.reshape(row.size, -1), gather)
    return [jnp.asarray(table, bf16) for table in shown]


def butterfly(parts):
    parts = list(parts)
    span = 1
    while span < len(parts):
        for start in range(0, len(parts), 2 * span):
            for k in range(start, start + span):
                first, second = parts[k], parts[k + span]
                parts[k], parts[k + span] = first + second, first - second
        span *= 2
    return parts


def whole(shape):
    return pl.BlockSpec(shape, lambda *_: (0,) * len(shape))


def params(mebibytes=8):
    return pltpu.CompilerParams(vmem_limit_bytes=mebibytes << 20)


def rotate_upstream_kernel(u_ref, sign_ref, had_ref, out_ref, x_ref, z_ref):
    turned = u_ref[...].astype(f32) * (1 - 2 * sign_ref[...]).astype(f32)
    for t in range(COLS // LANES):
        x_ref[2 * t : 2 * t + 2, :] = turned[:, LANES * t : LANES * (t + 1)]
    x_ref[...] = jnp.dot(
        x_ref[...].astype(bf16), had_ref[...], preferred_element_type=f32
    )
    for half in range(2):
        for b in range(BLOCKS):
            base = half * HALF // LANES + 8 * b
            mixed = butterfly([x_ref[2 * t : 2 * t + 2, :] for t in range(base, base + 8)])
            for k, part in enumerate(mixed):
                s, lane = divmod(8 * b + k, SEG // LANES)
                start = half * SEG + LANES * lane
                z_ref[2 * s : 2 * s + 2, start : start + LANES] = part * hadamard_norm
    out_ref[...] = z_ref[...].astype(bf16)


def rotate_upstream(upstream, signs, had):
    return pl.pallas_call(
        rotate_upstream_kernel,
        out_shape=jax.ShapeDtypeStruct((2 * SEGS, 2 * SEG), bf16),
        scratch_shapes=[
            pltpu.VMEM((2 * COLS // LANES, LANES), f32),
            pltpu.VMEM((2 * SEGS, 2 * SEG), f32),
        ],
        compiler_params=params(),
        name="rotate_upstream",
    )(upstream, signs, had)


def expand_hidden_kernel(
    hidden_ref, shrink_ref, spread_ref, widen_ref, same_ref, choice_ref, gather_ref,
    out_ref, scale_ref,
):
    rows = lax.dot_general(
        spread_ref[...],
        hidden_ref[...],
        (((1,), (1,)), ((), ())),
        preferred_element_type=f32,
    ).astype(bf16)
    wide = jnp.dot(rows, widen_ref[...], preferred_element_type=f32)
    out_ref[...] = (wide * same_ref[...].astype(f32)).astype(bf16)
    every = jnp.dot(spread_ref[...], shrink_ref[...], preferred_element_type=f32)
    chosen = (every * choice_ref[...].astype(f32)).astype(bf16)
    scale_ref[...] = jnp.dot(chosen, gather_ref[...], preferred_element_type=f32)


def expand_hidden(hidden, shrink, spread, widen, same, choice, gather):
    return pl.pallas_call(
        expand_hidden_kernel,
        out_shape=(
            jax.ShapeDtypeStruct(same.shape, bf16),
            jax.ShapeDtypeStruct((same.shape[0], gather.shape[1]), f32),
        ),
        compiler_params=params(),
        cost_estimate=pl.CostEstimate(
            flops=2 * 768 * 128 * 700, bytes_accessed=4 << 20, transcendentals=0
        ),
        name="expand_hidden",
    )(hidden, shrink, spread, widen, same, choice, gather)


def encode_kernel(half, by_line, left_ref, own_ref, other_ref, scale_ref, out_ref):
    depth = own_ref.shape[0]
    total = jnp.dot(left_ref[:, :depth], own_ref[...], preferred_element_type=f32)
    total += jnp.dot(left_ref[:, depth:], other_ref[...], preferred_element_type=f32)
    scales = scale_ref[...]
    column = lax.broadcasted_iota(jnp.int32, scales.shape, 1)
    here = column == half * (SEG // TILE) + pl.program_id(0)
    scale = jnp.sum(jnp.where(here, scales, 0.0), axis=1, keepdims=True)
    total = jnp.clip(total * scale, -clip_limit, clip_limit).astype(bf16)
    step = SEGS * OWN
    for d in range(REPLICAS):
        to = d % LINE * 2 + d // LINE if by_line else d
        out_ref[step * to : step * (to + 1), :] = total[step * d : step * (d + 1), :]


def encode(half, by_line, left, own, other, scale):
    rows = left.shape[0]
    depth = own.shape[0]
    tiles = SEG // TILE
    return pl.pallas_call(
        functools.partial(encode_kernel, half, by_line),
        out_shape=pltpu.HBM((rows, SEG), bf16),
        grid=(tiles,),
        in_specs=[
            whole(left.shape),
            pl.BlockSpec((depth, TILE), lambda n: (0, half * tiles + n)),
            pl.BlockSpec((depth, TILE), lambda n: (0, half * tiles + n)),
            whole(scale.shape),
        ],
        out_specs=pl.BlockSpec((rows, TILE), lambda n: (0, n)),
        compiler_params=params(12),
        cost_estimate=pl.CostEstimate(
            flops=4 * rows * depth * SEG, bytes_accessed=4 << 20, transcendentals=0
        ),
        name=f"encode_{half}",
    )(left, own, other, scale)


def update_kernel(
    half, count, power_ref, sign_ref, had_ref, first_ref, second_ref, weight_ref, *refs
):
    mean_ref, first_out, second_out, sent_ref, sum_ref, x_ref, y_ref = refs[-7:]
    total = None
    for received_ref in refs[:count]:
        for source in range(received_ref.shape[0]):
            term = received_ref[source].astype(f32)
            total = term if total is None else total + term
    sum_ref[...] = total
    x_ref[...] = jnp.zeros_like(x_ref)
    for t in range(HALF // LANES):
        s, lane = divmod(t, SEG // LANES)
        block = BLOCKS * half + t // 8
        x_ref[16 * t : 16 * t + OWN, :] = (
            sum_ref[OWN * s : OWN * (s + 1), LANES * lane : LANES * (lane + 1)]
            * power_ref[:, block : block + 1]
        )
    x = x_ref[...]
    high = x.astype(bf16)
    low = (x - high.astype(f32)).astype(bf16)
    y_ref[...] = jnp.dot(high, had_ref[...], preferred_element_type=f32) + jnp.dot(
        low, had_ref[...], preferred_element_type=f32
    )
    for b in range(BLOCKS):
        mixed = butterfly(
            [y_ref[16 * t : 16 * t + OWN, :] for t in range(8 * b, 8 * b + 8)]
        )
        for k, part in enumerate(mixed):
            t = 8 * b + k
            s, lane = divmod(t, SEG // LANES)
            lanes = slice(LANES * t, LANES * (t + 1))
            mean = part * (hadamard_norm / REPLICAS) * sign_ref[:, lanes]
            mean_ref[:, lanes] = mean
            first = 0.9 * first_ref[:, lanes] + 0.1 * mean
            second = 0.95 * second_ref[:, lanes] + 0.05 * mean * mean
            first_out[:, lanes] = first
            second_out[:, lanes] = second
            adjusted = first / 0.6513215599 / (jnp.sqrt(second / 0.4012630608) + 1e-08)
            sum_ref[OWN * s : OWN * (s + 1), LANES * lane : LANES * (lane + 1)] = (
                weight_ref[:, lanes].astype(f32) * (1.0 - 0.01 * 0.1) - 0.01 * adjusted
            )
    sent_ref[...] = sum_ref[...].astype(bf16)


def update(half, received, power, sign_row, had, first, second, weight, earlier):
    own = jax.ShapeDtypeStruct((OWN, COLS), f32)
    sent = jax.ShapeDtypeStruct((SEGS * OWN, SEG), bf16)

    def part(rows):
        return pl.BlockSpec((rows, HALF), lambda _: (0, half))

    kept = [pl.BlockSpec(memory_space=pl.ANY)] * len(earlier)
    return pl.pallas_call(
        functools.partial(update_kernel, half, len(received)),
        out_shape=(own, own, own, sent),
        grid=(1,),
        in_specs=[
            whole(power.shape),
            part(1),
            whole(had.shape),
            part(OWN),
            part(OWN),
            part(OWN),
        ]
        + [whole(array.shape) for array in received]
        + kept,
        out_specs=(part(OWN), part(OWN), part(OWN), whole(sent.shape)),
        scratch_shapes=[
            pltpu.VMEM((SEGS * OWN, SEG), f32),
            pltpu.VMEM((16 * HALF // LANES, LANES), f32),
            pltpu.VMEM((16 * HALF // LANES, LANES), f32),
        ],
        input_output_aliases={6 + len(received) + k: k for k in range(len(earlier))},
        compiler_params=params(),
        name=f"update_{half}",
    )(power, sign_row, had, first, second, weight, *received, *earlier)


def place_kernel(by_line, chunks_ref, *refs):
    out_ref, rows_ref = refs[-2:]
    for d in range(REPLICAS):
        source = d % LINE * 2 + d // LINE if by_line else d
        chunk = chunks_ref[source].astype(f32)
        for s in range(SEGS):
            rows_ref[OWN * d : OWN * (d + 1), SEG * s : SEG * (s + 1)] = chunk[
                OWN * s : OWN * (s + 1), :
            ]
    out_ref[...] = rows_ref[...].astype(bf16)


def place(half, by_line, chunks, earlier, flops):
    return pl.pallas_call(
        functools.partial(place_kernel, by_line),
        out_shape=jax.ShapeDtypeStruct((ROWS, COLS), bf16),
        grid=(1,),
        in_specs=[whole(chunks.shape)]
        + [pl.BlockSpec(memory_space=pl.ANY)] * len(earlier),
        out_specs=pl.BlockSpec((ROWS, HALF), lambda _: (0, half)),
        scratch_shapes=[pltpu.VMEM((ROWS, HALF), f32)],
        input_output_aliases={1 + k: k for k in range(len(earlier))},
        compiler_params=params(12),
        cost_estimate=pl.CostEstimate(
            flops=flops, bytes_accessed=3 << 20, transcendentals=0
        ),
        name=f"place_{half}",
    )(chunks, *earlier)


def rotate_weight_kernel(w_ref, sign_ref, had_ref, out_ref):
    turned = w_ref[...].astype(f32) * sign_ref[...]
    parts = [
        jnp.dot(
            turned[:, LANES * k : LANES * (k + 1)].astype(bf16),
            had_ref[...],
            preferred_element_type=f32,
        )
        for k in range(8)
    ]
    for k, part in enumerate(butterfly(parts)):
        out_ref[:, LANES * k : LANES * (k + 1)] = (part * hadamard_norm).astype(bf16)


def rotate_weight(weight, sign_row, had):
    return pl.pallas_call(
        rotate_weight_kernel,
        out_shape=jax.ShapeDtypeStruct((ROWS, COLS), bf16),
        grid=(COLS // 1024,),
        in_specs=[
            pl.BlockSpec((ROWS, 1024), lambda b: (0, b)),
            pl.BlockSpec((1, 1024), lambda b: (0, b)),
            whole((LANES, LANES)),
        ],
        out_specs=pl.BlockSpec((ROWS, 1024), lambda b: (0, b)),
        compiler_params=params(),
        cost_estimate=pl.CostEstimate(
            flops=2 * ROWS * COLS * 1024, bytes_accessed=5 << 20, transcendentals=0
        ),
        name="rotate_weight",
    )(weight, sign_row, had)


def pre_grad_kernel(own_ref, other_ref, w_ref, slope_ref, collect_ref, out_ref, acc_ref):
    rows = own_ref.shape[0]
    place_in_pair = lax.broadcasted_iota(jnp.int32, (rows, 1), 0) & (2 * SEGS - 1)
    for index, rows_ref in enumerate((own_ref, other_ref)):
        total = None
        for half in range(2):
            left = rows_ref[:, SEG * half : SEG * (half + 1)]
            chosen = jnp.zeros((rows, ROWS), f32)
            for s in range(SEGS):
                column = half * HALF + SEG * s
                part = lax.dot_general(
                    left,
                    w_ref[:, column : column + SEG],
                    (((1,), (1,)), ((), ())),
                    preferred_element_type=f32,
                )
                chosen = jnp.where(place_in_pair >> 1 == s, part, chosen)
            total = chosen if total is None else total + chosen
        acc_ref[rows * index : rows * (index + 1), :] = total
    hidden_grad = jnp.dot(
        collect_ref[...].astype(f32),
        acc_ref[...],
        precision=lax.Precision.HIGHEST,
        preferred_element_type=f32,
    )
    out_ref[...] = (hidden_grad * slope_ref[...]).astype(bf16)


def pre_grad_product(own, other, weight, slope, collect):
    return pl.pallas_call(
        pre_grad_kernel,
        out_shape=jax.ShapeDtypeStruct((TOK, ROWS), bf16),
        scratch_shapes=[pltpu.VMEM((2 * own.shape[0], ROWS), f32)],
        compiler_params=params(16),
        cost_estimate=pl.CostEstimate(
            flops=8 * 512 * 1536 * ROWS, bytes_accessed=6 << 20, transcendentals=0
        ),
        name="pre_grad",
    )(own, other, weight, slope, collect)


def swap(values, axis):
    return lax.ppermute(values, axis, [(0, 1), (1, 0)])


def to_all(values, axes, count):
    return lax.all_to_all(
        jnp.broadcast_to(values[None], (count,) + values.shape), axes, 0, 0, tiled=True
    )


def body(upstream, pre_act, w_down, first_moment, second_moment, signs, exponents):
    spread, widen, same, choice, gather = tables()
    had = jnp.asarray(hadamard(LANES), bf16)
    core = lax.axis_index("core")
    plane = lax.axis_index("z_lo")

    rotated = rotate_upstream(upstream, signs.reshape(1, COLS), had)
    own = to_all(rotated, ("z_hi", "y"), PEERS).reshape(-1, 2 * SEG)

    pairs = pre_act.reshape(PEERS, 2, 2, ROWS)
    mine = jnp.where(core == 0, pairs[:, 0], pairs[:, 1]).reshape(TOK // 2, ROWS)
    yours = jnp.where(core == 0, pairs[:, 1], pairs[:, 0]).reshape(TOK // 2, ROWS)
    preact = jnp.concatenate([mine, yours], axis=0).astype(f32)
    normal_cdf = 0.5 * (1.0 + lax.erf(preact * root_half))
    hidden = (preact * normal_cdf).astype(bf16)
    slope = normal_cdf + preact * jnp.exp(-0.5 * preact * preact) * density_norm
    scale_power = exponents.astype(f32)
    shrink = jnp.tile(jnp.exp2(-scale_power).astype(bf16), (1, COLS // 1024))
    left, scale = expand_hidden(hidden, shrink, spread, widen, same, choice, gather)

    own, left, scale = lax.optimization_barrier((own, left, scale))
    other = swap(own, "core")
    encoded0 = encode(0, True, left, own, other, scale)
    encoded0, left = lax.optimization_barrier((encoded0, left))
    encoded1 = encode(1, False, left, own, other, scale)

    sign_row = (1 - 2 * signs).astype(f32).reshape(1, COLS)
    offset = lax.axis_index(("z_lo", "x")) * OWN
    own_power = jnp.exp2(lax.dynamic_slice_in_dim(scale_power, offset, OWN, 0))
    own_weight = lax.dynamic_slice_in_dim(w_down, offset, OWN, 0)

    along = lax.psum_scatter(encoded0, "x", scatter_dimension=0, tiled=True)
    terms = lax.all_to_all(
        encoded1.reshape(REPLICAS, SEGS * OWN, SEG), ("z_lo", "x"), 0, 0, tiled=True
    )
    states = (sign_row, had, first_moment, second_moment, own_weight)
    *earlier, sent1 = update(1, [terms], own_power, *states, ())
    across = swap(sent1, "z_lo")
    both = jnp.where(
        plane == 0,
        jnp.concatenate([sent1, across], axis=0),
        jnp.concatenate([across, sent1], axis=0),
    )
    turned_weight = rotate_weight(w_down, sign_row, had)
    mixed = pre_grad_product(own, other, turned_weight, slope, widen)
    halves = mixed.reshape(2, PEERS, 2, ROWS)
    zero = jnp.where(core == 0, halves[0], halves[1])
    one = jnp.where(core == 0, halves[1], halves[0])
    pre_grad = jnp.stack([zero, one], axis=1).reshape(TOK, ROWS)

    both, along, pre_grad = lax.optimization_barrier((both, along, pre_grad))
    line = lax.all_gather(both, "x", axis=0, tiled=True)
    upper, lower = along[: SEGS * OWN], along[SEGS * OWN :]
    kept = jnp.where(plane == 0, upper, lower)
    taken = swap(jnp.where(plane == 0, lower, upper), "z_lo")
    *updated, sent0 = update(0, [kept[None], taken[None]], own_power, *states, earlier)
    direct = to_all(sent0, ("z_lo", "x"), REPLICAS)

    placed = place(1, True, line.reshape(REPLICAS, SEGS * OWN, SEG), (), 10**11)
    weight_new = place(0, False, direct, (placed,), 10**9)
    return (pre_grad, *updated, weight_new)


def solution(mesh):
    fine = Mesh(
        mesh.devices.reshape(2, 8, 4, 8, 2), ("z_lo", "x", "z_hi", "y", "core")
    )
    dp = ("z_lo", "x")
    mp = ("z_hi", "y", "core")
    placed = (
        P(dp + mp, None),
        P(dp, mp),
        P(mp, None),
        P(mp + dp, None),
        P(mp + dp, None),
        P(),
        P(mp, None),
    )
    return jax.shard_map(
        body,
        mesh=fine,
        in_specs=placed,
        out_specs=(
            P(dp, mp),
            P(mp + dp, None),
            P(mp + dp, None),
            P(mp + dp, None),
            P(mp, None),
        ),
        check_vma=False,
    )
```

```python
import jax
import jax.numpy as jnp
import numpy as np
from jax import lax
from jax.experimental import pallas as pl
from jax.experimental.pallas import tpu as pltpu
from jax.sharding import Mesh
from jax.sharding import PartitionSpec as P

hadamard_norm = 0.03125
clip_limit = 448.0
root_half = 0.7071067811865476
density_norm = 0.3989422804014327

REPLICAS = 16
ROWS = 192
OWN = 12
COLS = 6144
SEGS = 4
SEG = 1536
BLOCKS = 6
KEPT = 47
SPARE = 128
TILE = 256
TOK = 128
PEERS = 32
LANES = 128
bf16 = jnp.bfloat16
f32 = jnp.float32


def hadamard(order):
    indices = np.arange(order)
    common = indices[:, None] & indices[None, :]
    parity = np.zeros((order, order), np.int64)
    for position in range(order.bit_length() - 1):
        parity += common >> position & 1
    return (1 - 2 * (parity % 2)).astype(np.float32)


def tables():
    owner = np.concatenate([np.repeat(np.arange(REPLICAS), KEPT), np.arange(REPLICAS)])
    part = np.concatenate([np.tile(np.arange(KEPT), REPLICAS), np.full(REPLICAS, KEPT)])
    segment, own = part // OWN, part % OWN
    spread = (owner * OWN + own)[:, None] == np.arange(ROWS)[None, :]
    col = np.arange(2 * PEERS * SEGS * 2)
    patch = col // (SEGS * 2) * 2 + col % 2
    col_segment = col % (SEGS * 2) // 2
    widen = np.arange(TOK)[:, None] == patch[None, :]
    same = segment[:, None] == col_segment[None, :]
    tiles = SEG // TILE
    block = (3 * segment[:, None] + np.arange(tiles)[None, :] // 2) // 2
    choice = block[:, :, None] == np.arange(BLOCKS)
    gather = np.repeat(np.eye(tiles), BLOCKS, axis=0)
    shown = (spread, widen, same, choice.reshape(owner.size, -1), gather)
    return [jnp.asarray(table, bf16) for table in shown]


def butterfly(parts):
    parts = list(parts)
    span = 1
    while span < len(parts):
        for start in range(0, len(parts), 2 * span):
            for k in range(start, start + span):
                first, second = parts[k], parts[k + span]
                parts[k], parts[k + span] = first + second, first - second
        span *= 2
    return parts


def whole(shape):
    return pl.BlockSpec(shape, lambda *_: (0,) * len(shape))


def params(mebibytes=8):
    return pltpu.CompilerParams(vmem_limit_bytes=mebibytes << 20)


def rotate_upstream_kernel(u_ref, sign_ref, had_ref, out_ref, x_ref, z_ref):
    turned = u_ref[...].astype(f32) * (1 - 2 * sign_ref[...]).astype(f32)
    for t in range(COLS // LANES):
        x_ref[2 * t : 2 * t + 2, :] = turned[:, LANES * t : LANES * (t + 1)]
    x_ref[...] = jnp.dot(
        x_ref[...].astype(bf16), had_ref[...], preferred_element_type=f32
    )
    for b in range(BLOCKS):
        mixed = butterfly([x_ref[2 * t : 2 * t + 2, :] for t in range(8 * b, 8 * b + 8)])
        for k, part in enumerate(mixed):
            s, lane = divmod(8 * b + k, SEG // LANES)
            z_ref[2 * s : 2 * s + 2, LANES * lane : LANES * (lane + 1)] = (
                part * hadamard_norm
            )
    out_ref[...] = z_ref[...].astype(bf16)


def rotate_upstream(upstream, signs, had):
    return pl.pallas_call(
        rotate_upstream_kernel,
        out_shape=jax.ShapeDtypeStruct((2 * SEGS, SEG), bf16),
        scratch_shapes=[
            pltpu.VMEM((2 * COLS // LANES, LANES), f32),
            pltpu.VMEM((2 * SEGS, SEG), f32),
        ],
        compiler_params=params(),
        name="rotate_upstream",
    )(upstream, signs, had)


def expand_hidden_kernel(
    hidden_ref, shrink_ref, spread_ref, widen_ref, same_ref, choice_ref, gather_ref,
    out_ref, scale_ref,
):
    rows = lax.dot_general(
        spread_ref[...],
        hidden_ref[...],
        (((1,), (1,)), ((), ())),
        preferred_element_type=f32,
    ).astype(bf16)
    wide = jnp.dot(rows, widen_ref[...], preferred_element_type=f32)
    out_ref[...] = (wide * same_ref[...].astype(f32)).astype(bf16)
    every = jnp.dot(spread_ref[...], shrink_ref[...], preferred_element_type=f32)
    chosen = (every * choice_ref[...].astype(f32)).astype(bf16)
    scale_ref[...] = jnp.dot(chosen, gather_ref[...], preferred_element_type=f32)


def expand_hidden(hidden, shrink, spread, widen, same, choice, gather):
    return pl.pallas_call(
        expand_hidden_kernel,
        out_shape=(
            jax.ShapeDtypeStruct(same.shape, bf16),
            jax.ShapeDtypeStruct((same.shape[0], gather.shape[1]), f32),
        ),
        compiler_params=params(),
        cost_estimate=pl.CostEstimate(
            flops=2 * 768 * 128 * 700, bytes_accessed=4 << 20, transcendentals=0
        ),
        name="expand_hidden",
    )(hidden, shrink, spread, widen, same, choice, gather)


def encode_kernel(left_ref, own_ref, other_ref, scale_ref, out_ref, spare_ref):
    depth = own_ref.shape[0]
    full = REPLICAS * KEPT
    scales = scale_ref[...]
    spare_ref[...] = jnp.zeros_like(spare_ref)
    for n in range(SEG // TILE):
        lanes = slice(TILE * n, TILE * (n + 1))
        total = jnp.dot(
            left_ref[:, :depth], own_ref[:, lanes], preferred_element_type=f32
        )
        total += jnp.dot(
            left_ref[:, depth:], other_ref[:, lanes], preferred_element_type=f32
        )
        total = jnp.clip(total * scales[:, n : n + 1], -clip_limit, clip_limit)
        out_ref[:, lanes] = total[:full].astype(bf16)
        for k in range(TILE // SPARE):
            rows = pl.ds(TILE // SPARE * n + k, REPLICAS, stride=KEPT)
            spare_ref[rows, :] = total[full:, SPARE * k : SPARE * (k + 1)]
    out_ref[:, SEG:] = spare_ref[...].astype(bf16)


def encode(left, own, other, scale):
    full = REPLICAS * KEPT
    depth = own.shape[0]
    shape = (full, SEG + SPARE)
    return pl.pallas_call(
        encode_kernel,
        out_shape=pltpu.HBM(shape, bf16),
        grid=(1,),
        in_specs=[whole(array.shape) for array in (left, own, other, scale)],
        out_specs=whole(shape),
        scratch_shapes=[pltpu.VMEM((full, SPARE), f32)],
        compiler_params=params(24),
        cost_estimate=pl.CostEstimate(
            flops=4 * full * depth * SEG, bytes_accessed=6 << 20, transcendentals=0
        ),
        name="encode",
    )(left, own, other, scale)


def update_kernel(
    received_ref, power_ref, sign_ref, had_ref, first_ref, second_ref, weight_ref,
    mean_ref, first_out, second_out, sent_ref, sum_ref, x_ref, y_ref,
):
    total = received_ref[...].astype(f32)
    sum_ref[:KEPT, :] = total[:, :SEG]
    for k in range(SEG // SPARE):
        sum_ref[KEPT : KEPT + 1, SPARE * k : SPARE * (k + 1)] = total[k : k + 1, SEG:]
    x_ref[...] = jnp.zeros_like(x_ref)
    for t in range(COLS // LANES):
        s, lane = divmod(t, SEG // LANES)
        x_ref[16 * t : 16 * t + OWN, :] = (
            sum_ref[OWN * s : OWN * (s + 1), LANES * lane : LANES * (lane + 1)]
            * power_ref[:, t // 8 : t // 8 + 1]
        )
    x = x_ref[...]
    high = x.astype(bf16)
    low = (x - high.astype(f32)).astype(bf16)
    y_ref[...] = jnp.dot(high, had_ref[...], preferred_element_type=f32) + jnp.dot(
        low, had_ref[...], preferred_element_type=f32
    )
    for b in range(BLOCKS):
        mixed = butterfly(
            [y_ref[16 * t : 16 * t + OWN, :] for t in range(8 * b, 8 * b + 8)]
        )
        for k, part in enumerate(mixed):
            t = 8 * b + k
            s, lane = divmod(t, SEG // LANES)
            lanes = slice(LANES * t, LANES * (t + 1))
            mean = part * (hadamard_norm / REPLICAS) * sign_ref[:, lanes]
            mean_ref[:, lanes] = mean
            first = 0.9 * first_ref[:, lanes] + 0.1 * mean
            second = 0.95 * second_ref[:, lanes] + 0.05 * mean * mean
            first_out[:, lanes] = first
            second_out[:, lanes] = second
            adjusted = first / 0.6513215599 / (jnp.sqrt(second / 0.4012630608) + 1e-08)
            sum_ref[OWN * s : OWN * (s + 1), LANES * lane : LANES * (lane + 1)] = (
                weight_ref[:, lanes].astype(f32) * (1.0 - 0.01 * 0.1) - 0.01 * adjusted
            )
    sent_ref[...] = sum_ref[...].astype(bf16)


def update(received, power, sign_row, had, first, second, weight):
    own = jax.ShapeDtypeStruct((OWN, COLS), f32)
    return pl.pallas_call(
        update_kernel,
        out_shape=(own, own, own, jax.ShapeDtypeStruct((SEGS * OWN, SEG), bf16)),
        scratch_shapes=[
            pltpu.VMEM((SEGS * OWN, SEG), f32),
            pltpu.VMEM((16 * COLS // LANES, LANES), f32),
            pltpu.VMEM((16 * COLS // LANES, LANES), f32),
        ],
        compiler_params=params(),
        name="update",
    )(received, power, sign_row, had, first, second, weight)


def place_kernel(gathered_ref, out_ref, rows_ref):
    for d in range(REPLICAS):
        chunk = gathered_ref[d].astype(f32)
        for s in range(SEGS):
            rows_ref[OWN * d : OWN * (d + 1), SEG * s : SEG * (s + 1)] = chunk[
                OWN * s : OWN * (s + 1), :
            ]
    out_ref[...] = rows_ref[...].astype(bf16)


def place(gathered):
    return pl.pallas_call(
        place_kernel,
        out_shape=jax.ShapeDtypeStruct((ROWS, COLS), bf16),
        scratch_shapes=[pltpu.VMEM((ROWS, COLS), f32)],
        compiler_params=params(20),
        name="place",
    )(gathered)


def rotate_weight_kernel(w_ref, sign_ref, had_ref, out_ref):
    turned = w_ref[...].astype(f32) * sign_ref[...]
    parts = [
        jnp.dot(
            turned[:, LANES * k : LANES * (k + 1)].astype(bf16),
            had_ref[...],
            preferred_element_type=f32,
        )
        for k in range(8)
    ]
    for k, part in enumerate(butterfly(parts)):
        out_ref[:, LANES * k : LANES * (k + 1)] = (part * hadamard_norm).astype(bf16)


def rotate_weight(weight, sign_row, had):
    return pl.pallas_call(
        rotate_weight_kernel,
        out_shape=jax.ShapeDtypeStruct((ROWS, COLS), bf16),
        grid=(BLOCKS,),
        in_specs=[
            pl.BlockSpec((ROWS, 1024), lambda b: (0, b)),
            pl.BlockSpec((1, 1024), lambda b: (0, b)),
            whole((LANES, LANES)),
        ],
        out_specs=pl.BlockSpec((ROWS, 1024), lambda b: (0, b)),
        compiler_params=params(),
        cost_estimate=pl.CostEstimate(
            flops=2 * ROWS * COLS * 1024, bytes_accessed=5 << 20, transcendentals=0
        ),
        name="rotate_weight",
    )(weight, sign_row, had)


def pre_grad_kernel(own_ref, other_ref, w_ref, slope_ref, collect_ref, out_ref, acc_ref):
    half = own_ref.shape[0]
    place_in_pair = lax.broadcasted_iota(jnp.int32, (half, 1), 0) & (2 * SEGS - 1)
    for index, rows_ref in enumerate((own_ref, other_ref)):
        rows = rows_ref[...]
        total = jnp.zeros((half, ROWS), f32)
        for s in range(SEGS):
            part = lax.dot_general(
                rows,
                w_ref[:, SEG * s : SEG * (s + 1)],
                (((1,), (1,)), ((), ())),
                preferred_element_type=f32,
            )
            total = jnp.where(place_in_pair >> 1 == s, part, total)
        acc_ref[half * index : half * (index + 1), :] = total
    hidden_grad = jnp.dot(
        collect_ref[...].astype(f32),
        acc_ref[...],
        precision=lax.Precision.HIGHEST,
        preferred_element_type=f32,
    )
    out_ref[...] = (hidden_grad * slope_ref[...]).astype(bf16)


def pre_grad_product(own, other, weight, slope, collect):
    return pl.pallas_call(
        pre_grad_kernel,
        out_shape=jax.ShapeDtypeStruct((TOK, ROWS), bf16),
        scratch_shapes=[pltpu.VMEM((2 * own.shape[0], ROWS), f32)],
        compiler_params=params(16),
        cost_estimate=pl.CostEstimate(
            flops=8 * 512 * SEG * ROWS, bytes_accessed=6 << 20, transcendentals=0
        ),
        name="pre_grad",
    )(own, other, weight, slope, collect)


def to_all(values, axes, count):
    return lax.all_to_all(
        jnp.broadcast_to(values[None], (count,) + values.shape), axes, 0, 0, tiled=True
    )


def body(upstream, pre_act, w_down, first_moment, second_moment, signs, exponents):
    spread, widen, same, choice, gather = tables()
    had = jnp.asarray(hadamard(LANES), bf16)
    core = lax.axis_index("core")

    rotated = rotate_upstream(upstream, signs.reshape(1, COLS), had)
    own = to_all(rotated, ("z_hi", "y"), PEERS).reshape(-1, SEG)

    pairs = pre_act.reshape(PEERS, 2, 2, ROWS)
    mine = jnp.where(core == 0, pairs[:, 0], pairs[:, 1]).reshape(TOK // 2, ROWS)
    yours = jnp.where(core == 0, pairs[:, 1], pairs[:, 0]).reshape(TOK // 2, ROWS)
    preact = jnp.concatenate([mine, yours], axis=0).astype(f32)
    normal_cdf = 0.5 * (1.0 + lax.erf(preact * root_half))
    hidden = (preact * normal_cdf).astype(bf16)
    slope = normal_cdf + preact * jnp.exp(-0.5 * preact * preact) * density_norm
    scale_power = exponents.astype(f32)
    shrink = jnp.tile(jnp.exp2(-scale_power).astype(bf16), (1, SEG // TILE))
    left, scale = expand_hidden(hidden, shrink, spread, widen, same, choice, gather)
    sign_row = (1 - 2 * signs).astype(f32).reshape(1, COLS)
    turned_weight = rotate_weight(w_down, sign_row, had)
    offset = lax.axis_index(("z_lo", "x")) * OWN
    own_power = jnp.exp2(lax.dynamic_slice_in_dim(scale_power, offset, OWN, 0))
    own_weight = lax.dynamic_slice_in_dim(w_down, offset, OWN, 0)

    own, left, scale, turned_weight, own_power, own_weight = lax.optimization_barrier(
        (own, left, scale, turned_weight, own_power, own_weight)
    )
    other = lax.ppermute(own, "core", [(0, 1), (1, 0)])
    encoded = encode(left, own, other, scale)
    summed = lax.psum_scatter(encoded, ("z_lo", "x"), scatter_dimension=0, tiled=True)
    grad_mean, first_new, second_new, sent = update(
        summed, own_power, sign_row, had, first_moment, second_moment, own_weight
    )
    weight_new = place(to_all(sent, ("z_lo", "x"), REPLICAS))

    mixed = pre_grad_product(own, other, turned_weight, slope, widen)
    halves = mixed.reshape(2, PEERS, 2, ROWS)
    zero = jnp.where(core == 0, halves[0], halves[1])
    one = jnp.where(core == 0, halves[1], halves[0])
    pre_grad = jnp.stack([zero, one], axis=1).reshape(TOK, ROWS)
    return (pre_grad, grad_mean, first_new, second_new, weight_new)


def solution(mesh):
    fine = Mesh(
        mesh.devices.reshape(2, 8, 4, 8, 2), ("z_lo", "x", "z_hi", "y", "core")
    )
    dp = ("z_lo", "x")
    mp = ("z_hi", "y", "core")
    placed = (
        P(dp + mp, None),
        P(dp, mp),
        P(mp, None),
        P(mp + dp, None),
        P(mp + dp, None),
        P(),
        P(mp, None),
    )
    return jax.shard_map(
        body,
        mesh=fine,
        in_specs=placed,
        out_specs=(
            P(dp, mp),
            P(mp + dp, None),
            P(mp + dp, None),
            P(mp + dp, None),
            P(mp, None),
        ),
        check_vma=False,
    )
```

```python
import jax
import jax.numpy as jnp
import numpy as np
from jax import lax
from jax.experimental import pallas as pl
from jax.experimental.pallas import tpu as pltpu
from jax.sharding import Mesh
from jax.sharding import PartitionSpec as P

hadamard_norm = 0.03125
clip_limit = 448.0
root_half = 0.7071067811865476
density_norm = 0.3989422804014327

REPLICAS = 16
ROWS = 192
OWN = 12
COLS = 6144
SEGS = 4
SEG = 1536
BLOCKS = 6
LINE = 8
KEPT = 95
SPARE = 128
TILE = 256
TOK = 128
PEERS = 32
LANES = 128
bf16 = jnp.bfloat16
f32 = jnp.float32


def hadamard(order):
    indices = np.arange(order)
    common = indices[:, None] & indices[None, :]
    parity = np.zeros((order, order), np.int64)
    for position in range(order.bit_length() - 1):
        parity += common >> position & 1
    return (1 - 2 * (parity % 2)).astype(np.float32)


def tables():
    line = np.concatenate([np.repeat(np.arange(LINE), KEPT), np.arange(LINE)])
    part = np.concatenate([np.tile(np.arange(KEPT), LINE), np.full(LINE, KEPT)])
    owner = part // (SEGS * OWN) * LINE + line
    segment, own = part // OWN % SEGS, part % OWN
    spread = (owner * OWN + own)[:, None] == np.arange(ROWS)[None, :]
    col = np.arange(2 * PEERS * SEGS * 2)
    patch = col // (SEGS * 2) * 2 + col % 2
    col_segment = col % (SEGS * 2) // 2
    widen = np.arange(TOK)[:, None] == patch[None, :]
    same = segment[:, None] == col_segment[None, :]
    tiles = SEG // TILE
    block = (3 * segment[:, None] + np.arange(tiles)[None, :] // 2) // 2
    choice = block[:, :, None] == np.arange(BLOCKS)
    gather = np.repeat(np.eye(tiles), BLOCKS, axis=0)
    shown = (spread, widen, same, choice.reshape(owner.size, -1), gather)
    return [jnp.asarray(table, bf16) for table in shown]


def butterfly(parts):
    parts = list(parts)
    span = 1
    while span < len(parts):
        for start in range(0, len(parts), 2 * span):
            for k in range(start, start + span):
                first, second = parts[k], parts[k + span]
                parts[k], parts[k + span] = first + second, first - second
        span *= 2
    return parts


def whole(shape):
    return pl.BlockSpec(shape, lambda *_: (0,) * len(shape))


def params(mebibytes=8):
    return pltpu.CompilerParams(vmem_limit_bytes=mebibytes << 20)


def rotate_upstream_kernel(
    u_hbm, sign_hbm, had_hbm, out_ref, u_ref, sign_ref, had_ref, x_ref, z_ref, sems
):
    pairs = ((u_hbm, u_ref), (sign_hbm, sign_ref), (had_hbm, had_ref))
    copies = [
        pltpu.make_async_copy(source, target, sems.at[k])
        for k, (source, target) in enumerate(pairs)
    ]
    for copy in copies:
        copy.start()
    for copy in copies:
        copy.wait()
    turned = u_ref[...].astype(f32) * (1 - 2 * sign_ref[...]).astype(f32)
    for t in range(COLS // LANES):
        x_ref[2 * t : 2 * t + 2, :] = turned[:, LANES * t : LANES * (t + 1)]
    x_ref[...] = jnp.dot(
        x_ref[...].astype(bf16), had_ref[...], preferred_element_type=f32
    )
    for b in range(BLOCKS):
        mixed = butterfly([x_ref[2 * t : 2 * t + 2, :] for t in range(8 * b, 8 * b + 8)])
        for k, part in enumerate(mixed):
            s, lane = divmod(8 * b + k, SEG // LANES)
            z_ref[2 * s : 2 * s + 2, LANES * lane : LANES * (lane + 1)] = (
                part * hadamard_norm
            )
    out_ref[...] = z_ref[...].astype(bf16)


def rotate_upstream(upstream, signs, had):
    arrays = [
        pltpu.with_memory_space_constraint(array, pltpu.HBM)
        for array in (upstream, signs, had)
    ]
    return pl.pallas_call(
        rotate_upstream_kernel,
        out_shape=jax.ShapeDtypeStruct((2 * SEGS, SEG), bf16),
        in_specs=[pl.BlockSpec(memory_space=pltpu.HBM)] * 3,
        scratch_shapes=[pltpu.VMEM(array.shape, array.dtype) for array in arrays]
        + [
            pltpu.VMEM((2 * COLS // LANES, LANES), f32),
            pltpu.VMEM((2 * SEGS, SEG), f32),
            pltpu.SemaphoreType.DMA((3,)),
        ],
        compiler_params=params(),
        name="rotate_upstream",
    )(*arrays)


def expand_hidden_kernel(
    hidden_ref, shrink_ref, spread_ref, widen_ref, same_ref, choice_ref, gather_ref,
    out_ref, scale_ref,
):
    rows = lax.dot_general(
        spread_ref[...],
        hidden_ref[...],
        (((1,), (1,)), ((), ())),
        preferred_element_type=f32,
    ).astype(bf16)
    wide = jnp.dot(rows, widen_ref[...], preferred_element_type=f32)
    out_ref[...] = (wide * same_ref[...].astype(f32)).astype(bf16)
    every = jnp.dot(spread_ref[...], shrink_ref[...], preferred_element_type=f32)
    chosen = (every * choice_ref[...].astype(f32)).astype(bf16)
    scale_ref[...] = jnp.dot(chosen, gather_ref[...], preferred_element_type=f32)


def expand_hidden(hidden, shrink, spread, widen, same, choice, gather):
    return pl.pallas_call(
        expand_hidden_kernel,
        out_shape=(
            jax.ShapeDtypeStruct(same.shape, bf16),
            jax.ShapeDtypeStruct((same.shape[0], gather.shape[1]), f32),
        ),
        compiler_params=params(),
        cost_estimate=pl.CostEstimate(
            flops=2 * 768 * 128 * 700, bytes_accessed=4 << 20, transcendentals=0
        ),
        name="expand_hidden",
    )(hidden, shrink, spread, widen, same, choice, gather)


def encode_kernel(left_ref, own_ref, other_ref, scale_ref, out_ref, spare_ref):
    depth = own_ref.shape[0]
    full = LINE * KEPT
    scales = scale_ref[...]
    spare_ref[...] = jnp.zeros_like(spare_ref)
    for n in range(SEG // TILE):
        lanes = slice(TILE * n, TILE * (n + 1))
        total = jnp.dot(
            left_ref[:, :depth], own_ref[:, lanes], preferred_element_type=f32
        )
        total += jnp.dot(
            left_ref[:, depth:], other_ref[:, lanes], preferred_element_type=f32
        )
        total = jnp.clip(total * scales[:, n : n + 1], -clip_limit, clip_limit)
        out_ref[:, lanes] = total[:full].astype(bf16)
        for k in range(TILE // SPARE):
            rows = pl.ds(TILE // SPARE * n + k, LINE, stride=KEPT)
            spare_ref[rows, :] = total[full:, SPARE * k : SPARE * (k + 1)]
    out_ref[:, SEG:] = spare_ref[...].astype(bf16)


def encode(left, own, other, scale):
    full = LINE * KEPT
    depth = own.shape[0]
    shape = (full, SEG + SPARE)
    return pl.pallas_call(
        encode_kernel,
        out_shape=pltpu.HBM(shape, bf16),
        grid=(1,),
        in_specs=[whole(array.shape) for array in (left, own, other, scale)],
        out_specs=whole(shape),
        scratch_shapes=[pltpu.VMEM((full, SPARE), f32)],
        compiler_params=params(24),
        cost_estimate=pl.CostEstimate(
            flops=4 * full * depth * SEG, bytes_accessed=6 << 20, transcendentals=0
        ),
        name="encode",
    )(left, own, other, scale)


def split_kernel(plane_ref, summed_ref, kept_ref, given_ref, rows_ref):
    total = summed_ref[...].astype(f32)
    rows_ref[:KEPT, :] = total[:, :SEG]
    for k in range(SEG // SPARE):
        rows_ref[KEPT : KEPT + 1, SPARE * k : SPARE * (k + 1)] = total[k : k + 1, SEG:]
    upper = rows_ref[: SEGS * OWN, :].astype(bf16)
    lower = rows_ref[SEGS * OWN :, :].astype(bf16)
    first = plane_ref[0] == 0
    kept_ref[...] = jnp.where(first, upper, lower)
    given_ref[...] = jnp.where(first, lower, upper)


def split(plane, summed):
    part = jax.ShapeDtypeStruct((SEGS * OWN, SEG), bf16)
    return pl.pallas_call(
        split_kernel,
        out_shape=(part, part),
        in_specs=[
            pl.BlockSpec(memory_space=pltpu.SMEM),
            pl.BlockSpec(memory_space=pltpu.VMEM),
        ],
        scratch_shapes=[pltpu.VMEM((2 * SEGS * OWN, SEG), f32)],
        compiler_params=params(),
        name="split",
    )(plane, summed)


def update_kernel(
    kept_ref, taken_ref, power_ref, sign_ref, had_ref, first_ref, second_ref, weight_ref,
    mean_ref, first_out, second_out, sent_ref, sum_ref, x_ref, y_ref,
):
    sum_ref[...] = kept_ref[...].astype(f32) + taken_ref[...].astype(f32)
    x_ref[...] = jnp.zeros_like(x_ref)
    for t in range(COLS // LANES):
        s, lane = divmod(t, SEG // LANES)
        x_ref[16 * t : 16 * t + OWN, :] = (
            sum_ref[OWN * s : OWN * (s + 1), LANES * lane : LANES * (lane + 1)]
            * power_ref[:, t // 8 : t // 8 + 1]
        )
    x = x_ref[...]
    high = x.astype(bf16)
    low = (x - high.astype(f32)).astype(bf16)
    y_ref[...] = jnp.dot(high, had_ref[...], preferred_element_type=f32) + jnp.dot(
        low, had_ref[...], preferred_element_type=f32
    )
    for b in range(BLOCKS):
        mixed = butterfly(
            [y_ref[16 * t : 16 * t + OWN, :] for t in range(8 * b, 8 * b + 8)]
        )
        for k, part in enumerate(mixed):
            t = 8 * b + k
            s, lane = divmod(t, SEG // LANES)
            lanes = slice(LANES * t, LANES * (t + 1))
            mean = part * (hadamard_norm / REPLICAS) * sign_ref[:, lanes]
            mean_ref[:, lanes] = mean
            first = 0.9 * first_ref[:, lanes] + 0.1 * mean
            second = 0.95 * second_ref[:, lanes] + 0.05 * mean * mean
            first_out[:, lanes] = first
            second_out[:, lanes] = second
            adjusted = first / 0.6513215599 / (jnp.sqrt(second / 0.4012630608) + 1e-08)
            sum_ref[OWN * s : OWN * (s + 1), LANES * lane : LANES * (lane + 1)] = (
                weight_ref[:, lanes].astype(f32) * (1.0 - 0.01 * 0.1) - 0.01 * adjusted
            )
    sent_ref[...] = sum_ref[...].astype(bf16)


def update(kept, taken, power, sign_row, had, first, second, weight):
    own = jax.ShapeDtypeStruct((OWN, COLS), f32)
    return pl.pallas_call(
        update_kernel,
        out_shape=(own, own, own, jax.ShapeDtypeStruct((SEGS * OWN, SEG), bf16)),
        scratch_shapes=[
            pltpu.VMEM((SEGS * OWN, SEG), f32),
            pltpu.VMEM((16 * COLS // LANES, LANES), f32),
            pltpu.VMEM((16 * COLS // LANES, LANES), f32),
        ],
        compiler_params=params(),
        name="update",
    )(kept, taken, power, sign_row, had, first, second, weight)


def place_kernel(gathered_ref, out_ref, rows_ref):
    for d in range(REPLICAS):
        chunk = gathered_ref[d].astype(f32)
        for s in range(SEGS):
            rows_ref[OWN * d : OWN * (d + 1), SEG * s : SEG * (s + 1)] = chunk[
                OWN * s : OWN * (s + 1), :
            ]
    out_ref[...] = rows_ref[...].astype(bf16)


def place(gathered):
    return pl.pallas_call(
        place_kernel,
        out_shape=jax.ShapeDtypeStruct((ROWS, COLS), bf16),
        scratch_shapes=[pltpu.VMEM((ROWS, COLS), f32)],
        compiler_params=params(20),
        name="place",
    )(gathered)


def rotate_weight_kernel(w_ref, sign_ref, had_ref, out_ref):
    turned = w_ref[...].astype(f32) * sign_ref[...]
    parts = [
        jnp.dot(
            turned[:, LANES * k : LANES * (k + 1)].astype(bf16),
            had_ref[...],
            preferred_element_type=f32,
        )
        for k in range(8)
    ]
    for k, part in enumerate(butterfly(parts)):
        out_ref[:, LANES * k : LANES * (k + 1)] = (part * hadamard_norm).astype(bf16)


def rotate_weight(weight, sign_row, had):
    return pl.pallas_call(
        rotate_weight_kernel,
        out_shape=jax.ShapeDtypeStruct((ROWS, COLS), bf16),
        grid=(BLOCKS,),
        in_specs=[
            pl.BlockSpec((ROWS, 1024), lambda b: (0, b)),
            pl.BlockSpec((1, 1024), lambda b: (0, b)),
            whole((LANES, LANES)),
        ],
        out_specs=pl.BlockSpec((ROWS, 1024), lambda b: (0, b)),
        compiler_params=params(),
        cost_estimate=pl.CostEstimate(
            flops=2 * ROWS * COLS * 1024, bytes_accessed=5 << 20, transcendentals=0
        ),
        name="rotate_weight",
    )(weight, sign_row, had)


def pre_grad_kernel(own_ref, other_ref, w_ref, slope_ref, collect_ref, out_ref, acc_ref):
    half = own_ref.shape[0]
    place_in_pair = lax.broadcasted_iota(jnp.int32, (half, 1), 0) & (2 * SEGS - 1)
    for index, rows_ref in enumerate((own_ref, other_ref)):
        rows = rows_ref[...]
        total = jnp.zeros((half, ROWS), f32)
        for s in range(SEGS):
            part = lax.dot_general(
                rows,
                w_ref[:, SEG * s : SEG * (s + 1)],
                (((1,), (1,)), ((), ())),
                preferred_element_type=f32,
            )
            total = jnp.where(place_in_pair >> 1 == s, part, total)
        acc_ref[half * index : half * (index + 1), :] = total
    hidden_grad = jnp.dot(
        collect_ref[...].astype(f32),
        acc_ref[...],
        precision=lax.Precision.HIGHEST,
        preferred_element_type=f32,
    )
    out_ref[...] = (hidden_grad * slope_ref[...]).astype(bf16)


def pre_grad_product(own, other, weight, slope, collect):
    return pl.pallas_call(
        pre_grad_kernel,
        out_shape=jax.ShapeDtypeStruct((TOK, ROWS), bf16),
        scratch_shapes=[pltpu.VMEM((2 * own.shape[0], ROWS), f32)],
        compiler_params=params(16),
        cost_estimate=pl.CostEstimate(
            flops=8 * 512 * SEG * ROWS, bytes_accessed=6 << 20, transcendentals=0
        ),
        name="pre_grad",
    )(own, other, weight, slope, collect)


def to_all(values, axes, count):
    return lax.all_to_all(
        jnp.broadcast_to(values[None], (count,) + values.shape), axes, 0, 0, tiled=True
    )


def body(upstream, pre_act, w_down, first_moment, second_moment, signs, exponents):
    spread, widen, same, choice, gather = tables()
    had = jnp.asarray(hadamard(LANES), bf16)
    core = lax.axis_index("core")

    rotated = rotate_upstream(upstream, signs.reshape(1, COLS), had)
    own = to_all(rotated, ("z_hi", "y"), PEERS).reshape(-1, SEG)

    pairs = pre_act.reshape(PEERS, 2, 2, ROWS)
    mine = jnp.where(core == 0, pairs[:, 0], pairs[:, 1]).reshape(TOK // 2, ROWS)
    yours = jnp.where(core == 0, pairs[:, 1], pairs[:, 0]).reshape(TOK // 2, ROWS)
    preact = jnp.concatenate([mine, yours], axis=0).astype(f32)
    normal_cdf = 0.5 * (1.0 + lax.erf(preact * root_half))
    hidden = (preact * normal_cdf).astype(bf16)
    slope = normal_cdf + preact * jnp.exp(-0.5 * preact * preact) * density_norm
    scale_power = exponents.astype(f32)
    shrink = jnp.tile(jnp.exp2(-scale_power).astype(bf16), (1, SEG // TILE))
    left, scale = expand_hidden(hidden, shrink, spread, widen, same, choice, gather)
    sign_row = (1 - 2 * signs).astype(f32).reshape(1, COLS)
    turned_weight = rotate_weight(w_down, sign_row, had)
    offset = lax.axis_index(("z_lo", "x")) * OWN
    own_power = jnp.exp2(lax.dynamic_slice_in_dim(scale_power, offset, OWN, 0))
    own_weight = lax.dynamic_slice_in_dim(w_down, offset, OWN, 0)

    own, left, scale, turned_weight, own_power, own_weight = lax.optimization_barrier(
        (own, left, scale, turned_weight, own_power, own_weight)
    )
    other = lax.ppermute(own, "core", [(0, 1), (1, 0)])
    encoded = encode(left, own, other, scale)
    summed = lax.psum_scatter(encoded, "x", scatter_dimension=0, tiled=True)
    plane = lax.axis_index("z_lo").astype(jnp.int32).reshape(1)
    kept, given = split(plane, summed)
    taken = lax.ppermute(given, "z_lo", [(0, 1), (1, 0)])
    states = (own_power, sign_row, had, first_moment, second_moment, own_weight)
    grad_mean, first_new, second_new, sent = update(kept, taken, *states)
    weight_new = place(to_all(sent, ("z_lo", "x"), REPLICAS))

    mixed = pre_grad_product(own, other, turned_weight, slope, widen)
    halves = mixed.reshape(2, PEERS, 2, ROWS)
    zero = jnp.where(core == 0, halves[0], halves[1])
    one = jnp.where(core == 0, halves[1], halves[0])
    pre_grad = jnp.stack([zero, one], axis=1).reshape(TOK, ROWS)
    return (pre_grad, grad_mean, first_new, second_new, weight_new)


def solution(mesh):
    fine = Mesh(
        mesh.devices.reshape(2, 8, 4, 8, 2), ("z_lo", "x", "z_hi", "y", "core")
    )
    dp = ("z_lo", "x")
    mp = ("z_hi", "y", "core")
    placed = (
        P(dp + mp, None),
        P(dp, mp),
        P(mp, None),
        P(mp + dp, None),
        P(mp + dp, None),
        P(),
        P(mp, None),
    )
    return jax.shard_map(
        body,
        mesh=fine,
        in_specs=placed,
        out_specs=(
            P(dp, mp),
            P(mp + dp, None),
            P(mp + dp, None),
            P(mp + dp, None),
            P(mp, None),
        ),
        check_vma=False,
    )
```

```python
import jax
import jax.numpy as jnp
import numpy as np
from jax import lax
from jax.experimental import pallas as pl
from jax.experimental.pallas import tpu as pltpu
from jax.sharding import Mesh
from jax.sharding import PartitionSpec as P

hadamard_norm = 0.03125
clip_limit = 448.0
root_half = 0.7071067811865476
density_norm = 0.3989422804014327

REPLICAS = 16
ROWS = 192
OWN = 12
COLS = 6144
SEGS = 4
SEG = 1536
BLOCKS = 6
LINE = 8
KEPT = 47
SPARE = 128
RING = 640
TILE = 256
TOK = 128
PEERS = 32
LANES = 128
bf16 = jnp.bfloat16
f32 = jnp.float32


def hadamard(order):
    indices = np.arange(order)
    common = indices[:, None] & indices[None, :]
    parity = np.zeros((order, order), np.int64)
    for position in range(order.bit_length() - 1):
        parity += common >> position & 1
    return (1 - 2 * (parity % 2)).astype(np.float32)


def tables():
    owner = np.concatenate([np.repeat(np.arange(REPLICAS), KEPT), np.arange(REPLICAS)])
    part = np.concatenate([np.tile(np.arange(KEPT), REPLICAS), np.full(REPLICAS, KEPT)])
    segment, own = part // OWN, part % OWN
    spread = (owner * OWN + own)[:, None] == np.arange(ROWS)[None, :]
    col = np.arange(2 * PEERS * SEGS * 2)
    patch = col // (SEGS * 2) * 2 + col % 2
    col_segment = col % (SEGS * 2) // 2
    widen = np.arange(TOK)[:, None] == patch[None, :]
    same = segment[:, None] == col_segment[None, :]
    tiles = SEG // TILE
    block = (3 * segment[:, None] + np.arange(tiles)[None, :] // 2) // 2
    choice = block[:, :, None] == np.arange(BLOCKS)
    gather = np.repeat(np.eye(tiles), BLOCKS, axis=0)
    shown = (spread, widen, same, choice.reshape(owner.size, -1), gather)
    return [jnp.asarray(table, bf16) for table in shown]


def butterfly(parts):
    parts = list(parts)
    span = 1
    while span < len(parts):
        for start in range(0, len(parts), 2 * span):
            for k in range(start, start + span):
                first, second = parts[k], parts[k + span]
                parts[k], parts[k + span] = first + second, first - second
        span *= 2
    return parts


def whole(shape):
    return pl.BlockSpec(shape, lambda *_: (0,) * len(shape))


def params(mebibytes=8):
    return pltpu.CompilerParams(vmem_limit_bytes=mebibytes << 20)


def rotate_upstream_kernel(
    u_hbm, sign_hbm, had_hbm, out_ref, u_ref, sign_ref, had_ref, x_ref, z_ref, sems
):
    pairs = ((u_hbm, u_ref), (sign_hbm, sign_ref), (had_hbm, had_ref))
    copies = [
        pltpu.make_async_copy(source, target, sems.at[k])
        for k, (source, target) in enumerate(pairs)
    ]
    for copy in copies:
        copy.start()
    for copy in copies:
        copy.wait()
    turned = u_ref[...].astype(f32) * (1 - 2 * sign_ref[...]).astype(f32)
    for t in range(COLS // LANES):
        x_ref[2 * t : 2 * t + 2, :] = turned[:, LANES * t : LANES * (t + 1)]
    x_ref[...] = jnp.dot(
        x_ref[...].astype(bf16), had_ref[...], preferred_element_type=f32
    )
    for b in range(BLOCKS):
        mixed = butterfly([x_ref[2 * t : 2 * t + 2, :] for t in range(8 * b, 8 * b + 8)])
        for k, part in enumerate(mixed):
            s, lane = divmod(8 * b + k, SEG // LANES)
            z_ref[2 * s : 2 * s + 2, LANES * lane : LANES * (lane + 1)] = (
                part * hadamard_norm
            )
    out_ref[...] = z_ref[...].astype(bf16)


def rotate_upstream(upstream, signs, had):
    arrays = [
        pltpu.with_memory_space_constraint(array, pltpu.HBM)
        for array in (upstream, signs, had)
    ]
    return pl.pallas_call(
        rotate_upstream_kernel,
        out_shape=jax.ShapeDtypeStruct((2 * SEGS, SEG), bf16),
        in_specs=[pl.BlockSpec(memory_space=pltpu.HBM)] * 3,
        scratch_shapes=[pltpu.VMEM(array.shape, array.dtype) for array in arrays]
        + [
            pltpu.VMEM((2 * COLS // LANES, LANES), f32),
            pltpu.VMEM((2 * SEGS, SEG), f32),
            pltpu.SemaphoreType.DMA((3,)),
        ],
        compiler_params=params(),
        name="rotate_upstream",
    )(*arrays)


def expand_hidden_kernel(
    hidden_ref, shrink_ref, spread_ref, widen_ref, same_ref, choice_ref, gather_ref,
    out_ref, scale_ref,
):
    rows = lax.dot_general(
        spread_ref[...],
        hidden_ref[...],
        (((1,), (1,)), ((), ())),
        preferred_element_type=f32,
    ).astype(bf16)
    wide = jnp.dot(rows, widen_ref[...], preferred_element_type=f32)
    out_ref[...] = (wide * same_ref[...].astype(f32)).astype(bf16)
    every = jnp.dot(spread_ref[...], shrink_ref[...], preferred_element_type=f32)
    chosen = (every * choice_ref[...].astype(f32)).astype(bf16)
    scale_ref[...] = jnp.dot(chosen, gather_ref[...], preferred_element_type=f32)


def expand_hidden(hidden, shrink, spread, widen, same, choice, gather):
    return pl.pallas_call(
        expand_hidden_kernel,
        out_shape=(
            jax.ShapeDtypeStruct(same.shape, bf16),
            jax.ShapeDtypeStruct((same.shape[0], gather.shape[1]), f32),
        ),
        compiler_params=params(),
        cost_estimate=pl.CostEstimate(
            flops=2 * 768 * 128 * 700, bytes_accessed=4 << 20, transcendentals=0
        ),
        name="expand_hidden",
    )(hidden, shrink, spread, widen, same, choice, gather)


def encode_kernel(left_ref, own_ref, other_ref, scale_ref, out_ref, spare_ref):
    depth = own_ref.shape[0]
    full = REPLICAS * KEPT
    scales = scale_ref[...]
    spare_ref[...] = jnp.zeros_like(spare_ref)
    for n in range(SEG // TILE):
        lanes = slice(TILE * n, TILE * (n + 1))
        total = jnp.dot(
            left_ref[:, :depth], own_ref[:, lanes], preferred_element_type=f32
        )
        total += jnp.dot(
            left_ref[:, depth:], other_ref[:, lanes], preferred_element_type=f32
        )
        total = jnp.clip(total * scales[:, n : n + 1], -clip_limit, clip_limit)
        out_ref[:, lanes] = total[:full].astype(bf16)
        for k in range(TILE // SPARE):
            rows = pl.ds(TILE // SPARE * n + k, REPLICAS, stride=KEPT)
            spare_ref[rows, :] = total[full:, SPARE * k : SPARE * (k + 1)]
    out_ref[:, SEG:] = spare_ref[...].astype(bf16)


def encode(left, own, other, scale):
    full = REPLICAS * KEPT
    depth = own.shape[0]
    shape = (full, SEG + SPARE)
    return pl.pallas_call(
        encode_kernel,
        out_shape=pltpu.HBM(shape, bf16),
        grid=(1,),
        in_specs=[whole(array.shape) for array in (left, own, other, scale)],
        out_specs=whole(shape),
        scratch_shapes=[pltpu.VMEM((full, SPARE), f32)],
        compiler_params=params(24),
        cost_estimate=pl.CostEstimate(
            flops=4 * full * depth * SEG, bytes_accessed=6 << 20, transcendentals=0
        ),
        name="encode",
    )(left, own, other, scale)


def update_kernel(
    received_ref, power_ref, sign_ref, had_ref, first_ref, second_ref, weight_ref,
    mean_ref, first_out, second_out, ring_ref, direct_ref, sum_ref, x_ref, y_ref,
):
    total = received_ref[...].astype(f32)
    sum_ref[:KEPT, :] = total[:, :SEG]
    for k in range(SEG // SPARE):
        sum_ref[KEPT : KEPT + 1, SPARE * k : SPARE * (k + 1)] = total[k : k + 1, SEG:]
    x_ref[...] = jnp.zeros_like(x_ref)
    for t in range(COLS // LANES):
        s, lane = divmod(t, SEG // LANES)
        x_ref[16 * t : 16 * t + OWN, :] = (
            sum_ref[OWN * s : OWN * (s + 1), LANES * lane : LANES * (lane + 1)]
            * power_ref[:, t // 8 : t // 8 + 1]
        )
    x = x_ref[...]
    high = x.astype(bf16)
    low = (x - high.astype(f32)).astype(bf16)
    y_ref[...] = jnp.dot(high, had_ref[...], preferred_element_type=f32) + jnp.dot(
        low, had_ref[...], preferred_element_type=f32
    )
    for b in range(BLOCKS):
        mixed = butterfly(
            [y_ref[16 * t : 16 * t + OWN, :] for t in range(8 * b, 8 * b + 8)]
        )
        for k, part in enumerate(mixed):
            t = 8 * b + k
            s, lane = divmod(t, SEG // LANES)
            lanes = slice(LANES * t, LANES * (t + 1))
            mean = part * (hadamard_norm / REPLICAS) * sign_ref[:, lanes]
            mean_ref[:, lanes] = mean
            first = 0.9 * first_ref[:, lanes] + 0.1 * mean
            second = 0.95 * second_ref[:, lanes] + 0.05 * mean * mean
            first_out[:, lanes] = first
            second_out[:, lanes] = second
            adjusted = first / 0.6513215599 / (jnp.sqrt(second / 0.4012630608) + 1e-08)
            sum_ref[OWN * s : OWN * (s + 1), LANES * lane : LANES * (lane + 1)] = (
                weight_ref[:, lanes].astype(f32) * (1.0 - 0.01 * 0.1) - 0.01 * adjusted
            )
    ring_ref[...] = sum_ref[:, :RING].astype(bf16)
    direct_ref[...] = jnp.broadcast_to(
        sum_ref[:, RING:].astype(bf16)[None], direct_ref.shape
    )


def update(received, power, sign_row, had, first, second, weight):
    own = jax.ShapeDtypeStruct((OWN, COLS), f32)
    return pl.pallas_call(
        update_kernel,
        out_shape=(
            own,
            own,
            own,
            jax.ShapeDtypeStruct((SEGS * OWN, RING), bf16),
            jax.ShapeDtypeStruct((REPLICAS, SEGS * OWN, SEG - RING), bf16),
        ),
        scratch_shapes=[
            pltpu.VMEM((SEGS * OWN, SEG), f32),
            pltpu.VMEM((16 * COLS // LANES, LANES), f32),
            pltpu.VMEM((16 * COLS // LANES, LANES), f32),
        ],
        compiler_params=params(),
        name="update",
    )(received, power, sign_row, had, first, second, weight)


def place_kernel(ring_ref, direct_ref, out_ref, rows_ref):
    for d in range(REPLICAS):
        here = d % LINE * 2 + d // LINE
        parts = ((0, ring_ref[here].astype(f32)), (RING, direct_ref[d].astype(f32)))
        for lane, chunk in parts:
            for s in range(SEGS):
                start = SEG * s + lane
                rows_ref[OWN * d : OWN * (d + 1), start : start + chunk.shape[1]] = (
                    chunk[OWN * s : OWN * (s + 1), :]
                )
    out_ref[...] = rows_ref[...].astype(bf16)


def place(ring, direct):
    return pl.pallas_call(
        place_kernel,
        out_shape=jax.ShapeDtypeStruct((ROWS, COLS), bf16),
        scratch_shapes=[pltpu.VMEM((ROWS, COLS), f32)],
        compiler_params=params(20),
        name="place",
    )(ring, direct)


def rotate_weight_kernel(w_ref, sign_ref, had_ref, out_ref):
    turned = w_ref[...].astype(f32) * sign_ref[...]
    parts = [
        jnp.dot(
            turned[:, LANES * k : LANES * (k + 1)].astype(bf16),
            had_ref[...],
            preferred_element_type=f32,
        )
        for k in range(8)
    ]
    for k, part in enumerate(butterfly(parts)):
        out_ref[:, LANES * k : LANES * (k + 1)] = (part * hadamard_norm).astype(bf16)


def rotate_weight(weight, sign_row, had):
    return pl.pallas_call(
        rotate_weight_kernel,
        out_shape=jax.ShapeDtypeStruct((ROWS, COLS), bf16),
        grid=(BLOCKS,),
        in_specs=[
            pl.BlockSpec((ROWS, 1024), lambda b: (0, b)),
            pl.BlockSpec((1, 1024), lambda b: (0, b)),
            whole((LANES, LANES)),
        ],
        out_specs=pl.BlockSpec((ROWS, 1024), lambda b: (0, b)),
        compiler_params=params(),
        cost_estimate=pl.CostEstimate(
            flops=2 * ROWS * COLS * 1024, bytes_accessed=5 << 20, transcendentals=0
        ),
        name="rotate_weight",
    )(weight, sign_row, had)


def pre_grad_kernel(own_ref, other_ref, w_ref, slope_ref, collect_ref, out_ref, acc_ref):
    half = own_ref.shape[0]
    place_in_pair = lax.broadcasted_iota(jnp.int32, (half, 1), 0) & (2 * SEGS - 1)
    for index, rows_ref in enumerate((own_ref, other_ref)):
        rows = rows_ref[...]
        total = jnp.zeros((half, ROWS), f32)
        for s in range(SEGS):
            part = lax.dot_general(
                rows,
                w_ref[:, SEG * s : SEG * (s + 1)],
                (((1,), (1,)), ((), ())),
                preferred_element_type=f32,
            )
            total = jnp.where(place_in_pair >> 1 == s, part, total)
        acc_ref[half * index : half * (index + 1), :] = total
    hidden_grad = jnp.dot(
        collect_ref[...].astype(f32),
        acc_ref[...],
        precision=lax.Precision.HIGHEST,
        preferred_element_type=f32,
    )
    out_ref[...] = (hidden_grad * slope_ref[...]).astype(bf16)


def pre_grad_product(own, other, weight, slope, collect):
    return pl.pallas_call(
        pre_grad_kernel,
        out_shape=jax.ShapeDtypeStruct((TOK, ROWS), bf16),
        scratch_shapes=[pltpu.VMEM((2 * own.shape[0], ROWS), f32)],
        compiler_params=params(16),
        cost_estimate=pl.CostEstimate(
            flops=8 * 512 * SEG * ROWS, bytes_accessed=6 << 20, transcendentals=0
        ),
        name="pre_grad",
    )(own, other, weight, slope, collect)


def to_all(values, axes, count):
    return lax.all_to_all(
        jnp.broadcast_to(values[None], (count,) + values.shape), axes, 0, 0, tiled=True
    )


def body(upstream, pre_act, w_down, first_moment, second_moment, signs, exponents):
    spread, widen, same, choice, gather = tables()
    had = jnp.asarray(hadamard(LANES), bf16)
    core = lax.axis_index("core")

    rotated = rotate_upstream(upstream, signs.reshape(1, COLS), had)
    own = to_all(rotated, ("z_hi", "y"), PEERS).reshape(-1, SEG)

    pairs = pre_act.reshape(PEERS, 2, 2, ROWS)
    mine = jnp.where(core == 0, pairs[:, 0], pairs[:, 1]).reshape(TOK // 2, ROWS)
    yours = jnp.where(core == 0, pairs[:, 1], pairs[:, 0]).reshape(TOK // 2, ROWS)
    preact = jnp.concatenate([mine, yours], axis=0).astype(f32)
    normal_cdf = 0.5 * (1.0 + lax.erf(preact * root_half))
    hidden = (preact * normal_cdf).astype(bf16)
    slope = normal_cdf + preact * jnp.exp(-0.5 * preact * preact) * density_norm
    scale_power = exponents.astype(f32)
    shrink = jnp.tile(jnp.exp2(-scale_power).astype(bf16), (1, SEG // TILE))
    left, scale = expand_hidden(hidden, shrink, spread, widen, same, choice, gather)
    sign_row = (1 - 2 * signs).astype(f32).reshape(1, COLS)
    turned_weight = rotate_weight(w_down, sign_row, had)
    offset = lax.axis_index(("z_lo", "x")) * OWN
    own_power = jnp.exp2(lax.dynamic_slice_in_dim(scale_power, offset, OWN, 0))
    own_weight = lax.dynamic_slice_in_dim(w_down, offset, OWN, 0)

    own, left, scale, turned_weight, own_power, own_weight = lax.optimization_barrier(
        (own, left, scale, turned_weight, own_power, own_weight)
    )
    other = lax.ppermute(own, "core", [(0, 1), (1, 0)])
    encoded = encode(left, own, other, scale)
    summed = lax.psum_scatter(encoded, ("z_lo", "x"), scatter_dimension=0, tiled=True)
    grad_mean, first_new, second_new, ring, direct = update(
        summed, own_power, sign_row, had, first_moment, second_moment, own_weight
    )
    across = lax.ppermute(ring, "z_lo", [(0, 1), (1, 0)])
    both = jnp.where(
        lax.axis_index("z_lo") == 0,
        jnp.concatenate([ring, across], axis=0),
        jnp.concatenate([across, ring], axis=0),
    )
    both, own, direct = lax.optimization_barrier((both, own, direct))
    direct = lax.all_to_all(direct, ("z_lo", "x"), 0, 0, tiled=True)
    ring = lax.all_gather(both, "x", axis=0, tiled=True)
    weight_new = place(ring.reshape(REPLICAS, SEGS * OWN, RING), direct)

    mixed = pre_grad_product(own, other, turned_weight, slope, widen)
    halves = mixed.reshape(2, PEERS, 2, ROWS)
    zero = jnp.where(core == 0, halves[0], halves[1])
    one = jnp.where(core == 0, halves[1], halves[0])
    pre_grad = jnp.stack([zero, one], axis=1).reshape(TOK, ROWS)
    return (pre_grad, grad_mean, first_new, second_new, weight_new)


def solution(mesh):
    fine = Mesh(
        mesh.devices.reshape(2, 8, 4, 8, 2), ("z_lo", "x", "z_hi", "y", "core")
    )
    dp = ("z_lo", "x")
    mp = ("z_hi", "y", "core")
    placed = (
        P(dp + mp, None),
        P(dp, mp),
        P(mp, None),
        P(mp + dp, None),
        P(mp + dp, None),
        P(),
        P(mp, None),
    )
    return jax.shard_map(
        body,
        mesh=fine,
        in_specs=placed,
        out_specs=(
            P(dp, mp),
            P(mp + dp, None),
            P(mp + dp, None),
            P(mp + dp, None),
            P(mp, None),
        ),
        check_vma=False,
    )
```

```python
import jax
import jax.numpy as jnp
import numpy as np
from jax import lax
from jax.experimental import pallas as pl
from jax.experimental.pallas import tpu as pltpu
from jax.sharding import Mesh
from jax.sharding import PartitionSpec as P

hadamard_norm = 0.03125
clip_limit = 448.0
root_half = 0.7071067811865476
density_norm = 0.3989422804014327

REPLICAS = 16
ROWS = 192
OWN = 12
COLS = 6144
SEGS = 4
SEG = 1536
BLOCKS = 6
KEPT = 47
SPARE = 128
TILE = 256
TOK = 128
PEERS = 32
LANES = 128
bf16 = jnp.bfloat16
f32 = jnp.float32


def hadamard(order):
    indices = np.arange(order)
    common = indices[:, None] & indices[None, :]
    parity = np.zeros((order, order), np.int64)
    for position in range(order.bit_length() - 1):
        parity += common >> position & 1
    return (1 - 2 * (parity % 2)).astype(np.float32)


def tables():
    owner = np.concatenate([np.repeat(np.arange(REPLICAS), KEPT), np.arange(REPLICAS)])
    part = np.concatenate([np.tile(np.arange(KEPT), REPLICAS), np.full(REPLICAS, KEPT)])
    segment, own = part // OWN, part % OWN
    spread = (owner * OWN + own)[:, None] == np.arange(ROWS)[None, :]
    col = np.arange(2 * PEERS * SEGS * 2)
    patch = col // (SEGS * 2) * 2 + col % 2
    col_segment = col % (SEGS * 2) // 2
    widen = np.arange(TOK)[:, None] == patch[None, :]
    same = segment[:, None] == col_segment[None, :]
    tiles = SEG // TILE
    block = (3 * segment[:, None] + np.arange(tiles)[None, :] // 2) // 2
    choice = block[:, :, None] == np.arange(BLOCKS)
    gather = np.repeat(np.eye(tiles), BLOCKS, axis=0)
    shown = (spread, widen, same, choice.reshape(owner.size, -1), gather)
    return [jnp.asarray(table, bf16) for table in shown]


def butterfly(parts):
    parts = list(parts)
    span = 1
    while span < len(parts):
        for start in range(0, len(parts), 2 * span):
            for k in range(start, start + span):
                first, second = parts[k], parts[k + span]
                parts[k], parts[k + span] = first + second, first - second
        span *= 2
    return parts


def whole(shape):
    return pl.BlockSpec(shape, lambda *_: (0,) * len(shape))


def params(mebibytes=8):
    return pltpu.CompilerParams(vmem_limit_bytes=mebibytes << 20)


def rotate_upstream_kernel(
    u_hbm, sign_hbm, had_hbm, out_ref, u_ref, sign_ref, had_ref, x_ref, z_ref, sems
):
    pairs = ((u_hbm, u_ref), (sign_hbm, sign_ref), (had_hbm, had_ref))
    copies = [
        pltpu.make_async_copy(source, target, sems.at[k])
        for k, (source, target) in enumerate(pairs)
    ]
    for copy in copies:
        copy.start()
    for copy in copies:
        copy.wait()
    turned = u_ref[...].astype(f32) * (1 - 2 * sign_ref[...]).astype(f32)
    for t in range(COLS // LANES):
        x_ref[2 * t : 2 * t + 2, :] = turned[:, LANES * t : LANES * (t + 1)]
    x_ref[...] = jnp.dot(
        x_ref[...].astype(bf16), had_ref[...], preferred_element_type=f32
    )
    for b in range(BLOCKS):
        mixed = butterfly([x_ref[2 * t : 2 * t + 2, :] for t in range(8 * b, 8 * b + 8)])
        for k, part in enumerate(mixed):
            s, lane = divmod(8 * b + k, SEG // LANES)
            z_ref[2 * s : 2 * s + 2, LANES * lane : LANES * (lane + 1)] = (
                part * hadamard_norm
            )
    out_ref[...] = jnp.broadcast_to(z_ref[...].astype(bf16)[None], out_ref.shape)


def rotate_upstream(upstream, signs, had):
    arrays = [
        pltpu.with_memory_space_constraint(array, pltpu.HBM)
        for array in (upstream, signs, had)
    ]
    return pl.pallas_call(
        rotate_upstream_kernel,
        out_shape=pltpu.HBM((PEERS, 2 * SEGS, SEG), bf16),
        in_specs=[pl.BlockSpec(memory_space=pltpu.HBM)] * 3,
        scratch_shapes=[pltpu.VMEM(array.shape, array.dtype) for array in arrays]
        + [
            pltpu.VMEM((2 * COLS // LANES, LANES), f32),
            pltpu.VMEM((2 * SEGS, SEG), f32),
            pltpu.SemaphoreType.DMA((3,)),
        ],
        compiler_params=params(),
        name="rotate_upstream",
    )(*arrays)


def expand_hidden_kernel(
    hidden_ref, shrink_ref, spread_ref, widen_ref, same_ref, choice_ref, gather_ref,
    out_ref, scale_ref,
):
    rows = lax.dot_general(
        spread_ref[...],
        hidden_ref[...],
        (((1,), (1,)), ((), ())),
        preferred_element_type=f32,
    ).astype(bf16)
    wide = jnp.dot(rows, widen_ref[...], preferred_element_type=f32)
    out_ref[...] = (wide * same_ref[...].astype(f32)).astype(bf16)
    every = jnp.dot(spread_ref[...], shrink_ref[...], preferred_element_type=f32)
    chosen = (every * choice_ref[...].astype(f32)).astype(bf16)
    scale_ref[...] = jnp.dot(chosen, gather_ref[...], preferred_element_type=f32)


def expand_hidden(hidden, shrink, spread, widen, same, choice, gather):
    return pl.pallas_call(
        expand_hidden_kernel,
        out_shape=(
            jax.ShapeDtypeStruct(same.shape, bf16),
            jax.ShapeDtypeStruct((same.shape[0], gather.shape[1]), f32),
        ),
        compiler_params=params(),
        cost_estimate=pl.CostEstimate(
            flops=2 * 768 * 128 * 700, bytes_accessed=4 << 20, transcendentals=0
        ),
        name="expand_hidden",
    )(hidden, shrink, spread, widen, same, choice, gather)


def encode_kernel(
    left_ref, own_ref, other_ref, scale_ref, out_hbm, kept_hbm, done_ref, spare_ref, sems
):
    depth = own_ref.shape[0]
    full = REPLICAS * KEPT
    tiles = SEG // TILE
    scales = scale_ref[...]
    copies = [pltpu.make_async_copy(other_ref, kept_hbm, sems.at[0])]
    copies[0].start()

    def leave(lanes):
        copy = pltpu.make_async_copy(
            done_ref.at[:, lanes], out_hbm.at[:, lanes], sems.at[len(copies)]
        )
        copy.start()
        copies.append(copy)

    spare_ref[...] = jnp.zeros_like(spare_ref)
    for n in range(tiles):
        lanes = pl.ds(TILE * n, TILE)
        total = jnp.dot(
            left_ref[:, :depth], own_ref[:, lanes], preferred_element_type=f32
        )
        total += jnp.dot(
            left_ref[:, depth:], other_ref[:, lanes], preferred_element_type=f32
        )
        total = jnp.clip(total * scales[:, n : n + 1], -clip_limit, clip_limit)
        done_ref[:, lanes] = total[:full].astype(bf16)
        leave(lanes)
        for k in range(TILE // SPARE):
            rows = pl.ds(TILE // SPARE * n + k, REPLICAS, stride=KEPT)
            spare_ref[rows, :] = total[full:, SPARE * k : SPARE * (k + 1)]
    done_ref[:, SEG:] = spare_ref[...].astype(bf16)
    leave(pl.ds(SEG, SPARE))
    for copy in copies:
        copy.wait()


def encode(left, own, other, scale):
    full = REPLICAS * KEPT
    depth = own.shape[0]
    shape = (full, SEG + SPARE)
    return pl.pallas_call(
        encode_kernel,
        out_shape=(pltpu.HBM(shape, bf16), pltpu.HBM(other.shape, bf16)),
        out_specs=(pl.BlockSpec(memory_space=pltpu.HBM),) * 2,
        scratch_shapes=[
            pltpu.VMEM(shape, bf16),
            pltpu.VMEM((full, SPARE), f32),
            pltpu.SemaphoreType.DMA((SEG // TILE + 2,)),
        ],
        compiler_params=params(16),
        cost_estimate=pl.CostEstimate(
            flops=4 * full * depth * SEG, bytes_accessed=6 << 20, transcendentals=0
        ),
        name="encode",
    )(left, own, other, scale)


def update_kernel(
    received_ref, power_ref, sign_ref, had_ref, first_ref, second_ref, weight_ref,
    mean_ref, first_out, second_out, sent_ref, sum_ref, x_ref, y_ref,
):
    total = received_ref[...].astype(f32)
    sum_ref[:KEPT, :] = total[:, :SEG]
    for k in range(SEG // SPARE):
        sum_ref[KEPT : KEPT + 1, SPARE * k : SPARE * (k + 1)] = total[k : k + 1, SEG:]
    x_ref[...] = jnp.zeros_like(x_ref)
    for t in range(COLS // LANES):
        s, lane = divmod(t, SEG // LANES)
        x_ref[16 * t : 16 * t + OWN, :] = (
            sum_ref[OWN * s : OWN * (s + 1), LANES * lane : LANES * (lane + 1)]
            * power_ref[:, t // 8 : t // 8 + 1]
        )
    x = x_ref[...]
    high = x.astype(bf16)
    low = (x - high.astype(f32)).astype(bf16)
    y_ref[...] = jnp.dot(high, had_ref[...], preferred_element_type=f32) + jnp.dot(
        low, had_ref[...], preferred_element_type=f32
    )
    for b in range(BLOCKS):
        mixed = butterfly(
            [y_ref[16 * t : 16 * t + OWN, :] for t in range(8 * b, 8 * b + 8)]
        )
        for k, part in enumerate(mixed):
            t = 8 * b + k
            s, lane = divmod(t, SEG // LANES)
            lanes = slice(LANES * t, LANES * (t + 1))
            mean = part * (hadamard_norm / REPLICAS) * sign_ref[:, lanes]
            mean_ref[:, lanes] = mean
            first = 0.9 * first_ref[:, lanes] + 0.1 * mean
            second = 0.95 * second_ref[:, lanes] + 0.05 * mean * mean
            first_out[:, lanes] = first
            second_out[:, lanes] = second
            adjusted = first / 0.6513215599 / (jnp.sqrt(second / 0.4012630608) + 1e-08)
            sum_ref[OWN * s : OWN * (s + 1), LANES * lane : LANES * (lane + 1)] = (
                weight_ref[:, lanes].astype(f32) * (1.0 - 0.01 * 0.1) - 0.01 * adjusted
            )
    sent_ref[...] = jnp.broadcast_to(sum_ref[...].astype(bf16)[None], sent_ref.shape)


def update(received, power, sign_row, had, first, second, weight):
    own = jax.ShapeDtypeStruct((OWN, COLS), f32)
    return pl.pallas_call(
        update_kernel,
        out_shape=(
            own,
            own,
            own,
            pltpu.HBM((REPLICAS, SEGS * OWN, SEG), bf16),
        ),
        scratch_shapes=[
            pltpu.VMEM((SEGS * OWN, SEG), f32),
            pltpu.VMEM((16 * COLS // LANES, LANES), f32),
            pltpu.VMEM((16 * COLS // LANES, LANES), f32),
        ],
        compiler_params=params(),
        name="update",
    )(received, power, sign_row, had, first, second, weight)


GROUP = 4


def place_kernel(gathered_ref, out_hbm, rows_ref, done_ref, sems):
    step = GROUP * OWN
    copies = []
    for g in range(REPLICAS // GROUP):
        for k in range(GROUP):
            chunk = gathered_ref[GROUP * g + k].astype(f32)
            for s in range(SEGS):
                rows_ref[OWN * k : OWN * (k + 1), SEG * s : SEG * (s + 1)] = chunk[
                    OWN * s : OWN * (s + 1), :
                ]
        rows = pl.ds(step * g, step)
        done_ref[rows, :] = rows_ref[...].astype(bf16)
        copy = pltpu.make_async_copy(
            done_ref.at[rows, :], out_hbm.at[rows, :], sems.at[g]
        )
        copy.start()
        copies.append(copy)
    for copy in copies:
        copy.wait()


def place(gathered):
    return pl.pallas_call(
        place_kernel,
        out_shape=pltpu.HBM((ROWS, COLS), bf16),
        out_specs=pl.BlockSpec(memory_space=pltpu.HBM),
        scratch_shapes=[
            pltpu.VMEM((GROUP * OWN, COLS), f32),
            pltpu.VMEM((ROWS, COLS), bf16),
            pltpu.SemaphoreType.DMA((REPLICAS // GROUP,)),
        ],
        compiler_params=params(16),
        name="place",
    )(gathered)


def rotate_weight_kernel(w_ref, sign_ref, had_ref, out_ref):
    turned = w_ref[...].astype(f32) * sign_ref[...]
    parts = [
        jnp.dot(
            turned[:, LANES * k : LANES * (k + 1)].astype(bf16),
            had_ref[...],
            preferred_element_type=f32,
        )
        for k in range(8)
    ]
    for k, part in enumerate(butterfly(parts)):
        out_ref[:, LANES * k : LANES * (k + 1)] = (part * hadamard_norm).astype(bf16)


def rotate_weight(weight, sign_row, had):
    return pl.pallas_call(
        rotate_weight_kernel,
        out_shape=jax.ShapeDtypeStruct((ROWS, COLS), bf16),
        grid=(BLOCKS,),
        in_specs=[
            pl.BlockSpec((ROWS, 1024), lambda b: (0, b)),
            pl.BlockSpec((1, 1024), lambda b: (0, b)),
            whole((LANES, LANES)),
        ],
        out_specs=pl.BlockSpec((ROWS, 1024), lambda b: (0, b)),
        compiler_params=params(),
        cost_estimate=pl.CostEstimate(
            flops=2 * ROWS * COLS * 1024, bytes_accessed=5 << 20, transcendentals=0
        ),
        name="rotate_weight",
    )(weight, sign_row, had)


def pre_grad_kernel(own_ref, other_ref, w_ref, slope_ref, collect_ref, out_ref, acc_ref):
    half = own_ref.shape[0]
    place_in_pair = lax.broadcasted_iota(jnp.int32, (half, 1), 0) & (2 * SEGS - 1)
    for index, rows_ref in enumerate((own_ref, other_ref)):
        rows = rows_ref[...]
        total = jnp.zeros((half, ROWS), f32)
        for s in range(SEGS):
            part = lax.dot_general(
                rows,
                w_ref[:, SEG * s : SEG * (s + 1)],
                (((1,), (1,)), ((), ())),
                preferred_element_type=f32,
            )
            total = jnp.where(place_in_pair >> 1 == s, part, total)
        acc_ref[half * index : half * (index + 1), :] = total
    hidden_grad = jnp.dot(
        collect_ref[...].astype(f32),
        acc_ref[...],
        precision=lax.Precision.HIGHEST,
        preferred_element_type=f32,
    )
    out_ref[...] = (hidden_grad * slope_ref[...]).astype(bf16)


def pre_grad_product(own, other, weight, slope, collect):
    return pl.pallas_call(
        pre_grad_kernel,
        out_shape=jax.ShapeDtypeStruct((TOK, ROWS), bf16),
        scratch_shapes=[pltpu.VMEM((2 * own.shape[0], ROWS), f32)],
        compiler_params=params(16),
        cost_estimate=pl.CostEstimate(
            flops=8 * 512 * SEG * ROWS, bytes_accessed=6 << 20, transcendentals=0
        ),
        name="pre_grad",
    )(own, other, weight, slope, collect)


def to_all(copies, axes):
    return lax.all_to_all(copies, axes, 0, 0, tiled=True)


def body(upstream, pre_act, w_down, first_moment, second_moment, signs, exponents):
    spread, widen, same, choice, gather = tables()
    had = jnp.asarray(hadamard(LANES), bf16)
    core = lax.axis_index("core")

    rotated = rotate_upstream(upstream, signs.reshape(1, COLS), had)
    own = to_all(rotated, ("z_hi", "y")).reshape(-1, SEG)

    pairs = pre_act.reshape(PEERS, 2, 2, ROWS)
    mine = jnp.where(core == 0, pairs[:, 0], pairs[:, 1]).reshape(TOK // 2, ROWS)
    yours = jnp.where(core == 0, pairs[:, 1], pairs[:, 0]).reshape(TOK // 2, ROWS)
    preact = jnp.concatenate([mine, yours], axis=0).astype(f32)
    normal_cdf = 0.5 * (1.0 + lax.erf(preact * root_half))
    hidden = (preact * normal_cdf).astype(bf16)
    slope = normal_cdf + preact * jnp.exp(-0.5 * preact * preact) * density_norm
    scale_power = exponents.astype(f32)
    shrink = jnp.tile(jnp.exp2(-scale_power).astype(bf16), (1, SEG // TILE))
    left, scale = expand_hidden(hidden, shrink, spread, widen, same, choice, gather)
    sign_row = (1 - 2 * signs).astype(f32).reshape(1, COLS)
    turned_weight = rotate_weight(w_down, sign_row, had)
    offset = lax.axis_index(("z_lo", "x")) * OWN
    own_power = jnp.exp2(lax.dynamic_slice_in_dim(scale_power, offset, OWN, 0))
    own_weight = lax.dynamic_slice_in_dim(w_down, offset, OWN, 0)

    own, left, scale, turned_weight, own_power, own_weight = lax.optimization_barrier(
        (own, left, scale, turned_weight, own_power, own_weight)
    )
    other = lax.ppermute(own, "core", [(0, 1), (1, 0)])
    encoded, other = encode(left, own, other, scale)
    summed = lax.psum_scatter(encoded, ("z_lo", "x"), scatter_dimension=0, tiled=True)
    grad_mean, first_new, second_new, sent = update(
        summed, own_power, sign_row, had, first_moment, second_moment, own_weight
    )
    weight_new = place(to_all(sent, ("z_lo", "x")))

    mixed = pre_grad_product(own, other, turned_weight, slope, widen)
    halves = mixed.reshape(2, PEERS, 2, ROWS)
    zero = jnp.where(core == 0, halves[0], halves[1])
    one = jnp.where(core == 0, halves[1], halves[0])
    pre_grad = jnp.stack([zero, one], axis=1).reshape(TOK, ROWS)
    return (pre_grad, grad_mean, first_new, second_new, weight_new)


def solution(mesh):
    fine = Mesh(
        mesh.devices.reshape(2, 8, 4, 8, 2), ("z_lo", "x", "z_hi", "y", "core")
    )
    dp = ("z_lo", "x")
    mp = ("z_hi", "y", "core")
    placed = (
        P(dp + mp, None),
        P(dp, mp),
        P(mp, None),
        P(mp + dp, None),
        P(mp + dp, None),
        P(),
        P(mp, None),
    )
    return jax.shard_map(
        body,
        mesh=fine,
        in_specs=placed,
        out_specs=(
            P(dp, mp),
            P(mp + dp, None),
            P(mp + dp, None),
            P(mp + dp, None),
            P(mp, None),
        ),
        check_vma=False,
    )
```

```python
import jax
import jax.numpy as jnp
import numpy as np
from jax import lax
from jax.experimental import pallas as pl
from jax.experimental.pallas import tpu as pltpu
from jax.sharding import Mesh
from jax.sharding import PartitionSpec as P

hadamard_norm = 0.03125
clip_limit = 448.0
root_half = 0.7071067811865476
density_norm = 0.3989422804014327

REPLICAS = 16
ROWS = 192
OWN = 12
COLS = 6144
SEGS = 4
SEG = 1536
BLOCKS = 6
KEPT = 47
SPARE = 128
TILE = 256
TOK = 128
PEERS = 32
LANES = 128
bf16 = jnp.bfloat16
f32 = jnp.float32


def hadamard(order):
    indices = np.arange(order)
    common = indices[:, None] & indices[None, :]
    parity = np.zeros((order, order), np.int64)
    for position in range(order.bit_length() - 1):
        parity += common >> position & 1
    return (1 - 2 * (parity % 2)).astype(np.float32)


def tables():
    owner = np.concatenate([np.repeat(np.arange(REPLICAS), KEPT), np.arange(REPLICAS)])
    part = np.concatenate([np.tile(np.arange(KEPT), REPLICAS), np.full(REPLICAS, KEPT)])
    segment, own = part // OWN, part % OWN
    spread = (owner * OWN + own)[:, None] == np.arange(ROWS)[None, :]
    col = np.arange(2 * PEERS * SEGS * 2)
    patch = col // (SEGS * 2) * 2 + col % 2
    col_segment = col % (SEGS * 2) // 2
    widen = np.arange(TOK)[:, None] == patch[None, :]
    same = segment[:, None] == col_segment[None, :]
    tiles = SEG // TILE
    block = (3 * segment[:, None] + np.arange(tiles)[None, :] // 2) // 2
    choice = block[:, :, None] == np.arange(BLOCKS)
    gather = np.repeat(np.eye(tiles), BLOCKS, axis=0)
    shown = (spread, widen, same, choice.reshape(owner.size, -1), gather)
    return [jnp.asarray(table, bf16) for table in shown]


def butterfly(parts):
    parts = list(parts)
    span = 1
    while span < len(parts):
        for start in range(0, len(parts), 2 * span):
            for k in range(start, start + span):
                first, second = parts[k], parts[k + span]
                parts[k], parts[k + span] = first + second, first - second
        span *= 2
    return parts


def whole(shape):
    return pl.BlockSpec(shape, lambda *_: (0,) * len(shape))


def params(mebibytes=8):
    return pltpu.CompilerParams(vmem_limit_bytes=mebibytes << 20)


def rotate_upstream_kernel(
    u_hbm, sign_hbm, had_hbm, out_ref, u_ref, sign_ref, had_ref, x_ref, z_ref, sems
):
    pairs = ((u_hbm, u_ref), (sign_hbm, sign_ref), (had_hbm, had_ref))
    copies = [
        pltpu.make_async_copy(source, target, sems.at[k])
        for k, (source, target) in enumerate(pairs)
    ]
    for copy in copies:
        copy.start()
    for copy in copies:
        copy.wait()
    turned = u_ref[...].astype(f32) * (1 - 2 * sign_ref[...]).astype(f32)
    for t in range(COLS // LANES):
        x_ref[2 * t : 2 * t + 2, :] = turned[:, LANES * t : LANES * (t + 1)]
    x_ref[...] = jnp.dot(
        x_ref[...].astype(bf16), had_ref[...], preferred_element_type=f32
    )
    for b in range(BLOCKS):
        mixed = butterfly([x_ref[2 * t : 2 * t + 2, :] for t in range(8 * b, 8 * b + 8)])
        for k, part in enumerate(mixed):
            s, lane = divmod(8 * b + k, SEG // LANES)
            z_ref[2 * s : 2 * s + 2, LANES * lane : LANES * (lane + 1)] = (
                part * hadamard_norm
            )
    out_ref[...] = jnp.broadcast_to(z_ref[...].astype(bf16)[None], out_ref.shape)


def rotate_upstream(upstream, signs, had):
    arrays = [
        pltpu.with_memory_space_constraint(array, pltpu.HBM)
        for array in (upstream, signs, had)
    ]
    return pl.pallas_call(
        rotate_upstream_kernel,
        out_shape=pltpu.HBM((PEERS, 2 * SEGS, SEG), bf16),
        in_specs=[pl.BlockSpec(memory_space=pltpu.HBM)] * 3,
        scratch_shapes=[pltpu.VMEM(array.shape, array.dtype) for array in arrays]
        + [
            pltpu.VMEM((2 * COLS // LANES, LANES), f32),
            pltpu.VMEM((2 * SEGS, SEG), f32),
            pltpu.SemaphoreType.DMA((3,)),
        ],
        compiler_params=params(),
        name="rotate_upstream",
    )(*arrays)


def expand_hidden_kernel(
    hidden_ref, shrink_ref, spread_ref, widen_ref, same_ref, choice_ref, gather_ref,
    out_ref, scale_ref,
):
    rows = lax.dot_general(
        spread_ref[...],
        hidden_ref[...],
        (((1,), (1,)), ((), ())),
        preferred_element_type=f32,
    ).astype(bf16)
    wide = jnp.dot(rows, widen_ref[...], preferred_element_type=f32)
    out_ref[...] = (wide * same_ref[...].astype(f32)).astype(bf16)
    every = jnp.dot(spread_ref[...], shrink_ref[...], preferred_element_type=f32)
    chosen = (every * choice_ref[...].astype(f32)).astype(bf16)
    scale_ref[...] = jnp.dot(chosen, gather_ref[...], preferred_element_type=f32)


def expand_hidden(hidden, shrink, spread, widen, same, choice, gather):
    return pl.pallas_call(
        expand_hidden_kernel,
        out_shape=(
            jax.ShapeDtypeStruct(same.shape, bf16),
            jax.ShapeDtypeStruct((same.shape[0], gather.shape[1]), f32),
        ),
        compiler_params=params(),
        cost_estimate=pl.CostEstimate(
            flops=2 * 768 * 128 * 700, bytes_accessed=4 << 20, transcendentals=0
        ),
        name="expand_hidden",
    )(hidden, shrink, spread, widen, same, choice, gather)


def encode_kernel(
    left_ref, own_ref, other_ref, scale_ref, out_hbm, kept_hbm, done_ref, spare_ref, sems
):
    depth = own_ref.shape[0]
    full = REPLICAS * KEPT
    tiles = SEG // TILE
    scales = scale_ref[...]
    copies = [pltpu.make_async_copy(other_ref, kept_hbm, sems.at[0])]
    copies[0].start()

    def leave(lanes):
        copy = pltpu.make_async_copy(
            done_ref.at[:, lanes], out_hbm.at[:, lanes], sems.at[len(copies)]
        )
        copy.start()
        copies.append(copy)

    spare_ref[...] = jnp.zeros_like(spare_ref)
    for n in range(tiles):
        lanes = pl.ds(TILE * n, TILE)
        total = jnp.dot(
            left_ref[:, :depth], own_ref[:, lanes], preferred_element_type=f32
        )
        total += jnp.dot(
            left_ref[:, depth:], other_ref[:, lanes], preferred_element_type=f32
        )
        total = jnp.clip(total * scales[:, n : n + 1], -clip_limit, clip_limit)
        done_ref[:, lanes] = total[:full].astype(bf16)
        leave(lanes)
        for k in range(TILE // SPARE):
            rows = pl.ds(TILE // SPARE * n + k, REPLICAS, stride=KEPT)
            spare_ref[rows, :] = total[full:, SPARE * k : SPARE * (k + 1)]
    done_ref[:, SEG:] = spare_ref[...].astype(bf16)
    leave(pl.ds(SEG, SPARE))
    for copy in copies:
        copy.wait()


def encode(left, own, other, scale):
    full = REPLICAS * KEPT
    depth = own.shape[0]
    shape = (full, SEG + SPARE)
    return pl.pallas_call(
        encode_kernel,
        out_shape=(pltpu.HBM(shape, bf16), pltpu.HBM(other.shape, bf16)),
        out_specs=(pl.BlockSpec(memory_space=pltpu.HBM),) * 2,
        scratch_shapes=[
            pltpu.VMEM(shape, bf16),
            pltpu.VMEM((full, SPARE), f32),
            pltpu.SemaphoreType.DMA((SEG // TILE + 2,)),
        ],
        compiler_params=params(16),
        cost_estimate=pl.CostEstimate(
            flops=4 * full * depth * SEG, bytes_accessed=6 << 20, transcendentals=0
        ),
        name="encode",
    )(left, own, other, scale)


def update_kernel(
    received_ref, power_ref, sign_ref, had_ref, first_ref, second_ref, weight_ref,
    mean_ref, first_out, second_out, sent_ref, sum_ref, x_ref, y_ref,
):
    total = received_ref[...].astype(f32)
    sum_ref[:KEPT, :] = total[:, :SEG]
    for k in range(SEG // SPARE):
        sum_ref[KEPT : KEPT + 1, SPARE * k : SPARE * (k + 1)] = total[k : k + 1, SEG:]
    x_ref[...] = jnp.zeros_like(x_ref)
    for t in range(COLS // LANES):
        s, lane = divmod(t, SEG // LANES)
        x_ref[16 * t : 16 * t + OWN, :] = (
            sum_ref[OWN * s : OWN * (s + 1), LANES * lane : LANES * (lane + 1)]
            * power_ref[:, t // 8 : t // 8 + 1]
        )
    x = x_ref[...]
    high = x.astype(bf16)
    low = (x - high.astype(f32)).astype(bf16)
    y_ref[...] = jnp.dot(high, had_ref[...], preferred_element_type=f32) + jnp.dot(
        low, had_ref[...], preferred_element_type=f32
    )
    for b in range(BLOCKS):
        mixed = butterfly(
            [y_ref[16 * t : 16 * t + OWN, :] for t in range(8 * b, 8 * b + 8)]
        )
        for k, part in enumerate(mixed):
            t = 8 * b + k
            s, lane = divmod(t, SEG // LANES)
            lanes = slice(LANES * t, LANES * (t + 1))
            mean = part * (hadamard_norm / REPLICAS) * sign_ref[:, lanes]
            mean_ref[:, lanes] = mean
            first = 0.9 * first_ref[:, lanes] + 0.1 * mean
            second = 0.95 * second_ref[:, lanes] + 0.05 * mean * mean
            first_out[:, lanes] = first
            second_out[:, lanes] = second
            adjusted = first / 0.6513215599 / (jnp.sqrt(second / 0.4012630608) + 1e-08)
            sum_ref[OWN * s : OWN * (s + 1), LANES * lane : LANES * (lane + 1)] = (
                weight_ref[:, lanes].astype(f32) * (1.0 - 0.01 * 0.1) - 0.01 * adjusted
            )
    sent_ref[...] = jnp.broadcast_to(sum_ref[...].astype(bf16)[None], sent_ref.shape)


def update(received, power, sign_row, had, first, second, weight):
    own = jax.ShapeDtypeStruct((OWN, COLS), f32)
    return pl.pallas_call(
        update_kernel,
        out_shape=(
            own,
            own,
            own,
            pltpu.HBM((REPLICAS, SEGS * OWN, SEG), bf16),
        ),
        scratch_shapes=[
            pltpu.VMEM((SEGS * OWN, SEG), f32),
            pltpu.VMEM((16 * COLS // LANES, LANES), f32),
            pltpu.VMEM((16 * COLS // LANES, LANES), f32),
        ],
        compiler_params=params(),
        name="update",
    )(received, power, sign_row, had, first, second, weight)


GROUP = 4


def place_kernel(gathered_ref, out_hbm, rows_ref, done_ref, sems):
    step = GROUP * OWN
    copies = []
    for g in range(REPLICAS // GROUP):
        for k in range(GROUP):
            plane, line = divmod(GROUP * g + k, REPLICAS // 2)
            chunk = gathered_ref[2 * line + plane].astype(f32)
            for s in range(SEGS):
                rows_ref[OWN * k : OWN * (k + 1), SEG * s : SEG * (s + 1)] = chunk[
                    OWN * s : OWN * (s + 1), :
                ]
        rows = pl.ds(step * g, step)
        done_ref[rows, :] = rows_ref[...].astype(bf16)
        copy = pltpu.make_async_copy(
            done_ref.at[rows, :], out_hbm.at[rows, :], sems.at[g]
        )
        copy.start()
        copies.append(copy)
    for copy in copies:
        copy.wait()


def place(gathered):
    return pl.pallas_call(
        place_kernel,
        out_shape=pltpu.HBM((ROWS, COLS), bf16),
        out_specs=pl.BlockSpec(memory_space=pltpu.HBM),
        scratch_shapes=[
            pltpu.VMEM((GROUP * OWN, COLS), f32),
            pltpu.VMEM((ROWS, COLS), bf16),
            pltpu.SemaphoreType.DMA((REPLICAS // GROUP,)),
        ],
        compiler_params=params(16),
        name="place",
    )(gathered)


def rotate_weight_kernel(w_ref, sign_ref, had_ref, out_ref):
    turned = w_ref[...].astype(f32) * sign_ref[...]
    parts = [
        jnp.dot(
            turned[:, LANES * k : LANES * (k + 1)].astype(bf16),
            had_ref[...],
            preferred_element_type=f32,
        )
        for k in range(8)
    ]
    for k, part in enumerate(butterfly(parts)):
        out_ref[:, LANES * k : LANES * (k + 1)] = (part * hadamard_norm).astype(bf16)


def rotate_weight(weight, sign_row, had):
    return pl.pallas_call(
        rotate_weight_kernel,
        out_shape=jax.ShapeDtypeStruct((ROWS, COLS), bf16),
        grid=(BLOCKS,),
        in_specs=[
            pl.BlockSpec((ROWS, 1024), lambda b: (0, b)),
            pl.BlockSpec((1, 1024), lambda b: (0, b)),
            whole((LANES, LANES)),
        ],
        out_specs=pl.BlockSpec((ROWS, 1024), lambda b: (0, b)),
        compiler_params=params(),
        cost_estimate=pl.CostEstimate(
            flops=2 * ROWS * COLS * 1024, bytes_accessed=5 << 20, transcendentals=0
        ),
        name="rotate_weight",
    )(weight, sign_row, had)


def pre_grad_kernel(own_ref, other_ref, w_ref, slope_ref, collect_ref, out_ref, acc_ref):
    half = own_ref.shape[0]
    place_in_pair = lax.broadcasted_iota(jnp.int32, (half, 1), 0) & (2 * SEGS - 1)
    for index, rows_ref in enumerate((own_ref, other_ref)):
        rows = rows_ref[...]
        total = jnp.zeros((half, ROWS), f32)
        for s in range(SEGS):
            part = lax.dot_general(
                rows,
                w_ref[:, SEG * s : SEG * (s + 1)],
                (((1,), (1,)), ((), ())),
                preferred_element_type=f32,
            )
            total = jnp.where(place_in_pair >> 1 == s, part, total)
        acc_ref[half * index : half * (index + 1), :] = total
    hidden_grad = jnp.dot(
        collect_ref[...].astype(f32),
        acc_ref[...],
        precision=lax.Precision.HIGHEST,
        preferred_element_type=f32,
    )
    out_ref[...] = (hidden_grad * slope_ref[...]).astype(bf16)


def pre_grad_product(own, other, weight, slope, collect):
    return pl.pallas_call(
        pre_grad_kernel,
        out_shape=jax.ShapeDtypeStruct((TOK, ROWS), bf16),
        scratch_shapes=[pltpu.VMEM((2 * own.shape[0], ROWS), f32)],
        compiler_params=params(16),
        cost_estimate=pl.CostEstimate(
            flops=8 * 512 * SEG * ROWS, bytes_accessed=6 << 20, transcendentals=0
        ),
        name="pre_grad",
    )(own, other, weight, slope, collect)


def to_all(copies, axes):
    return lax.all_to_all(copies, axes, 0, 0, tiled=True)


def body(upstream, pre_act, w_down, first_moment, second_moment, signs, exponents):
    spread, widen, same, choice, gather = tables()
    had = jnp.asarray(hadamard(LANES), bf16)
    core = lax.axis_index("core")

    rotated = rotate_upstream(upstream, signs.reshape(1, COLS), had)
    own = to_all(rotated, ("z_hi", "y")).reshape(-1, SEG)

    pairs = pre_act.reshape(PEERS, 2, 2, ROWS)
    mine = jnp.where(core == 0, pairs[:, 0], pairs[:, 1]).reshape(TOK // 2, ROWS)
    yours = jnp.where(core == 0, pairs[:, 1], pairs[:, 0]).reshape(TOK // 2, ROWS)
    preact = jnp.concatenate([mine, yours], axis=0).astype(f32)
    normal_cdf = 0.5 * (1.0 + lax.erf(preact * root_half))
    hidden = (preact * normal_cdf).astype(bf16)
    slope = normal_cdf + preact * jnp.exp(-0.5 * preact * preact) * density_norm
    scale_power = exponents.astype(f32)
    shrink = jnp.tile(jnp.exp2(-scale_power).astype(bf16), (1, SEG // TILE))
    left, scale = expand_hidden(hidden, shrink, spread, widen, same, choice, gather)
    sign_row = (1 - 2 * signs).astype(f32).reshape(1, COLS)
    turned_weight = rotate_weight(w_down, sign_row, had)
    offset = lax.axis_index(("z_lo", "x")) * OWN
    own_power = jnp.exp2(lax.dynamic_slice_in_dim(scale_power, offset, OWN, 0))
    own_weight = lax.dynamic_slice_in_dim(w_down, offset, OWN, 0)

    own, left, scale, turned_weight, own_power, own_weight = lax.optimization_barrier(
        (own, left, scale, turned_weight, own_power, own_weight)
    )
    other = lax.ppermute(own, "core", [(0, 1), (1, 0)])
    encoded, other = encode(left, own, other, scale)
    summed = lax.psum_scatter(encoded, ("z_lo", "x"), scatter_dimension=0, tiled=True)
    grad_mean, first_new, second_new, sent = update(
        summed, own_power, sign_row, had, first_moment, second_moment, own_weight
    )
    weight_new = place(to_all(sent, ("x", "z_lo")))

    mixed = pre_grad_product(own, other, turned_weight, slope, widen)
    halves = mixed.reshape(2, PEERS, 2, ROWS)
    zero = jnp.where(core == 0, halves[0], halves[1])
    one = jnp.where(core == 0, halves[1], halves[0])
    pre_grad = jnp.stack([zero, one], axis=1).reshape(TOK, ROWS)
    return (pre_grad, grad_mean, first_new, second_new, weight_new)


def solution(mesh):
    fine = Mesh(
        mesh.devices.reshape(2, 8, 4, 8, 2), ("z_lo", "x", "z_hi", "y", "core")
    )
    dp = ("z_lo", "x")
    mp = ("z_hi", "y", "core")
    placed = (
        P(dp + mp, None),
        P(dp, mp),
        P(mp, None),
        P(mp + dp, None),
        P(mp + dp, None),
        P(),
        P(mp, None),
    )
    return jax.shard_map(
        body,
        mesh=fine,
        in_specs=placed,
        out_specs=(
            P(dp, mp),
            P(mp + dp, None),
            P(mp + dp, None),
            P(mp + dp, None),
            P(mp, None),
        ),
        check_vma=False,
    )
```

```python
import jax
import jax.numpy as jnp
import numpy as np
from jax import lax
from jax.experimental import pallas as pl
from jax.experimental.pallas import tpu as pltpu
from jax.sharding import Mesh
from jax.sharding import PartitionSpec as P

hadamard_norm = 0.03125
clip_limit = 448.0
root_half = 0.7071067811865476
density_norm = 0.3989422804014327

REPLICAS = 16
ROWS = 192
OWN = 12
COLS = 6144
SEGS = 4
SEG = 1536
BLOCKS = 6
KEPT = 47
SPARE = 128
TILE = 256
TOK = 128
PEERS = 32
LANES = 128
bf16 = jnp.bfloat16
f32 = jnp.float32


def hadamard(order):
    indices = np.arange(order)
    common = indices[:, None] & indices[None, :]
    parity = np.zeros((order, order), np.int64)
    for position in range(order.bit_length() - 1):
        parity += common >> position & 1
    return (1 - 2 * (parity % 2)).astype(np.float32)


def tables():
    owner = np.concatenate([np.repeat(np.arange(REPLICAS), KEPT), np.arange(REPLICAS)])
    part = np.concatenate([np.tile(np.arange(KEPT), REPLICAS), np.full(REPLICAS, KEPT)])
    owner = owner % 2 * (REPLICAS // 2) + owner // 2
    segment, own = part // OWN, part % OWN
    spread = (owner * OWN + own)[:, None] == np.arange(ROWS)[None, :]
    col = np.arange(2 * PEERS * SEGS * 2)
    patch = col // (SEGS * 2) * 2 + col % 2
    col_segment = col % (SEGS * 2) // 2
    widen = np.arange(TOK)[:, None] == patch[None, :]
    same = segment[:, None] == col_segment[None, :]
    tiles = SEG // TILE
    block = (3 * segment[:, None] + np.arange(tiles)[None, :] // 2) // 2
    choice = block[:, :, None] == np.arange(BLOCKS)
    gather = np.repeat(np.eye(tiles), BLOCKS, axis=0)
    shown = (spread, widen, same, choice.reshape(owner.size, -1), gather)
    return [jnp.asarray(table, bf16) for table in shown]


def butterfly(parts):
    parts = list(parts)
    span = 1
    while span < len(parts):
        for start in range(0, len(parts), 2 * span):
            for k in range(start, start + span):
                first, second = parts[k], parts[k + span]
                parts[k], parts[k + span] = first + second, first - second
        span *= 2
    return parts


def whole(shape):
    return pl.BlockSpec(shape, lambda *_: (0,) * len(shape))


def params(mebibytes=8):
    return pltpu.CompilerParams(vmem_limit_bytes=mebibytes << 20)


def rotate_upstream_kernel(
    u_hbm, sign_hbm, had_hbm, out_ref, u_ref, sign_ref, had_ref, x_ref, z_ref, sems
):
    pairs = ((u_hbm, u_ref), (sign_hbm, sign_ref), (had_hbm, had_ref))
    copies = [
        pltpu.make_async_copy(source, target, sems.at[k])
        for k, (source, target) in enumerate(pairs)
    ]
    for copy in copies:
        copy.start()
    for copy in copies:
        copy.wait()
    turned = u_ref[...].astype(f32) * (1 - 2 * sign_ref[...]).astype(f32)
    for t in range(COLS // LANES):
        x_ref[2 * t : 2 * t + 2, :] = turned[:, LANES * t : LANES * (t + 1)]
    x_ref[...] = jnp.dot(
        x_ref[...].astype(bf16), had_ref[...], preferred_element_type=f32
    )
    for b in range(BLOCKS):
        mixed = butterfly([x_ref[2 * t : 2 * t + 2, :] for t in range(8 * b, 8 * b + 8)])
        for k, part in enumerate(mixed):
            s, lane = divmod(8 * b + k, SEG // LANES)
            z_ref[2 * s : 2 * s + 2, LANES * lane : LANES * (lane + 1)] = (
                part * hadamard_norm
            )
    out_ref[...] = jnp.broadcast_to(z_ref[...].astype(bf16)[None], out_ref.shape)


def rotate_upstream(upstream, signs, had):
    arrays = [
        pltpu.with_memory_space_constraint(array, pltpu.HBM)
        for array in (upstream, signs, had)
    ]
    return pl.pallas_call(
        rotate_upstream_kernel,
        out_shape=pltpu.HBM((PEERS, 2 * SEGS, SEG), bf16),
        in_specs=[pl.BlockSpec(memory_space=pltpu.HBM)] * 3,
        scratch_shapes=[pltpu.VMEM(array.shape, array.dtype) for array in arrays]
        + [
            pltpu.VMEM((2 * COLS // LANES, LANES), f32),
            pltpu.VMEM((2 * SEGS, SEG), f32),
            pltpu.SemaphoreType.DMA((3,)),
        ],
        compiler_params=params(),
        name="rotate_upstream",
    )(*arrays)


def expand_hidden_kernel(
    hidden_ref, shrink_ref, spread_ref, widen_ref, same_ref, choice_ref, gather_ref,
    out_ref, scale_ref,
):
    rows = lax.dot_general(
        spread_ref[...],
        hidden_ref[...],
        (((1,), (1,)), ((), ())),
        preferred_element_type=f32,
    ).astype(bf16)
    wide = jnp.dot(rows, widen_ref[...], preferred_element_type=f32)
    out_ref[...] = (wide * same_ref[...].astype(f32)).astype(bf16)
    every = jnp.dot(spread_ref[...], shrink_ref[...], preferred_element_type=f32)
    chosen = (every * choice_ref[...].astype(f32)).astype(bf16)
    scale_ref[...] = jnp.dot(chosen, gather_ref[...], preferred_element_type=f32)


def expand_hidden(hidden, shrink, spread, widen, same, choice, gather):
    return pl.pallas_call(
        expand_hidden_kernel,
        out_shape=(
            jax.ShapeDtypeStruct(same.shape, bf16),
            jax.ShapeDtypeStruct((same.shape[0], gather.shape[1]), f32),
        ),
        compiler_params=params(),
        cost_estimate=pl.CostEstimate(
            flops=2 * 768 * 128 * 700, bytes_accessed=4 << 20, transcendentals=0
        ),
        name="expand_hidden",
    )(hidden, shrink, spread, widen, same, choice, gather)


def encode_kernel(
    left_ref, own_ref, other_ref, scale_ref, out_hbm, kept_hbm, done_ref, spare_ref, sems
):
    depth = own_ref.shape[0]
    full = REPLICAS * KEPT
    tiles = SEG // TILE
    scales = scale_ref[...]
    copies = [pltpu.make_async_copy(other_ref, kept_hbm, sems.at[0])]
    copies[0].start()

    def leave(lanes):
        copy = pltpu.make_async_copy(
            done_ref.at[:, lanes], out_hbm.at[:, lanes], sems.at[len(copies)]
        )
        copy.start()
        copies.append(copy)

    spare_ref[...] = jnp.zeros_like(spare_ref)
    for n in range(tiles):
        lanes = pl.ds(TILE * n, TILE)
        total = jnp.dot(
            left_ref[:, :depth], own_ref[:, lanes], preferred_element_type=f32
        )
        total += jnp.dot(
            left_ref[:, depth:], other_ref[:, lanes], preferred_element_type=f32
        )
        total = jnp.clip(total * scales[:, n : n + 1], -clip_limit, clip_limit)
        done_ref[:, lanes] = total[:full].astype(bf16)
        leave(lanes)
        for k in range(TILE // SPARE):
            rows = pl.ds(TILE // SPARE * n + k, REPLICAS, stride=KEPT)
            spare_ref[rows, :] = total[full:, SPARE * k : SPARE * (k + 1)]
    done_ref[:, SEG:] = spare_ref[...].astype(bf16)
    leave(pl.ds(SEG, SPARE))
    for copy in copies:
        copy.wait()


def encode(left, own, other, scale):
    full = REPLICAS * KEPT
    depth = own.shape[0]
    shape = (full, SEG + SPARE)
    return pl.pallas_call(
        encode_kernel,
        out_shape=(pltpu.HBM(shape, bf16), pltpu.HBM(other.shape, bf16)),
        out_specs=(pl.BlockSpec(memory_space=pltpu.HBM),) * 2,
        scratch_shapes=[
            pltpu.VMEM(shape, bf16),
            pltpu.VMEM((full, SPARE), f32),
            pltpu.SemaphoreType.DMA((SEG // TILE + 2,)),
        ],
        compiler_params=params(16),
        cost_estimate=pl.CostEstimate(
            flops=4 * full * depth * SEG, bytes_accessed=6 << 20, transcendentals=0
        ),
        name="encode",
    )(left, own, other, scale)


def update_kernel(
    received_ref, power_ref, sign_ref, had_ref, first_ref, second_ref, weight_ref,
    mean_ref, first_out, second_out, sent_ref, sum_ref, x_ref, y_ref,
):
    total = received_ref[...].astype(f32)
    sum_ref[:KEPT, :] = total[:, :SEG]
    for k in range(SEG // SPARE):
        sum_ref[KEPT : KEPT + 1, SPARE * k : SPARE * (k + 1)] = total[k : k + 1, SEG:]
    x_ref[...] = jnp.zeros_like(x_ref)
    for t in range(COLS // LANES):
        s, lane = divmod(t, SEG // LANES)
        x_ref[16 * t : 16 * t + OWN, :] = (
            sum_ref[OWN * s : OWN * (s + 1), LANES * lane : LANES * (lane + 1)]
            * power_ref[:, t // 8 : t // 8 + 1]
        )
    x = x_ref[...]
    high = x.astype(bf16)
    low = (x - high.astype(f32)).astype(bf16)
    y_ref[...] = jnp.dot(high, had_ref[...], preferred_element_type=f32) + jnp.dot(
        low, had_ref[...], preferred_element_type=f32
    )
    for b in range(BLOCKS):
        mixed = butterfly(
            [y_ref[16 * t : 16 * t + OWN, :] for t in range(8 * b, 8 * b + 8)]
        )
        for k, part in enumerate(mixed):
            t = 8 * b + k
            s, lane = divmod(t, SEG // LANES)
            lanes = slice(LANES * t, LANES * (t + 1))
            mean = part * (hadamard_norm / REPLICAS) * sign_ref[:, lanes]
            mean_ref[:, lanes] = mean
            first = 0.9 * first_ref[:, lanes] + 0.1 * mean
            second = 0.95 * second_ref[:, lanes] + 0.05 * mean * mean
            first_out[:, lanes] = first
            second_out[:, lanes] = second
            adjusted = first / 0.6513215599 / (jnp.sqrt(second / 0.4012630608) + 1e-08)
            sum_ref[OWN * s : OWN * (s + 1), LANES * lane : LANES * (lane + 1)] = (
                weight_ref[:, lanes].astype(f32) * (1.0 - 0.01 * 0.1) - 0.01 * adjusted
            )
    sent_ref[...] = jnp.broadcast_to(sum_ref[...].astype(bf16)[None], sent_ref.shape)


def update(received, power, sign_row, had, first, second, weight):
    own = jax.ShapeDtypeStruct((OWN, COLS), f32)
    return pl.pallas_call(
        update_kernel,
        out_shape=(
            own,
            own,
            own,
            pltpu.HBM((REPLICAS, SEGS * OWN, SEG), bf16),
        ),
        scratch_shapes=[
            pltpu.VMEM((SEGS * OWN, SEG), f32),
            pltpu.VMEM((16 * COLS // LANES, LANES), f32),
            pltpu.VMEM((16 * COLS // LANES, LANES), f32),
        ],
        compiler_params=params(),
        name="update",
    )(received, power, sign_row, had, first, second, weight)


GROUP = 4


def place_kernel(gathered_ref, out_hbm, rows_ref, done_ref, sems):
    step = GROUP * OWN
    copies = []
    for g in range(REPLICAS // GROUP):
        for k in range(GROUP):
            plane, line = divmod(GROUP * g + k, REPLICAS // 2)
            chunk = gathered_ref[2 * line + plane].astype(f32)
            for s in range(SEGS):
                rows_ref[OWN * k : OWN * (k + 1), SEG * s : SEG * (s + 1)] = chunk[
                    OWN * s : OWN * (s + 1), :
                ]
        rows = pl.ds(step * g, step)
        done_ref[rows, :] = rows_ref[...].astype(bf16)
        copy = pltpu.make_async_copy(
            done_ref.at[rows, :], out_hbm.at[rows, :], sems.at[g]
        )
        copy.start()
        copies.append(copy)
    for copy in copies:
        copy.wait()


def place(gathered):
    return pl.pallas_call(
        place_kernel,
        out_shape=pltpu.HBM((ROWS, COLS), bf16),
        out_specs=pl.BlockSpec(memory_space=pltpu.HBM),
        scratch_shapes=[
            pltpu.VMEM((GROUP * OWN, COLS), f32),
            pltpu.VMEM((ROWS, COLS), bf16),
            pltpu.SemaphoreType.DMA((REPLICAS // GROUP,)),
        ],
        compiler_params=params(16),
        name="place",
    )(gathered)


def rotate_weight_kernel(w_ref, sign_ref, had_ref, out_ref):
    turned = w_ref[...].astype(f32) * sign_ref[...]
    parts = [
        jnp.dot(
            turned[:, LANES * k : LANES * (k + 1)].astype(bf16),
            had_ref[...],
            preferred_element_type=f32,
        )
        for k in range(8)
    ]
    for k, part in enumerate(butterfly(parts)):
        out_ref[:, LANES * k : LANES * (k + 1)] = (part * hadamard_norm).astype(bf16)


def rotate_weight(weight, sign_row, had):
    return pl.pallas_call(
        rotate_weight_kernel,
        out_shape=jax.ShapeDtypeStruct((ROWS, COLS), bf16),
        grid=(BLOCKS,),
        in_specs=[
            pl.BlockSpec((ROWS, 1024), lambda b: (0, b)),
            pl.BlockSpec((1, 1024), lambda b: (0, b)),
            whole((LANES, LANES)),
        ],
        out_specs=pl.BlockSpec((ROWS, 1024), lambda b: (0, b)),
        compiler_params=params(),
        cost_estimate=pl.CostEstimate(
            flops=2 * ROWS * COLS * 1024, bytes_accessed=5 << 20, transcendentals=0
        ),
        name="rotate_weight",
    )(weight, sign_row, had)


def pre_grad_kernel(own_ref, other_ref, w_ref, slope_ref, collect_ref, out_ref, acc_ref):
    half = own_ref.shape[0]
    place_in_pair = lax.broadcasted_iota(jnp.int32, (half, 1), 0) & (2 * SEGS - 1)
    for index, rows_ref in enumerate((own_ref, other_ref)):
        rows = rows_ref[...]
        total = jnp.zeros((half, ROWS), f32)
        for s in range(SEGS):
            part = lax.dot_general(
                rows,
                w_ref[:, SEG * s : SEG * (s + 1)],
                (((1,), (1,)), ((), ())),
                preferred_element_type=f32,
            )
            total = jnp.where(place_in_pair >> 1 == s, part, total)
        acc_ref[half * index : half * (index + 1), :] = total
    hidden_grad = jnp.dot(
        collect_ref[...].astype(f32),
        acc_ref[...],
        precision=lax.Precision.HIGHEST,
        preferred_element_type=f32,
    )
    out_ref[...] = (hidden_grad * slope_ref[...]).astype(bf16)


def pre_grad_product(own, other, weight, slope, collect):
    return pl.pallas_call(
        pre_grad_kernel,
        out_shape=jax.ShapeDtypeStruct((TOK, ROWS), bf16),
        scratch_shapes=[pltpu.VMEM((2 * own.shape[0], ROWS), f32)],
        compiler_params=params(16),
        cost_estimate=pl.CostEstimate(
            flops=8 * 512 * SEG * ROWS, bytes_accessed=6 << 20, transcendentals=0
        ),
        name="pre_grad",
    )(own, other, weight, slope, collect)


def to_all(copies, axes):
    return lax.all_to_all(copies, axes, 0, 0, tiled=True)


def body(upstream, pre_act, w_down, first_moment, second_moment, signs, exponents):
    spread, widen, same, choice, gather = tables()
    had = jnp.asarray(hadamard(LANES), bf16)
    core = lax.axis_index("core")

    rotated = rotate_upstream(upstream, signs.reshape(1, COLS), had)
    own = to_all(rotated, ("z_hi", "y")).reshape(-1, SEG)

    pairs = pre_act.reshape(PEERS, 2, 2, ROWS)
    mine = jnp.where(core == 0, pairs[:, 0], pairs[:, 1]).reshape(TOK // 2, ROWS)
    yours = jnp.where(core == 0, pairs[:, 1], pairs[:, 0]).reshape(TOK // 2, ROWS)
    preact = jnp.concatenate([mine, yours], axis=0).astype(f32)
    normal_cdf = 0.5 * (1.0 + lax.erf(preact * root_half))
    hidden = (preact * normal_cdf).astype(bf16)
    slope = normal_cdf + preact * jnp.exp(-0.5 * preact * preact) * density_norm
    scale_power = exponents.astype(f32)
    shrink = jnp.tile(jnp.exp2(-scale_power).astype(bf16), (1, SEG // TILE))
    left, scale = expand_hidden(hidden, shrink, spread, widen, same, choice, gather)
    sign_row = (1 - 2 * signs).astype(f32).reshape(1, COLS)
    turned_weight = rotate_weight(w_down, sign_row, had)
    offset = lax.axis_index(("z_lo", "x")) * OWN
    own_power = jnp.exp2(lax.dynamic_slice_in_dim(scale_power, offset, OWN, 0))
    own_weight = lax.dynamic_slice_in_dim(w_down, offset, OWN, 0)

    own, left, scale, turned_weight, own_power, own_weight = lax.optimization_barrier(
        (own, left, scale, turned_weight, own_power, own_weight)
    )
    other = lax.ppermute(own, "core", [(0, 1), (1, 0)])
    encoded, other = encode(left, own, other, scale)
    summed = lax.psum_scatter(encoded, ("x", "z_lo"), scatter_dimension=0, tiled=True)
    grad_mean, first_new, second_new, sent = update(
        summed, own_power, sign_row, had, first_moment, second_moment, own_weight
    )
    weight_new = place(to_all(sent, ("x", "z_lo")))

    mixed = pre_grad_product(own, other, turned_weight, slope, widen)
    halves = mixed.reshape(2, PEERS, 2, ROWS)
    zero = jnp.where(core == 0, halves[0], halves[1])
    one = jnp.where(core == 0, halves[1], halves[0])
    pre_grad = jnp.stack([zero, one], axis=1).reshape(TOK, ROWS)
    return (pre_grad, grad_mean, first_new, second_new, weight_new)


def solution(mesh):
    fine = Mesh(
        mesh.devices.reshape(2, 8, 4, 8, 2), ("z_lo", "x", "z_hi", "y", "core")
    )
    dp = ("z_lo", "x")
    mp = ("z_hi", "y", "core")
    placed = (
        P(dp + mp, None),
        P(dp, mp),
        P(mp, None),
        P(mp + dp, None),
        P(mp + dp, None),
        P(),
        P(mp, None),
    )
    return jax.shard_map(
        body,
        mesh=fine,
        in_specs=placed,
        out_specs=(
            P(dp, mp),
            P(mp + dp, None),
            P(mp + dp, None),
            P(mp + dp, None),
            P(mp, None),
        ),
        check_vma=False,
    )
```

```python
import jax
import jax.numpy as jnp
import numpy as np
from jax import lax
from jax.experimental import pallas as pl
from jax.experimental.pallas import tpu as pltpu
from jax.sharding import Mesh
from jax.sharding import PartitionSpec as P

hadamard_norm = 0.03125
clip_limit = 448.0
root_half = 0.7071067811865476
density_norm = 0.3989422804014327

REPLICAS = 16
ROWS = 192
OWN = 12
COLS = 6144
SEGS = 4
SEG = 1536
BLOCKS = 6
KEPT = 47
SPARE = 128
TILE = 256
TOK = 128
PEERS = 32
LANES = 128
bf16 = jnp.bfloat16
f32 = jnp.float32


def hadamard(order):
    indices = np.arange(order)
    common = indices[:, None] & indices[None, :]
    parity = np.zeros((order, order), np.int64)
    for position in range(order.bit_length() - 1):
        parity += common >> position & 1
    return (1 - 2 * (parity % 2)).astype(np.float32)


def tables():
    owner = np.concatenate([np.repeat(np.arange(REPLICAS), KEPT), np.arange(REPLICAS)])
    part = np.concatenate([np.tile(np.arange(KEPT), REPLICAS), np.full(REPLICAS, KEPT)])
    owner = np.where(owner < REPLICAS // 2, owner, 3 * REPLICAS // 2 - 1 - owner)
    segment, own = part // OWN, part % OWN
    spread = (owner * OWN + own)[:, None] == np.arange(ROWS)[None, :]
    col = np.arange(2 * PEERS * SEGS * 2)
    patch = col // (SEGS * 2) * 2 + col % 2
    col_segment = col % (SEGS * 2) // 2
    widen = np.arange(TOK)[:, None] == patch[None, :]
    same = segment[:, None] == col_segment[None, :]
    tiles = SEG // TILE
    block = (3 * segment[:, None] + np.arange(tiles)[None, :] // 2) // 2
    choice = block[:, :, None] == np.arange(BLOCKS)
    gather = np.repeat(np.eye(tiles), BLOCKS, axis=0)
    shown = (spread, widen, same, choice.reshape(owner.size, -1), gather)
    return [jnp.asarray(table, bf16) for table in shown]


def butterfly(parts):
    parts = list(parts)
    span = 1
    while span < len(parts):
        for start in range(0, len(parts), 2 * span):
            for k in range(start, start + span):
                first, second = parts[k], parts[k + span]
                parts[k], parts[k + span] = first + second, first - second
        span *= 2
    return parts


def whole(shape):
    return pl.BlockSpec(shape, lambda *_: (0,) * len(shape))


def params(mebibytes=8):
    return pltpu.CompilerParams(vmem_limit_bytes=mebibytes << 20)


def rotate_upstream_kernel(
    u_hbm, sign_hbm, had_hbm, out_ref, u_ref, sign_ref, had_ref, x_ref, z_ref, sems
):
    pairs = ((u_hbm, u_ref), (sign_hbm, sign_ref), (had_hbm, had_ref))
    copies = [
        pltpu.make_async_copy(source, target, sems.at[k])
        for k, (source, target) in enumerate(pairs)
    ]
    for copy in copies:
        copy.start()
    for copy in copies:
        copy.wait()
    turned = u_ref[...].astype(f32) * (1 - 2 * sign_ref[...]).astype(f32)
    for t in range(COLS // LANES):
        x_ref[2 * t : 2 * t + 2, :] = turned[:, LANES * t : LANES * (t + 1)]
    x_ref[...] = jnp.dot(
        x_ref[...].astype(bf16), had_ref[...], preferred_element_type=f32
    )
    for b in range(BLOCKS):
        mixed = butterfly([x_ref[2 * t : 2 * t + 2, :] for t in range(8 * b, 8 * b + 8)])
        for k, part in enumerate(mixed):
            s, lane = divmod(8 * b + k, SEG // LANES)
            z_ref[2 * s : 2 * s + 2, LANES * lane : LANES * (lane + 1)] = (
                part * hadamard_norm
            )
    out_ref[...] = jnp.broadcast_to(z_ref[...].astype(bf16)[None], out_ref.shape)


def rotate_upstream(upstream, signs, had):
    arrays = [
        pltpu.with_memory_space_constraint(array, pltpu.HBM)
        for array in (upstream, signs, had)
    ]
    return pl.pallas_call(
        rotate_upstream_kernel,
        out_shape=pltpu.HBM((PEERS, 2 * SEGS, SEG), bf16),
        in_specs=[pl.BlockSpec(memory_space=pltpu.HBM)] * 3,
        scratch_shapes=[pltpu.VMEM(array.shape, array.dtype) for array in arrays]
        + [
            pltpu.VMEM((2 * COLS // LANES, LANES), f32),
            pltpu.VMEM((2 * SEGS, SEG), f32),
            pltpu.SemaphoreType.DMA((3,)),
        ],
        compiler_params=params(),
        name="rotate_upstream",
    )(*arrays)


def expand_hidden_kernel(
    hidden_ref, shrink_ref, spread_ref, widen_ref, same_ref, choice_ref, gather_ref,
    out_ref, scale_ref,
):
    rows = lax.dot_general(
        spread_ref[...],
        hidden_ref[...],
        (((1,), (1,)), ((), ())),
        preferred_element_type=f32,
    ).astype(bf16)
    wide = jnp.dot(rows, widen_ref[...], preferred_element_type=f32)
    out_ref[...] = (wide * same_ref[...].astype(f32)).astype(bf16)
    every = jnp.dot(spread_ref[...], shrink_ref[...], preferred_element_type=f32)
    chosen = (every * choice_ref[...].astype(f32)).astype(bf16)
    scale_ref[...] = jnp.dot(chosen, gather_ref[...], preferred_element_type=f32)


def expand_hidden(hidden, shrink, spread, widen, same, choice, gather):
    return pl.pallas_call(
        expand_hidden_kernel,
        out_shape=(
            jax.ShapeDtypeStruct(same.shape, bf16),
            jax.ShapeDtypeStruct((same.shape[0], gather.shape[1]), f32),
        ),
        compiler_params=params(),
        cost_estimate=pl.CostEstimate(
            flops=2 * 768 * 128 * 700, bytes_accessed=4 << 20, transcendentals=0
        ),
        name="expand_hidden",
    )(hidden, shrink, spread, widen, same, choice, gather)


def encode_kernel(
    left_ref, own_ref, other_ref, scale_ref, out_hbm, kept_hbm, done_ref, spare_ref, sems
):
    depth = own_ref.shape[0]
    full = REPLICAS * KEPT
    tiles = SEG // TILE
    scales = scale_ref[...]
    copies = [pltpu.make_async_copy(other_ref, kept_hbm, sems.at[0])]
    copies[0].start()

    def leave(lanes):
        copy = pltpu.make_async_copy(
            done_ref.at[:, lanes], out_hbm.at[:, lanes], sems.at[len(copies)]
        )
        copy.start()
        copies.append(copy)

    spare_ref[...] = jnp.zeros_like(spare_ref)
    for n in range(tiles):
        lanes = pl.ds(TILE * n, TILE)
        total = jnp.dot(
            left_ref[:, :depth], own_ref[:, lanes], preferred_element_type=f32
        )
        total += jnp.dot(
            left_ref[:, depth:], other_ref[:, lanes], preferred_element_type=f32
        )
        total = jnp.clip(total * scales[:, n : n + 1], -clip_limit, clip_limit)
        done_ref[:, lanes] = total[:full].astype(bf16)
        leave(lanes)
        for k in range(TILE // SPARE):
            rows = pl.ds(TILE // SPARE * n + k, REPLICAS, stride=KEPT)
            spare_ref[rows, :] = total[full:, SPARE * k : SPARE * (k + 1)]
    done_ref[:, SEG:] = spare_ref[...].astype(bf16)
    leave(pl.ds(SEG, SPARE))
    for copy in copies:
        copy.wait()


def encode(left, own, other, scale):
    full = REPLICAS * KEPT
    depth = own.shape[0]
    shape = (full, SEG + SPARE)
    return pl.pallas_call(
        encode_kernel,
        out_shape=(pltpu.HBM(shape, bf16), pltpu.HBM(other.shape, bf16)),
        out_specs=(pl.BlockSpec(memory_space=pltpu.HBM),) * 2,
        scratch_shapes=[
            pltpu.VMEM(shape, bf16),
            pltpu.VMEM((full, SPARE), f32),
            pltpu.SemaphoreType.DMA((SEG // TILE + 2,)),
        ],
        compiler_params=params(16),
        cost_estimate=pl.CostEstimate(
            flops=4 * full * depth * SEG, bytes_accessed=6 << 20, transcendentals=0
        ),
        name="encode",
    )(left, own, other, scale)


def update_kernel(
    received_ref, power_ref, sign_ref, had_ref, first_ref, second_ref, weight_ref,
    mean_ref, first_out, second_out, sent_ref, sum_ref, x_ref, y_ref,
):
    total = received_ref[...].astype(f32)
    sum_ref[:KEPT, :] = total[:, :SEG]
    for k in range(SEG // SPARE):
        sum_ref[KEPT : KEPT + 1, SPARE * k : SPARE * (k + 1)] = total[k : k + 1, SEG:]
    x_ref[...] = jnp.zeros_like(x_ref)
    for t in range(COLS // LANES):
        s, lane = divmod(t, SEG // LANES)
        x_ref[16 * t : 16 * t + OWN, :] = (
            sum_ref[OWN * s : OWN * (s + 1), LANES * lane : LANES * (lane + 1)]
            * power_ref[:, t // 8 : t // 8 + 1]
        )
    x = x_ref[...]
    high = x.astype(bf16)
    low = (x - high.astype(f32)).astype(bf16)
    y_ref[...] = jnp.dot(high, had_ref[...], preferred_element_type=f32) + jnp.dot(
        low, had_ref[...], preferred_element_type=f32
    )
    for b in range(BLOCKS):
        mixed = butterfly(
            [y_ref[16 * t : 16 * t + OWN, :] for t in range(8 * b, 8 * b + 8)]
        )
        for k, part in enumerate(mixed):
            t = 8 * b + k
            s, lane = divmod(t, SEG // LANES)
            lanes = slice(LANES * t, LANES * (t + 1))
            mean = part * (hadamard_norm / REPLICAS) * sign_ref[:, lanes]
            mean_ref[:, lanes] = mean
            first = 0.9 * first_ref[:, lanes] + 0.1 * mean
            second = 0.95 * second_ref[:, lanes] + 0.05 * mean * mean
            first_out[:, lanes] = first
            second_out[:, lanes] = second
            adjusted = first / 0.6513215599 / (jnp.sqrt(second / 0.4012630608) + 1e-08)
            sum_ref[OWN * s : OWN * (s + 1), LANES * lane : LANES * (lane + 1)] = (
                weight_ref[:, lanes].astype(f32) * (1.0 - 0.01 * 0.1) - 0.01 * adjusted
            )
    sent_ref[...] = jnp.broadcast_to(sum_ref[...].astype(bf16)[None], sent_ref.shape)


def update(received, power, sign_row, had, first, second, weight):
    own = jax.ShapeDtypeStruct((OWN, COLS), f32)
    return pl.pallas_call(
        update_kernel,
        out_shape=(
            own,
            own,
            own,
            pltpu.HBM((REPLICAS, SEGS * OWN, SEG), bf16),
        ),
        scratch_shapes=[
            pltpu.VMEM((SEGS * OWN, SEG), f32),
            pltpu.VMEM((16 * COLS // LANES, LANES), f32),
            pltpu.VMEM((16 * COLS // LANES, LANES), f32),
        ],
        compiler_params=params(),
        name="update",
    )(received, power, sign_row, had, first, second, weight)


GROUP = 4


def place_kernel(gathered_ref, out_hbm, rows_ref, done_ref, sems):
    step = GROUP * OWN
    copies = []
    for g in range(REPLICAS // GROUP):
        for k in range(GROUP):
            plane, line = divmod(GROUP * g + k, REPLICAS // 2)
            chunk = gathered_ref[2 * line + plane].astype(f32)
            for s in range(SEGS):
                rows_ref[OWN * k : OWN * (k + 1), SEG * s : SEG * (s + 1)] = chunk[
                    OWN * s : OWN * (s + 1), :
                ]
        rows = pl.ds(step * g, step)
        done_ref[rows, :] = rows_ref[...].astype(bf16)
        copy = pltpu.make_async_copy(
            done_ref.at[rows, :], out_hbm.at[rows, :], sems.at[g]
        )
        copy.start()
        copies.append(copy)
    for copy in copies:
        copy.wait()


def place(gathered):
    return pl.pallas_call(
        place_kernel,
        out_shape=pltpu.HBM((ROWS, COLS), bf16),
        out_specs=pl.BlockSpec(memory_space=pltpu.HBM),
        scratch_shapes=[
            pltpu.VMEM((GROUP * OWN, COLS), f32),
            pltpu.VMEM((ROWS, COLS), bf16),
            pltpu.SemaphoreType.DMA((REPLICAS // GROUP,)),
        ],
        compiler_params=params(16),
        name="place",
    )(gathered)


def rotate_weight_kernel(w_ref, sign_ref, had_ref, out_ref):
    turned = w_ref[...].astype(f32) * sign_ref[...]
    parts = [
        jnp.dot(
            turned[:, LANES * k : LANES * (k + 1)].astype(bf16),
            had_ref[...],
            preferred_element_type=f32,
        )
        for k in range(8)
    ]
    for k, part in enumerate(butterfly(parts)):
        out_ref[:, LANES * k : LANES * (k + 1)] = (part * hadamard_norm).astype(bf16)


def rotate_weight(weight, sign_row, had):
    return pl.pallas_call(
        rotate_weight_kernel,
        out_shape=jax.ShapeDtypeStruct((ROWS, COLS), bf16),
        grid=(BLOCKS,),
        in_specs=[
            pl.BlockSpec((ROWS, 1024), lambda b: (0, b)),
            pl.BlockSpec((1, 1024), lambda b: (0, b)),
            whole((LANES, LANES)),
        ],
        out_specs=pl.BlockSpec((ROWS, 1024), lambda b: (0, b)),
        compiler_params=params(),
        cost_estimate=pl.CostEstimate(
            flops=2 * ROWS * COLS * 1024, bytes_accessed=5 << 20, transcendentals=0
        ),
        name="rotate_weight",
    )(weight, sign_row, had)


def pre_grad_kernel(own_ref, other_ref, w_ref, slope_ref, collect_ref, out_ref, acc_ref):
    half = own_ref.shape[0]
    place_in_pair = lax.broadcasted_iota(jnp.int32, (half, 1), 0) & (2 * SEGS - 1)
    for index, rows_ref in enumerate((own_ref, other_ref)):
        rows = rows_ref[...]
        total = jnp.zeros((half, ROWS), f32)
        for s in range(SEGS):
            part = lax.dot_general(
                rows,
                w_ref[:, SEG * s : SEG * (s + 1)],
                (((1,), (1,)), ((), ())),
                preferred_element_type=f32,
            )
            total = jnp.where(place_in_pair >> 1 == s, part, total)
        acc_ref[half * index : half * (index + 1), :] = total
    hidden_grad = jnp.dot(
        collect_ref[...].astype(f32),
        acc_ref[...],
        precision=lax.Precision.HIGHEST,
        preferred_element_type=f32,
    )
    out_ref[...] = (hidden_grad * slope_ref[...]).astype(bf16)


def pre_grad_product(own, other, weight, slope, collect):
    return pl.pallas_call(
        pre_grad_kernel,
        out_shape=jax.ShapeDtypeStruct((TOK, ROWS), bf16),
        scratch_shapes=[pltpu.VMEM((2 * own.shape[0], ROWS), f32)],
        compiler_params=params(16),
        cost_estimate=pl.CostEstimate(
            flops=8 * 512 * SEG * ROWS, bytes_accessed=6 << 20, transcendentals=0
        ),
        name="pre_grad",
    )(own, other, weight, slope, collect)


def to_all(copies, axes):
    return lax.all_to_all(copies, axes, 0, 0, tiled=True)


def body(upstream, pre_act, w_down, first_moment, second_moment, signs, exponents):
    spread, widen, same, choice, gather = tables()
    had = jnp.asarray(hadamard(LANES), bf16)
    core = lax.axis_index("core")

    rotated = rotate_upstream(upstream, signs.reshape(1, COLS), had)
    own = to_all(rotated, ("z_hi", "y")).reshape(-1, SEG)

    pairs = pre_act.reshape(PEERS, 2, 2, ROWS)
    mine = jnp.where(core == 0, pairs[:, 0], pairs[:, 1]).reshape(TOK // 2, ROWS)
    yours = jnp.where(core == 0, pairs[:, 1], pairs[:, 0]).reshape(TOK // 2, ROWS)
    preact = jnp.concatenate([mine, yours], axis=0).astype(f32)
    normal_cdf = 0.5 * (1.0 + lax.erf(preact * root_half))
    hidden = (preact * normal_cdf).astype(bf16)
    slope = normal_cdf + preact * jnp.exp(-0.5 * preact * preact) * density_norm
    scale_power = exponents.astype(f32)
    shrink = jnp.tile(jnp.exp2(-scale_power).astype(bf16), (1, SEG // TILE))
    left, scale = expand_hidden(hidden, shrink, spread, widen, same, choice, gather)
    sign_row = (1 - 2 * signs).astype(f32).reshape(1, COLS)
    turned_weight = rotate_weight(w_down, sign_row, had)
    offset = lax.axis_index(("z_lo", "x")) * OWN
    own_power = jnp.exp2(lax.dynamic_slice_in_dim(scale_power, offset, OWN, 0))
    own_weight = lax.dynamic_slice_in_dim(w_down, offset, OWN, 0)

    own, left, scale, turned_weight, own_power, own_weight = lax.optimization_barrier(
        (own, left, scale, turned_weight, own_power, own_weight)
    )
    other = lax.ppermute(own, "core", [(0, 1), (1, 0)])
    encoded, other = encode(left, own, other, scale)
    half = REPLICAS // 2
    ring = [*range(half), *range(REPLICAS - 1, half - 1, -1)]
    summed = lax.psum_scatter(
        encoded,
        ("z_lo", "x"),
        scatter_dimension=0,
        axis_index_groups=[ring],
        tiled=True,
    )
    grad_mean, first_new, second_new, sent = update(
        summed, own_power, sign_row, had, first_moment, second_moment, own_weight
    )
    weight_new = place(to_all(sent, ("x", "z_lo")))

    mixed = pre_grad_product(own, other, turned_weight, slope, widen)
    halves = mixed.reshape(2, PEERS, 2, ROWS)
    zero = jnp.where(core == 0, halves[0], halves[1])
    one = jnp.where(core == 0, halves[1], halves[0])
    pre_grad = jnp.stack([zero, one], axis=1).reshape(TOK, ROWS)
    return (pre_grad, grad_mean, first_new, second_new, weight_new)


def solution(mesh):
    fine = Mesh(
        mesh.devices.reshape(2, 8, 4, 8, 2), ("z_lo", "x", "z_hi", "y", "core")
    )
    dp = ("z_lo", "x")
    mp = ("z_hi", "y", "core")
    placed = (
        P(dp + mp, None),
        P(dp, mp),
        P(mp, None),
        P(mp + dp, None),
        P(mp + dp, None),
        P(),
        P(mp, None),
    )
    return jax.shard_map(
        body,
        mesh=fine,
        in_specs=placed,
        out_specs=(
            P(dp, mp),
            P(mp + dp, None),
            P(mp + dp, None),
            P(mp + dp, None),
            P(mp, None),
        ),
        check_vma=False,
    )
```
